32 devices in a mesh: seq: 8 (over z, y), head: 4 (over x, core).
Axes of the slice: x: 2, y: 2, z: 4, core: 2. Of those that a mesh axis runs over, the one named last changes fastest.
Arguments:
- hidden_states: bfloat16 [8, 5, 8192], P(None, None, 'seq'), may hold values from -6 to 6
- w_query: bfloat16 [8192, 8192], P('seq', 'head'), may hold values from -0.0625 to 0.0625
- w_key: bfloat16 [8192, 1024], P('seq', 'head'), may hold values from -0.15625 to 0.15625
- w_value: bfloat16 [8192, 1024], P('seq', 'head'), may hold values from -0.0625 to 0.0625
- w_out: bfloat16 [8192, 8192], P('head', 'seq'), may hold values from -0.0625 to 0.0625
- key_cache: bfloat16 [8, 8192, 1024], P(None, 'seq', 'head'), may hold values from -104 to 104
- value_cache: bfloat16 [8, 8192, 1024], P(None, 'seq', 'head'), may hold values from -6 to 6
- context_lengths: int32 [8], replicated, may hold values from 2048 to 8192, as said below
- keep_blocks: int32 [8, 64], P(None, 'seq'), may hold values from 0 to 1, as said below
Outputs:
- verify_out: bfloat16 [8, 5, 8192], P(None, None, 'seq')
- draft_out: bfloat16 [8, 4, 8192], P(None, None, 'seq')
The draws below stay inside these ranges and needn't reach their ends.
Inputs may be any that keep to these rules, and one draw needn't show every extreme that they name: `keep_blocks`: block 0 of every sequence is kept. `context_lengths`: one sequence has length 8192.
All inputs are finite; a program needn't handle non-finite values.
Results may differ from the reference program's by a relative error of at most 0.017.
Values may be sent and summed in bfloat16 or wider, within the bound.
A program may use at most 64 MiB of HBM per device.

```python
import jax
import jax.numpy as jnp
from jax import lax

D = 8192
HEADS = 64
KV_HEADS = 8
HEAD_DIM = 128
B = 8
VERIFY = 5
BLOCK = 128
CONTEXT = 8192
DRAFT = 4
N_HEAD = 4


def draw_key_cache(key, part):
    shape_all = (B, CONTEXT, KV_HEADS * HEAD_DIM)
    values = 2.5 * jax.random.truncated_normal(key, -4.0, 4.0, shape_all, jnp.float32)
    return values.astype(jnp.bfloat16)


def draw_context_lengths(key, part):
    length_key, row_key = jax.random.split(key)
    lengths = jax.random.randint(length_key, (B,), CONTEXT // 4, CONTEXT + 1)
    full_row = jax.random.randint(row_key, (), 0, B)
    return jnp.where(jnp.arange(B) == full_row, CONTEXT, lengths).astype(jnp.int32)


def draw_keep_blocks(key, part):
    kept_flags = jax.random.randint(key, (B, CONTEXT // BLOCK), 0, 4) == 0
    first_block = jnp.arange(CONTEXT // BLOCK)[None, :] == 0
    return (kept_flags | first_block).astype(jnp.int32)


def steps_of(rng, shape, shards, smallest, largest):
    gain, own = 1.0, jax.random.fold_in(rng, 6)
    for axis_at, blocks in shards:
        draws = jnp.exp(jax.random.uniform(jax.random.fold_in(own, axis_at), (blocks,), jnp.float32, smallest / len(shards), largest / len(shards)))
        gain = gain * jnp.repeat(draws, shape[axis_at] // blocks).reshape([-1 if axis == axis_at else 1 for axis in range(len(shape))])
    return gain


def normal_values(key, extent, deviation, limit, pieces=(), kind=jnp.bfloat16):
    values = deviation * jax.random.normal(key, extent, jnp.float32)
    if pieces:
        values = values * steps_of(key, extent, pieces, -0.22, 0.18)
    return jnp.clip(values, -limit, limit).astype(kind)


def setup_inputs(seed: int = 0) -> dict:
    key_list = jax.random.split(jax.random.key(seed), 10)
    return {
        "hidden_states": normal_values(key_list[0], (B, VERIFY, D), 1.0, 6.0, ((2, 8),)),
        "w_query": normal_values(key_list[1], (D, HEADS * HEAD_DIM), D ** -0.5, 0.0625, ((0, 8), (1, 4))),
        "w_key": normal_values(key_list[2], (D, KV_HEADS * HEAD_DIM), (D // 6) ** -0.5, 0.15625, ((0, 8), (1, 4))),
        "w_value": normal_values(key_list[3], (D, KV_HEADS * HEAD_DIM), D ** -0.5, 0.0625, ((0, 8), (1, 4))),
        "w_out": normal_values(key_list[4], (HEADS * HEAD_DIM, D), (HEADS * HEAD_DIM) ** -0.5, 0.0625, ((0, 4), (1, 8))),
        "key_cache": draw_key_cache(jax.random.fold_in(key_list[9], 71), 0),
        "value_cache": normal_values(key_list[6], (B, CONTEXT, KV_HEADS * HEAD_DIM), 1.0, 6.0, ((1, 8), (2, 4))),
        "context_lengths": draw_context_lengths(jax.random.fold_in(key_list[9], 71), 0),
        "keep_blocks": draw_keep_blocks(jax.random.fold_in(key_list[9], 71), 0),
    }


big_negative = -1.0e30


def rotate(values_in, positions):
    half_dim = HEAD_DIM // 2
    inverse = 500000.0 ** (-(jnp.arange(half_dim, dtype=jnp.float32) * 2.0) / HEAD_DIM)
    angles = positions[:, :, None, None].astype(jnp.float32) * inverse
    cosine = jnp.cos(angles)
    sine = jnp.sin(angles)
    first_half = values_in[..., :half_dim]
    second_half = values_in[..., half_dim:]
    return jnp.concatenate([first_half * cosine - second_half * sine, second_half * cosine + first_half * sine], axis=-1)


def attend(scores, new_scores, cache_mask, new_mask, cache_values, new_values):
    masked = jnp.where(cache_mask[None, None, None, :], scores, big_negative)
    masked_new = jnp.where(new_mask[None, :, None, :], new_scores, big_negative)
    peak_value = jnp.maximum(jnp.max(masked, axis=-1), jnp.max(masked_new, axis=-1))
    cache_weights = jnp.where(cache_mask[None, None, None, :], jnp.exp(masked - peak_value[..., None]), 0.0)
    new_weights = jnp.where(new_mask[None, :, None, :], jnp.exp(masked_new - peak_value[..., None]), 0.0)
    total_sum = jnp.sum(cache_weights, axis=-1) + jnp.sum(new_weights, axis=-1)
    weighted = jnp.einsum("kjgt,tkd->kjgd", cache_weights.astype(jnp.bfloat16).astype(jnp.float32), cache_values.astype(jnp.float32))
    weighted = weighted + jnp.einsum("kjgi,ikd->kjgd", new_weights.astype(jnp.bfloat16).astype(jnp.float32), new_values.astype(jnp.float32))
    result = weighted / total_sum[..., None]
    return result.transpose(1, 0, 2, 3).reshape(result.shape[1], HEADS * HEAD_DIM)


def project_groups(attended, w_out):
    group_cols = HEADS * HEAD_DIM // N_HEAD
    total = jnp.zeros((attended.shape[0], D), jnp.float32)
    for group in range(N_HEAD):
        part_rows = attended[:, group * group_cols:(group + 1) * group_cols]
        part_weight = w_out[group * group_cols:(group + 1) * group_cols]
        partial_value = jnp.dot(part_rows, part_weight, preferred_element_type=jnp.float32).astype(jnp.bfloat16)
        total = total + partial_value.astype(jnp.float32)
    return total.astype(jnp.bfloat16)


def reference(hidden_states, w_query, w_key, w_value, w_out, key_cache, value_cache, context_lengths, keep_blocks):
    group_size = HEADS // KV_HEADS
    score_scale = HEAD_DIM ** -0.5
    tok_rows = hidden_states.reshape(B * VERIFY, D)
    query_raw = jnp.dot(tok_rows, w_query, preferred_element_type=jnp.float32).reshape(B, VERIFY, HEADS, HEAD_DIM)
    key_raw = jnp.dot(tok_rows, w_key, preferred_element_type=jnp.float32).reshape(B, VERIFY, KV_HEADS, HEAD_DIM)
    value_raw = jnp.dot(tok_rows, w_value, preferred_element_type=jnp.float32).reshape(B, VERIFY, KV_HEADS, HEAD_DIM)
    positions = context_lengths[:, None] + jnp.arange(VERIFY, dtype=jnp.int32)[None, :]
    query_rot = rotate(query_raw, positions).astype(jnp.bfloat16)
    key_rot = rotate(key_raw, positions).astype(jnp.bfloat16)
    new_values = value_raw.astype(jnp.bfloat16)
    key_positions = jnp.arange(CONTEXT, dtype=jnp.int32)
    causal = jnp.arange(VERIFY)[None, :] <= jnp.arange(VERIFY)[:, None]

    def one_sequence(row_items):
        query_row, key_row, value_row, cache_keys, cache_values, length, keep_row = row_items
        grouped = query_row.reshape(VERIFY, KV_HEADS, group_size, HEAD_DIM).astype(jnp.float32)
        cache_keys = cache_keys.reshape(CONTEXT, KV_HEADS, HEAD_DIM)
        cache_values = cache_values.reshape(CONTEXT, KV_HEADS, HEAD_DIM)
        scores = jnp.einsum("jkgd,tkd->kjgt", grouped, cache_keys.astype(jnp.float32)) * score_scale
        new_scores = jnp.einsum("jkgd,ikd->kjgi", grouped, key_row.astype(jnp.float32)) * score_scale
        live_mask = key_positions < length
        kept_mask = live_mask & (jnp.repeat(keep_row, BLOCK) > 0)
        target_heads = attend(scores, new_scores, live_mask, causal, cache_values, value_row)
        draft_heads = attend(scores[:, :DRAFT], new_scores[:, :DRAFT], kept_mask, causal[:DRAFT], cache_values, value_row)
        return target_heads.astype(jnp.bfloat16), draft_heads.astype(jnp.bfloat16)

    target_all, draft_all = lax.map(one_sequence, (query_rot, key_rot, new_values, key_cache, value_cache, context_lengths, keep_blocks))
    verify_out = project_groups(target_all.reshape(B * VERIFY, HEADS * HEAD_DIM), w_out)
    draft_out = project_groups(draft_all.reshape(B * DRAFT, HEADS * HEAD_DIM), w_out)
    return verify_out.reshape(B, VERIFY, D), draft_out.reshape(B, DRAFT, D)
```

```python
import functools
import math

import jax
import jax.numpy as jnp
import numpy as np
from jax import lax
from jax.experimental import pallas as pl
from jax.experimental.pallas import tpu as pltpu
from jax.sharding import PartitionSpec as P

HEAD_DIM = 128
BLOCK = 128
NEG = -1e30
MESH = pl.DeviceIdType.MESH
F32 = jnp.float32
BF16 = jnp.bfloat16


def round_up(value, unit):
    return -(-value // unit) * unit


def kernel(
    dims,
    hid,
    inv,
    ctx,
    keep,
    wq,
    wk,
    wv,
    wo,
    kc,
    vc,
    out,
    w_buf,
    wo_buf,
    k_buf,
    v_buf,
    hs,
    part,
    pack,
    send1,
    recv1,
    qkv,
    send3,
    recv3,
    sendml,
    recvml,
    mscr,
    lscr,
    coefs,
    coef_t,
    att,
    att32,
    x_buf,
    send4,
    recv4,
    fin,
    w_sem,
    wo_sem,
    k_sem,
    v_sem,
    s1_sem,
    r1_sem,
    s2_sem,
    r2_sem,
    s3_sem,
    r3_sem,
    sm_sem,
    rm_sem,
    s5_sem,
    r5_sem,
    s4_sem,
    r4_sem,
    s6_sem,
    r6_sem,
):
    n_seq, n_head, batch, verify, kv_local, heads, ctx_local, col_parts = dims
    draft = verify - 1
    group = heads // kv_local
    per = n_seq // batch
    slots = heads + 2 * kv_local
    qrows = verify * heads
    grows = verify * group
    srows = 2 * qrows
    q_cols = heads * HEAD_DIM
    kv_cols = kv_local * HEAD_DIM
    me = lax.axis_index("seq")
    hd = lax.axis_index("head")
    my_b = me // per
    scale = HEAD_DIM ** (-0.5)

    def on_owner(body):
        if per == 1:
            body()
        else:
            pl.when(lax.rem(me, per) == 0)(body)

    barrier = pltpu.get_barrier_semaphore()
    for off in range(1, n_seq):
        pl.semaphore_signal(
            barrier, inc=1, device_id=(lax.rem(me + off, n_seq), hd), device_id_type=MESH
        )
    for off in range(1, n_head):
        pl.semaphore_signal(
            barrier, inc=1, device_id=(me, lax.rem(hd + off, n_head)), device_id_type=MESH
        )

    step = min(512, q_cols)
    pieces = [(wq, c, step, c) for c in range(0, q_cols, step)]
    pieces += [(wk, 0, kv_cols, q_cols), (wv, 0, kv_cols, q_cols + kv_cols)]
    w_copies = []
    for at, (src, c0, width, d0) in enumerate(pieces):
        copy = pltpu.make_async_copy(
            src.at[:, pl.ds(c0, width)], w_buf.at[:, pl.ds(d0, width)], w_sem.at[at]
        )
        copy.start()
        w_copies.append(copy)

    def cache_copies(b):
        return (
            pltpu.make_async_copy(kc.at[b], k_buf.at[b], k_sem.at[b]),
            pltpu.make_async_copy(vc.at[b], v_buf.at[b], v_sem.at[b]),
        )

    @pl.loop(0, batch)
    def _(i):
        b = lax.rem(my_b + i, batch)
        for copy in cache_copies(b):
            copy.start()

    wo_copy = pltpu.make_async_copy(wo, wo_buf, wo_sem)
    wo_copy.start()

    hs[...] = jnp.zeros_like(hs)
    pack[...] = jnp.zeros_like(pack)
    coefs[...] = jnp.zeros_like(coefs)
    for b in range(batch):
        hs[8 * b : 8 * b + verify, :] = hid[b].astype(F32)
    x_in = hs[...].astype(BF16)
    for copy, (src, c0, width, d0) in zip(w_copies, pieces):
        copy.wait()
        part[:, d0 : d0 + width] = jnp.dot(
            x_in, w_buf[:, d0 : d0 + width], preferred_element_type=F32
        )

    pl.semaphore_wait(barrier, n_seq - 1 + n_head - 1)

    def copy1(b, src):
        return pltpu.make_async_remote_copy(
            src_ref=send1.at[b],
            dst_ref=recv1.at[src],
            send_sem=s1_sem.at[b],
            recv_sem=r1_sem.at[src],
            device_id=(b * per, hd),
            device_id_type=MESH,
        )

    @pl.loop(0, batch)
    def _(i):
        b = lax.rem(my_b + 1 + i, batch)
        row = pl.multiple_of(b * 8, 8)
        for s in range(slots):
            pack[verify * s : verify * s + 8, :] = part[
                pl.ds(row, 8), s * HEAD_DIM : (s + 1) * HEAD_DIM
            ]
        send1[b] = pack[...].astype(BF16)

        @pl.when(b * per != me)
        def _():
            copy1(b, me).start()

    def copy_gather(buf, send_sem, recv_sem, b, dst):
        return pltpu.make_async_remote_copy(
            src_ref=buf.at[b],
            dst_ref=buf.at[b],
            send_sem=send_sem.at[dst],
            recv_sem=recv_sem.at[b],
            device_id=(dst, hd),
            device_id_type=MESH,
        )

    def owner_rotate():
        def add(off, acc):
            src = lax.rem(me + off, n_seq)
            copy1(my_b, src).wait_recv()
            return acc + recv1[src].astype(F32)

        total = lax.fori_loop(1, n_seq, add, send1[my_b].astype(F32))
        shape = total.shape
        row = lax.broadcasted_iota(jnp.int32, shape, 0)
        lane = lax.broadcasted_iota(jnp.int32, shape, 1)
        slot = lax.div(row, verify)
        pos = (ctx[my_b] + (row - slot * verify)).astype(F32)
        angle = pos * inv[...]
        turned = slot < heads + kv_local
        cosine = jnp.where(turned, jnp.cos(angle), 1.0)
        sine = jnp.where(turned, jnp.sin(angle), 0.0)
        sine = jnp.where(lane < HEAD_DIM // 2, -sine, sine)
        qkv[my_b] = (total * cosine + pltpu.roll(total, HEAD_DIM // 2, 1) * sine).astype(BF16)

        @pl.loop(1, n_seq)
        def _(off):
            copy_gather(qkv, s2_sem, r2_sem, my_b, lax.rem(me + off, n_seq)).start()

    on_owner(owner_rotate)

    def statistics(peak, total):
        lane = lax.broadcasted_iota(jnp.int32, (srows, HEAD_DIM), 1)
        wide = jnp.where(lane == 0, peak, jnp.where(lane == 1, total, 0.0))
        extra = sendml.shape[2] - srows
        if extra:
            wide = jnp.concatenate([wide, jnp.zeros((extra, HEAD_DIM), F32)], axis=0)
        return wide.T[0:2, :]

    def softmax(scores, mask):
        masked = jnp.where(mask, scores, NEG)
        peak = jnp.max(masked, axis=1, keepdims=True)
        weights = jnp.where(mask, jnp.exp(masked - peak), 0.0)
        return peak, jnp.sum(weights, axis=1, keepdims=True), weights

    def copy3(b, src):
        return pltpu.make_async_remote_copy(
            src_ref=send3.at[b],
            dst_ref=recv3.at[src],
            send_sem=s3_sem.at[b],
            recv_sem=r3_sem.at[src],
            device_id=(b * per, hd),
            device_id_type=MESH,
        )

    def copyml(b, src):
        return pltpu.make_async_remote_copy(
            src_ref=sendml.at[b],
            dst_ref=recvml.at[src],
            send_sem=sm_sem.at[b],
            recv_sem=rm_sem.at[src],
            device_id=(b * per, hd),
            device_id_type=MESH,
        )

    @pl.loop(0, batch)
    def _(i):
        b = lax.rem(my_b + i, batch)

        @pl.when(b * per != me)
        def _():
            copy_gather(qkv, s2_sem, r2_sem, b, me).wait_recv()

        for copy in cache_copies(b):
            copy.wait()
        query = qkv[b].astype(F32)[0:qrows]
        row = lax.broadcasted_iota(jnp.int32, query.shape, 0)
        spread = jnp.concatenate(
            [
                jnp.where((row >= kv * grows) & (row < (kv + 1) * grows), query, 0.0)
                for kv in range(kv_local)
            ],
            axis=1,
        ).astype(BF16)
        scores = (
            lax.dot_general(
                spread, k_buf[b], (((1,), (1,)), ((), ())), preferred_element_type=F32
            )
            * scale
        )
        lane = lax.broadcasted_iota(jnp.int32, (1, ctx_local), 1)
        live = lane + me * ctx_local < ctx[b]
        flags = jnp.concatenate(
            [
                jnp.full((1, BLOCK), keep[b, blk], jnp.int32)
                for blk in range(ctx_local // BLOCK)
            ],
            axis=1,
        )
        kept = live & (flags > 0)
        t_peak, t_total, t_weights = softmax(scores, live)
        d_peak, d_total, d_weights = softmax(scores, kept)
        weights = jnp.concatenate([t_weights, d_weights], axis=0).astype(BF16)
        values = jnp.dot(weights, v_buf[b], preferred_element_type=F32)
        blocks = []
        for half in range(2):
            for kv in range(kv_local):
                r0 = half * qrows + kv * grows
                blocks.append(values[r0 : r0 + grows, kv * HEAD_DIM : (kv + 1) * HEAD_DIM])
        send3[b] = jnp.concatenate(blocks, axis=0).astype(BF16)
        sendml[b] = statistics(
            jnp.concatenate([t_peak, d_peak], axis=0),
            jnp.concatenate([t_total, d_total], axis=0),
        )

        @pl.when(b * per != me)
        def _():
            copy3(b, me).start()
            copyml(b, me).start()

    def owner_merge():
        rows_all = qkv[my_b].astype(F32)
        query = rows_all[0:qrows]
        raw = lax.dot_general(
            query.astype(BF16), qkv[my_b], (((1,), (1,)), ((), ())), preferred_element_type=F32
        )
        scores = raw * scale
        row = lax.broadcasted_iota(jnp.int32, scores.shape, 0)
        col = lax.broadcasted_iota(jnp.int32, scores.shape, 1) - qrows
        row_head = lax.div(row, verify)
        row_j = row - row_head * verify
        row_kv = lax.div(row_head, group)
        first = row_kv * verify
        mask = (col >= first) & (col <= first + row_j)
        peak, total, weights = softmax(scores, mask)
        weights = weights.astype(BF16)
        vrow = lax.broadcasted_iota(jnp.int32, rows_all.shape, 0) - qrows
        shift = kv_local * verify
        moved = pltpu.roll(rows_all, rows_all.shape[0] - shift, 0)
        moved = jnp.where((vrow >= 0) & (vrow < shift), moved, 0.0).astype(BF16)
        values = jnp.dot(weights, moved, preferred_element_type=F32)
        recv3[n_seq] = jnp.concatenate([values, values], axis=0).astype(BF16)
        recvml[n_seq] = statistics(
            jnp.concatenate([peak, peak], axis=0), jnp.concatenate([total, total], axis=0)
        )
        recv3[me] = send3[my_b]
        recvml[me] = sendml[my_b]

        @pl.loop(1, n_seq)
        def _(off):
            src = lax.rem(me + off, n_seq)
            copyml(my_b, src).wait_recv()
            copy3(my_b, src).wait_recv()

        for s in range(n_seq + 1):
            both = recvml[s]
            mscr[s : s + 1, :] = both[0:1]
            lscr[s : s + 1, :] = both[1:2]
        m_all = mscr[0 : n_seq + 1, :]
        l_all = lscr[0 : n_seq + 1, :]
        factor = jnp.exp(m_all - jnp.max(m_all, axis=0, keepdims=True))
        norm = jnp.sum(factor * l_all, axis=0, keepdims=True)
        norm = jnp.where(norm > 0.0, norm, 1.0)
        coefs[0 : n_seq + 1, :] = factor / norm
        coef_t[...] = coefs[...].T
        acc = jnp.zeros((srows, HEAD_DIM), F32)
        for s in range(n_seq + 1):
            acc = acc + coef_t[0:srows, s : s + 1] * recv3[s].astype(F32)
        att[my_b] = acc.astype(BF16)

        @pl.loop(1, n_seq)
        def _(off):
            copy_gather(att, s5_sem, r5_sem, my_b, lax.rem(me + off, n_seq)).start()

    on_owner(owner_merge)

    @pl.loop(0, batch)
    def _(i):
        b = lax.rem(my_b + i, batch)

        @pl.when(b * per != me)
        def _():
            copy_gather(att, s5_sem, r5_sem, b, me).wait_recv()

        att32[pl.ds(pl.multiple_of(b * srows, 8), srows), :] = att[b].astype(F32)

    planes = [j for j in range(verify)] + [qrows + j for j in range(draft)]
    for pair in range(x_buf.shape[0] // 16):
        for h in range(heads):
            halves = []
            for at in (2 * pair, 2 * pair + 1):
                if at < len(planes):
                    halves.append(
                        att32[pl.ds(planes[at] + h * verify, batch, stride=srows), :]
                    )
                else:
                    halves.append(jnp.zeros((batch, HEAD_DIM), F32))
            x_buf[16 * pair : 16 * pair + 16, h * HEAD_DIM : (h + 1) * HEAD_DIM] = (
                jnp.concatenate(halves, axis=0).astype(BF16)
            )

    part_rows, part_cols = send4.shape[1:]

    def place(at):
        return (at // col_parts) * part_rows, (at % col_parts) * part_cols

    def copy4(at, src):
        return pltpu.make_async_remote_copy(
            src_ref=send4.at[at],
            dst_ref=recv4.at[src],
            send_sem=s4_sem.at[at],
            recv_sem=r4_sem.at[src],
            device_id=(me, at),
            device_id_type=MESH,
        )

    wo_copy.wait()
    for at in range(n_head):
        r0, c0 = place(at)
        send4[at] = jnp.dot(
            x_buf[r0 : r0 + part_rows, :],
            wo_buf[:, c0 : c0 + part_cols],
            preferred_element_type=F32,
        ).astype(BF16)

        @pl.when(hd != at)
        def _():
            copy4(at, hd).start()

    def add_head(off, acc):
        src = lax.rem(hd + off, n_head)
        copy4(hd, src).wait_recv()
        return acc + recv4[src].astype(F32)

    fin[hd] = lax.fori_loop(1, n_head, add_head, send4[hd].astype(F32)).astype(BF16)

    def copy6(at, dst):
        return pltpu.make_async_remote_copy(
            src_ref=fin.at[at],
            dst_ref=fin.at[at],
            send_sem=s6_sem.at[dst],
            recv_sem=r6_sem.at[at],
            device_id=(me, dst),
            device_id_type=MESH,
        )

    @pl.loop(1, n_head)
    def _(off):
        copy6(hd, lax.rem(hd + off, n_head)).start()

    @pl.loop(1, n_head)
    def _(off):
        copy6(lax.rem(hd + off, n_head), hd).wait_recv()

    for at in range(n_head):
        r0, c0 = place(at)
        out[r0 : r0 + part_rows, c0 : c0 + part_cols] = fin[at]

    @pl.loop(0, batch)
    def _(b):
        @pl.when(b * per != me)
        def _():
            copy1(b, me).wait_send()
            copy3(b, me).wait_send()
            copyml(b, me).wait_send()

    def owner_sent():
        @pl.loop(1, n_seq)
        def _(off):
            dst = lax.rem(me + off, n_seq)
            copy_gather(qkv, s2_sem, r2_sem, my_b, dst).wait_send()
            copy_gather(att, s5_sem, r5_sem, my_b, dst).wait_send()

    on_owner(owner_sent)

    @pl.loop(1, n_head)
    def _(off):
        dst = lax.rem(hd + off, n_head)
        copy4(dst, hd).wait_send()
        copy6(hd, dst).wait_send()


def per_device(
    n_seq,
    n_head,
    hidden_states,
    w_query,
    w_key,
    w_value,
    w_out,
    key_cache,
    value_cache,
    context_lengths,
    keep_blocks,
):
    batch, verify, width = hidden_states.shape
    draft = verify - 1
    ctx_local = key_cache.shape[1]
    kv_cols = key_cache.shape[2]
    kv_local = kv_cols // HEAD_DIM
    q_cols = w_query.shape[1]
    heads = q_cols // HEAD_DIM
    out_cols = w_out.shape[1]
    slots = heads + 2 * kv_local
    rows1 = round_up(verify * slots, 16)
    srows = 2 * verify * heads
    lanes = round_up(srows, HEAD_DIM)
    n_rows = batch * (verify + draft)
    col_parts = math.gcd(n_head, out_cols // HEAD_DIM)
    row_parts = n_head // col_parts
    part_rows = round_up(-(-n_rows // row_parts), 16)
    part_cols = out_cols // col_parts
    all_rows = part_rows * row_parts
    src_rows = round_up(n_seq + 1, 8)
    dims = (n_seq, n_head, batch, verify, kv_local, heads, ctx_local, col_parts)

    inverse = (500000.0 ** (-(np.arange(HEAD_DIM // 2) * 2.0) / HEAD_DIM)).astype(np.float32)
    inverse = jnp.asarray(np.concatenate([inverse, inverse])[None, :])

    vmem = pl.BlockSpec(memory_space=pltpu.VMEM)
    smem = pl.BlockSpec(memory_space=pltpu.SMEM)
    hbm = pl.BlockSpec(memory_space=pl.ANY)
    dma = pltpu.SemaphoreType.DMA
    result = pl.pallas_call(
        functools.partial(kernel, dims),
        out_shape=jax.ShapeDtypeStruct((all_rows, out_cols), BF16),
        in_specs=[vmem, vmem, smem, smem] + [hbm] * 6,
        out_specs=vmem,
        scratch_shapes=[
            pltpu.VMEM((width, q_cols + 2 * kv_cols), BF16),
            pltpu.VMEM(w_out.shape, BF16),
            pltpu.VMEM(key_cache.shape, BF16),
            pltpu.VMEM(value_cache.shape, BF16),
            pltpu.VMEM((8 * batch, width), F32),
            pltpu.VMEM((8 * batch, q_cols + 2 * kv_cols), F32),
            pltpu.VMEM((rows1, HEAD_DIM), F32),
            pltpu.VMEM((batch, rows1, HEAD_DIM), BF16),
            pltpu.VMEM((n_seq, rows1, HEAD_DIM), BF16),
            pltpu.VMEM((batch, rows1, HEAD_DIM), BF16),
            pltpu.VMEM((batch, srows, HEAD_DIM), BF16),
            pltpu.VMEM((n_seq + 1, srows, HEAD_DIM), BF16),
            pltpu.VMEM((batch, 2, lanes), F32),
            pltpu.VMEM((n_seq + 1, 2, lanes), F32),
            pltpu.VMEM((src_rows, lanes), F32),
            pltpu.VMEM((src_rows, lanes), F32),
            pltpu.VMEM((HEAD_DIM, lanes), F32),
            pltpu.VMEM((lanes, HEAD_DIM), F32),
            pltpu.VMEM((batch, srows, HEAD_DIM), BF16),
            pltpu.VMEM((batch * srows, HEAD_DIM), F32),
            pltpu.VMEM((all_rows, q_cols), BF16),
            pltpu.VMEM((n_head, part_rows, part_cols), BF16),
            pltpu.VMEM((n_head, part_rows, part_cols), BF16),
            pltpu.VMEM((n_head, part_rows, part_cols), BF16),
            dma((q_cols // min(512, q_cols) + 2,)),
            dma,
            dma((batch,)),
            dma((batch,)),
            dma((batch,)),
            dma((n_seq,)),
            dma((n_seq,)),
            dma((batch,)),
            dma((batch,)),
            dma((n_seq,)),
            dma((batch,)),
            dma((n_seq,)),
            dma((n_seq,)),
            dma((batch,)),
            dma((n_head,)),
            dma((n_head,)),
            dma((n_head,)),
            dma((n_head,)),
        ],
        compiler_params=pltpu.CompilerParams(
            collective_id=0, has_side_effects=True, vmem_limit_bytes=56 * 1024 * 1024
        ),
        name="verify_round",
    )(
        hidden_states,
        inverse,
        context_lengths,
        keep_blocks,
        w_query,
        w_key,
        w_value,
        w_out,
        key_cache,
        value_cache,
    )
    target_rows = batch * verify
    verify_out = result[:target_rows].reshape(verify, batch, out_cols).transpose(1, 0, 2)
    draft_out = result[target_rows:n_rows].reshape(draft, batch, out_cols).transpose(1, 0, 2)
    return verify_out, draft_out


def solution(mesh):
    placed = (
        P(None, None, "seq"),
        P("seq", "head"),
        P("seq", "head"),
        P("seq", "head"),
        P("head", "seq"),
        P(None, "seq", "head"),
        P(None, "seq", "head"),
        P(),
        P(None, "seq"),
    )
    return jax.shard_map(
        functools.partial(per_device, mesh.shape["seq"], mesh.shape["head"]),
        mesh=mesh,
        in_specs=placed,
        out_specs=(P(None, None, "seq"), P(None, None, "seq")),
        check_vma=False,
    )
```

```python
import functools
import math

import jax
import jax.numpy as jnp
import numpy as np
from jax import lax
from jax.experimental import pallas as pl
from jax.experimental.pallas import tpu as pltpu
from jax.sharding import PartitionSpec as P

HEAD_DIM = 128
BLOCK = 128
NEG = -1e30
MESH = pl.DeviceIdType.MESH
F32 = jnp.float32
BF16 = jnp.bfloat16


def round_up(value, unit):
    return -(-value // unit) * unit


def kernel(
    dims,
    hid,
    inv,
    ctx,
    keep,
    wq,
    wk,
    wv,
    wo,
    kc,
    vc,
    out_v,
    out_d,
    w_buf,
    wo_buf,
    k_buf,
    v_buf,
    pack,
    send1,
    recv1,
    qkv,
    query_all,
    send3,
    recv3,
    pair3,
    sendml,
    recvml,
    pairml,
    pairs,
    mscr,
    lscr,
    coefs,
    coef_t,
    att,
    att32,
    x_buf,
    send4,
    recv4,
    fin,
    y32,
    w_sem,
    wo_sem,
    k_sem,
    v_sem,
    s1_sem,
    r1_sem,
    s2_sem,
    r2_sem,
    s3_sem,
    r3_sem,
    p3_sem,
    sm_sem,
    rm_sem,
    pm_sem,
    s5_sem,
    r5_sem,
    f5_sem,
    s4_sem,
    r4_sem,
    s6_sem,
    r6_sem,
):
    n_seq, n_head, batch, verify, kv_local, heads, ctx_local, col_parts = dims
    draft = verify - 1
    group = heads // kv_local
    per = n_seq // batch
    slots = heads + 2 * kv_local
    qrows = verify * heads
    grows = verify * group
    srows = 2 * qrows
    q_cols = heads * HEAD_DIM
    kv_cols = kv_local * HEAD_DIM
    me = lax.axis_index("seq")
    hd = lax.axis_index("head")
    my_b = me // per
    scale = HEAD_DIM ** (-0.5) * math.log2(math.e)
    rows1 = send1.shape[1]
    lines = n_seq // 2
    line, side = me // 2, lax.rem(me, 2)
    partner = me + 1 - 2 * side

    def use_order(i):
        if per > 1:
            return lax.rem(my_b + i, batch)
        other = jnp.where((i >= 1) & (i <= lines), 1 - side, side)
        return 2 * lax.rem(line + i, lines) + other

    def gather_order(i):
        if per > 1:
            return lax.rem(my_b + i, batch)
        return 2 * lax.rem(line + i, lines) + jnp.where(i < lines, side, 1 - side)

    def is_mine(b):
        return lax.rem(b * per, 2) == side

    def is_own(b):
        return b * per == me

    def on_owner(body):
        if per == 1:
            body()
        else:
            pl.when(lax.rem(me, per) == 0)(body)

    barrier = pltpu.get_barrier_semaphore()
    for off in range(1, n_seq):
        pl.semaphore_signal(
            barrier, inc=1, device_id=(lax.rem(me + off, n_seq), hd), device_id_type=MESH
        )
    for off in range(1, n_head):
        pl.semaphore_signal(
            barrier, inc=1, device_id=(me, lax.rem(hd + off, n_head)), device_id_type=MESH
        )

    step = min(512, q_cols)
    pieces = [(wq, c, step, c) for c in range(0, q_cols, step)]
    pieces += [(wk, 0, kv_cols, q_cols), (wv, 0, kv_cols, q_cols + kv_cols)]
    w_copies = []
    for at, (src, c0, width, d0) in enumerate(pieces):
        copy = pltpu.make_async_copy(
            src.at[:, pl.ds(c0, width)], w_buf.at[:, pl.ds(d0, width)], w_sem.at[at]
        )
        copy.start()
        w_copies.append(copy)

    def cache_copies(b):
        return (
            pltpu.make_async_copy(kc.at[b], k_buf.at[b], k_sem.at[b]),
            pltpu.make_async_copy(vc.at[b], v_buf.at[b], v_sem.at[b]),
        )

    pack[...] = jnp.zeros_like(pack)
    coefs[...] = jnp.zeros_like(coefs)
    pairs[...] = jnp.zeros_like(pairs)
    x_in = hid[...]
    for copy, (src, c0, width, d0) in zip(w_copies, pieces):
        copy.wait()
        piece = jnp.dot(x_in, w_buf[:, d0 : d0 + width], preferred_element_type=F32)
        for s in range(width // HEAD_DIM):
            slot = d0 // HEAD_DIM + s
            for j in range(verify):
                pack[pl.ds(slot * verify + j, batch, stride=rows1), :] = piece[
                    j * batch : (j + 1) * batch, s * HEAD_DIM : (s + 1) * HEAD_DIM
                ]

    @pl.loop(0, batch)
    def _(i):
        for copy in cache_copies(use_order(i)):
            copy.start()

    wo_copy = pltpu.make_async_copy(wo, wo_buf, wo_sem)
    wo_copy.start()

    pl.semaphore_wait(barrier, n_seq - 1 + n_head - 1)

    def copy1(b, src):
        return pltpu.make_async_remote_copy(
            src_ref=send1.at[b],
            dst_ref=recv1.at[src],
            send_sem=s1_sem.at[b],
            recv_sem=r1_sem.at[src],
            device_id=(b * per, hd),
            device_id_type=MESH,
        )

    @pl.loop(0, batch)
    def _(i):
        b = lax.rem(my_b + 1 + i, batch)
        send1[b] = pack[pl.ds(pl.multiple_of(b * rows1, 16), rows1), :].astype(BF16)

        @pl.when(b * per != me)
        def _():
            copy1(b, me).start()

    def copy_gather(buf, send_sem, recv_sem, b, dst):
        return pltpu.make_async_remote_copy(
            src_ref=buf.at[b],
            dst_ref=buf.at[b],
            send_sem=send_sem.at[dst],
            recv_sem=recv_sem.at[b],
            device_id=(dst, hd),
            device_id_type=MESH,
        )

    def owner_rotate():
        def add(off, acc):
            src = lax.rem(me + off, n_seq)
            copy1(my_b, src).wait_recv()
            return acc + recv1[src].astype(F32)

        total = lax.fori_loop(1, n_seq, add, send1[my_b].astype(F32))
        shape = total.shape
        row = lax.broadcasted_iota(jnp.int32, shape, 0)
        lane = lax.broadcasted_iota(jnp.int32, shape, 1)
        slot = lax.div(row, verify)
        pos = (ctx[my_b] + (row - slot * verify)).astype(F32)
        angle = pos * inv[...]
        turned = slot < heads + kv_local
        cosine = jnp.where(turned, jnp.cos(angle), 1.0)
        sine = jnp.where(turned, jnp.sin(angle), 0.0)
        sine = jnp.where(lane < HEAD_DIM // 2, -sine, sine)
        turned = total * cosine + pltpu.roll(total, HEAD_DIM // 2, 1) * sine
        qkv[...] = turned.astype(BF16)
        query_all[my_b] = turned[0 : query_all.shape[1]].astype(BF16)

        @pl.loop(1, n_seq)
        def _(off):
            if per > 1:
                dst = lax.rem(me + off, n_seq)
            else:
                other = jnp.where(off <= lines, 1 - side, side)
                dst = 2 * lax.rem(line + n_seq - off, lines) + other
            copy_gather(query_all, s2_sem, r2_sem, my_b, dst).start()

    on_owner(owner_rotate)

    def statistics(peak, total):
        lane = lax.broadcasted_iota(jnp.int32, (srows, HEAD_DIM), 1)
        wide = jnp.where(lane == 0, peak, jnp.where(lane == 1, total, 0.0))
        extra = sendml.shape[2] - srows
        if extra:
            wide = jnp.concatenate([wide, jnp.zeros((extra, HEAD_DIM), F32)], axis=0)
        return wide.T[0:2, :]

    def softmax(scores, mask):
        masked = jnp.where(mask, scores, NEG)
        peak = jnp.maximum(jnp.max(masked, axis=1, keepdims=True), NEG / 8)
        weights = jnp.exp2(masked - peak)
        return peak, jnp.sum(weights, axis=1, keepdims=True), weights

    def copies_up(b, src):
        return [
            pltpu.make_async_remote_copy(
                src_ref=source.at[b],
                dst_ref=target.at[src // 2],
                send_sem=send_sem.at[b],
                recv_sem=recv_sem.at[src // 2],
                device_id=(b * per, hd),
                device_id_type=MESH,
            )
            for source, target, send_sem, recv_sem in (
                (sendml, recvml, sm_sem, rm_sem),
                (send3, recv3, s3_sem, r3_sem),
            )
        ]

    def copies_across(b):
        return [
            pltpu.make_async_remote_copy(
                src_ref=source.at[b],
                dst_ref=target.at[b],
                send_sem=send_sem.at[b],
                recv_sem=recv_sem.at[b],
                device_id=(partner, hd),
                device_id_type=MESH,
            )
            for source, target, send_sem, recv_sem in (
                (sendml, pairml, sm_sem, pm_sem),
                (send3, pair3, s3_sem, p3_sem),
            )
        ]

    @pl.loop(0, batch)
    def _(i):
        b = use_order(i)

        @pl.when(b * per != me)
        def _():
            copy_gather(query_all, s2_sem, r2_sem, b, me).wait_recv()

        for copy in cache_copies(b):
            copy.wait()
        query = query_all[b].astype(F32)[0:qrows]
        row = lax.broadcasted_iota(jnp.int32, query.shape, 0)
        spread = jnp.concatenate(
            [
                jnp.where((row >= kv * grows) & (row < (kv + 1) * grows), query, 0.0)
                for kv in range(kv_local)
            ],
            axis=1,
        ).astype(BF16)
        scores = (
            lax.dot_general(
                spread, k_buf[b], (((1,), (1,)), ((), ())), preferred_element_type=F32
            )
            * scale
        )
        lane = lax.broadcasted_iota(jnp.int32, (1, ctx_local), 1)
        live = lane + me * ctx_local < ctx[b]
        flags = jnp.concatenate(
            [
                jnp.full((1, BLOCK), keep[b, blk], jnp.int32)
                for blk in range(ctx_local // BLOCK)
            ],
            axis=1,
        )
        kept = live & (flags > 0)
        t_peak, t_total, t_weights = softmax(scores, live)
        d_peak, d_total, d_weights = softmax(scores, kept)
        weights = jnp.concatenate([t_weights, d_weights], axis=0).astype(BF16)
        values = jnp.dot(weights, v_buf[b], preferred_element_type=F32)
        blocks = []
        for half in range(2):
            for kv in range(kv_local):
                r0 = half * qrows + kv * grows
                blocks.append(values[r0 : r0 + grows, kv * HEAD_DIM : (kv + 1) * HEAD_DIM])
        values = jnp.concatenate(blocks, axis=0)
        peak = jnp.concatenate([t_peak, d_peak], axis=0)
        total = jnp.concatenate([t_total, d_total], axis=0)

        @pl.when(is_own(b))
        def _():
            recv3[line] = values.astype(BF16)
            recvml[line] = statistics(peak, total)

        @pl.when(jnp.logical_not(is_mine(b)))
        def _():
            send3[b] = values.astype(BF16)
            sendml[b] = statistics(peak, total)
            for copy in copies_across(b):
                copy.start()

        @pl.when(is_mine(b) & jnp.logical_not(is_own(b)))
        def _():
            for copy in copies_across(b):
                copy.wait_recv()
            pairs[0:2, :] = pairml[b]
            theirs = pairs[...].T
            their_peak = theirs[0:srows, 0:1]
            joint = jnp.maximum(peak, their_peak)
            ours = jnp.exp2(peak - joint)
            other = jnp.exp2(their_peak - joint)
            send3[b] = (values * ours + pair3[b].astype(F32) * other).astype(BF16)
            sendml[b] = statistics(joint, total * ours + theirs[0:srows, 1:2] * other)
            for copy in copies_up(b, me):
                copy.start()

    def owner_merge():
        rows_all = qkv[...].astype(F32)
        query = rows_all[0:qrows]
        raw = lax.dot_general(
            query.astype(BF16), qkv[...], (((1,), (1,)), ((), ())), preferred_element_type=F32
        )
        scores = raw * scale
        row = lax.broadcasted_iota(jnp.int32, scores.shape, 0)
        col = lax.broadcasted_iota(jnp.int32, scores.shape, 1) - qrows
        row_head = lax.div(row, verify)
        row_j = row - row_head * verify
        row_kv = lax.div(row_head, group)
        first = row_kv * verify
        mask = (col >= first) & (col <= first + row_j)
        peak, total, weights = softmax(scores, mask)
        weights = weights.astype(BF16)
        vrow = lax.broadcasted_iota(jnp.int32, rows_all.shape, 0) - qrows
        shift = kv_local * verify
        moved = pltpu.roll(rows_all, rows_all.shape[0] - shift, 0)
        moved = jnp.where((vrow >= 0) & (vrow < shift), moved, 0.0).astype(BF16)
        values = jnp.dot(weights, moved, preferred_element_type=F32)
        fresh = lines + 1
        recv3[fresh] = jnp.concatenate([values, values], axis=0).astype(BF16)
        recvml[fresh] = statistics(
            jnp.concatenate([peak, peak], axis=0), jnp.concatenate([total, total], axis=0)
        )
        for copy in copies_across(my_b):
            copy.wait_recv()
        recv3[lines] = pair3[my_b]
        recvml[lines] = pairml[my_b]

        @pl.loop(1, lines)
        def _(off):
            for copy in copies_up(my_b, 2 * lax.rem(line + off, lines)):
                copy.wait_recv()

        n_src = lines + 2
        for s in range(n_src):
            both = recvml[s]
            mscr[s : s + 1, :] = both[0:1]
            lscr[s : s + 1, :] = both[1:2]
        m_all = mscr[0:n_src, :]
        l_all = lscr[0:n_src, :]
        factor = jnp.exp2(m_all - jnp.max(m_all, axis=0, keepdims=True))
        norm = jnp.sum(factor * l_all, axis=0, keepdims=True)
        norm = jnp.where(norm > 0.0, norm, 1.0)
        coefs[0:n_src, :] = factor / norm
        coef_t[...] = coefs[...].T
        acc = jnp.zeros((srows, HEAD_DIM), F32)
        for s in range(n_src):
            acc = acc + coef_t[0:srows, s : s + 1] * recv3[s].astype(F32)
        att[my_b] = acc.astype(BF16)

        copy_gather(att, s5_sem, r5_sem, my_b, partner).start()

        @pl.loop(1, lines)
        def _(off):
            dst = 2 * lax.rem(line + off, lines) + side
            copy_gather(att, s5_sem, r5_sem, my_b, dst).start()

    on_owner(owner_merge)

    def copy_forward(b):
        return pltpu.make_async_remote_copy(
            src_ref=att.at[b],
            dst_ref=att.at[b],
            send_sem=f5_sem.at[b],
            recv_sem=r5_sem.at[b],
            device_id=(partner, hd),
            device_id_type=MESH,
        )

    @pl.loop(0, batch)
    def _(i):
        b = gather_order(i)

        @pl.when(jnp.logical_not(is_own(b)))
        def _():
            copy_forward(b).wait_recv()

        @pl.when(is_mine(b) & jnp.logical_not(is_own(b)))
        def _():
            copy_forward(b).start()

        att32[pl.ds(pl.multiple_of(b * srows, 8), srows), :] = att[b].astype(F32)

    planes = [j for j in range(verify)] + [qrows + j for j in range(draft)]
    for pair in range(x_buf.shape[0] // 16):
        for h in range(heads):
            halves = []
            for at in (2 * pair, 2 * pair + 1):
                if at < len(planes):
                    halves.append(
                        att32[pl.ds(planes[at] + h * verify, batch, stride=srows), :]
                    )
                else:
                    halves.append(jnp.zeros((batch, HEAD_DIM), F32))
            x_buf[16 * pair : 16 * pair + 16, h * HEAD_DIM : (h + 1) * HEAD_DIM] = (
                jnp.concatenate(halves, axis=0).astype(BF16)
            )

    part_rows, part_cols = send4.shape[1:]
    all_rows = x_buf.shape[0]

    def place(at):
        return (at // col_parts) * part_rows, (at % col_parts) * part_cols

    def copy4(at, src):
        return pltpu.make_async_remote_copy(
            src_ref=send4.at[at],
            dst_ref=recv4.at[src],
            send_sem=s4_sem.at[at],
            recv_sem=r4_sem.at[src],
            device_id=(me, at),
            device_id_type=MESH,
        )

    wo_copy.wait()
    for at in range(n_head):
        r0, c0 = place(at)
        send4[at] = jnp.dot(
            x_buf[r0 : r0 + part_rows, :],
            wo_buf[:, c0 : c0 + part_cols],
            preferred_element_type=F32,
        ).astype(BF16)

        @pl.when(hd != at)
        def _():
            copy4(at, hd).start()

    def add_head(off, acc):
        src = lax.rem(hd + off, n_head)
        copy4(hd, src).wait_recv()
        return acc + recv4[src].astype(F32)

    fin[hd] = lax.fori_loop(1, n_head, add_head, send4[hd].astype(F32)).astype(BF16)

    def copy6(at, dst):
        return pltpu.make_async_remote_copy(
            src_ref=fin.at[at],
            dst_ref=fin.at[at],
            send_sem=s6_sem.at[dst],
            recv_sem=r6_sem.at[at],
            device_id=(me, dst),
            device_id_type=MESH,
        )

    @pl.loop(1, n_head)
    def _(off):
        copy6(hd, lax.rem(hd + off, n_head)).start()

    @pl.loop(1, n_head)
    def _(off):
        copy6(lax.rem(hd + off, n_head), hd).wait_recv()

    for at in range(n_head):
        r0, c0 = place(at)
        for c in range(part_cols // HEAD_DIM):
            base = (c0 // HEAD_DIM + c) * all_rows + r0
            y32[base : base + part_rows, :] = fin[
                at, :, c * HEAD_DIM : (c + 1) * HEAD_DIM
            ].astype(F32)
    target_rows = verify * batch
    chunks = range(out_v.shape[1] // HEAD_DIM)
    for c in chunks:
        out_v[:, c * HEAD_DIM : (c + 1) * HEAD_DIM] = y32[
            c * all_rows : c * all_rows + target_rows, :
        ].astype(BF16)
    for b in range(batch):
        out_d[b] = jnp.concatenate(
            [
                y32[pl.ds(c * all_rows + target_rows + b, draft, stride=batch), :]
                for c in chunks
            ],
            axis=1,
        ).astype(BF16)

    @pl.loop(0, batch)
    def _(b):
        @pl.when(b * per != me)
        def _():
            copy1(b, me).wait_send()
            for copy in copies_up(b, me):
                copy.wait_send()

        @pl.when(is_mine(b) & jnp.logical_not(is_own(b)))
        def _():
            copy_forward(b).wait_send()

    def owner_sent():
        @pl.loop(1, n_seq)
        def _(off):
            dst = lax.rem(me + off, n_seq)
            copy_gather(query_all, s2_sem, r2_sem, my_b, dst).wait_send()

            @pl.when((dst == partner) | (lax.rem(dst, 2) == side))
            def _():
                copy_gather(att, s5_sem, r5_sem, my_b, dst).wait_send()

    on_owner(owner_sent)

    @pl.loop(1, n_head)
    def _(off):
        dst = lax.rem(hd + off, n_head)
        copy4(dst, hd).wait_send()
        copy6(hd, dst).wait_send()


def per_device(
    n_seq,
    n_head,
    hidden_states,
    w_query,
    w_key,
    w_value,
    w_out,
    key_cache,
    value_cache,
    context_lengths,
    keep_blocks,
):
    batch, verify, width = hidden_states.shape
    draft = verify - 1
    ctx_local = key_cache.shape[1]
    kv_cols = key_cache.shape[2]
    kv_local = kv_cols // HEAD_DIM
    q_cols = w_query.shape[1]
    heads = q_cols // HEAD_DIM
    out_cols = w_out.shape[1]
    slots = heads + 2 * kv_local
    rows1 = round_up(verify * slots, 16)
    srows = 2 * verify * heads
    lanes = round_up(srows, HEAD_DIM)
    n_rows = batch * (verify + draft)
    col_parts = math.gcd(n_head, out_cols // HEAD_DIM)
    row_parts = n_head // col_parts
    part_rows = round_up(-(-n_rows // row_parts), 16)
    part_cols = out_cols // col_parts
    all_rows = part_rows * row_parts
    n_src = n_seq // 2 + 2
    src_rows = round_up(n_src, 8)
    qpad = round_up(verify * heads, 16)
    dims = (n_seq, n_head, batch, verify, kv_local, heads, ctx_local, col_parts)

    inverse = (500000.0 ** (-(np.arange(HEAD_DIM // 2) * 2.0) / HEAD_DIM)).astype(np.float32)
    inverse = jnp.asarray(np.concatenate([inverse, inverse])[None, :])

    vmem = pl.BlockSpec(memory_space=pltpu.VMEM)
    smem = pl.BlockSpec(memory_space=pltpu.SMEM)
    hbm = pl.BlockSpec(memory_space=pl.ANY)
    dma = pltpu.SemaphoreType.DMA
    target, drafted = pl.pallas_call(
        functools.partial(kernel, dims),
        out_shape=(
            jax.ShapeDtypeStruct((batch * verify, out_cols), BF16),
            jax.ShapeDtypeStruct((batch, draft, out_cols), BF16),
        ),
        in_specs=[vmem, vmem, smem, smem] + [hbm] * 6,
        out_specs=(vmem, vmem),
        scratch_shapes=[
            pltpu.VMEM((width, q_cols + 2 * kv_cols), BF16),
            pltpu.VMEM(w_out.shape, BF16),
            pltpu.VMEM(key_cache.shape, BF16),
            pltpu.VMEM(value_cache.shape, BF16),
            pltpu.VMEM((batch * rows1, HEAD_DIM), F32),
            pltpu.VMEM((batch, rows1, HEAD_DIM), BF16),
            pltpu.VMEM((n_seq, rows1, HEAD_DIM), BF16),
            pltpu.VMEM((rows1, HEAD_DIM), BF16),
            pltpu.VMEM((batch, qpad, HEAD_DIM), BF16),
            pltpu.VMEM((batch, srows, HEAD_DIM), BF16),
            pltpu.VMEM((n_src, srows, HEAD_DIM), BF16),
            pltpu.VMEM((batch, srows, HEAD_DIM), BF16),
            pltpu.VMEM((batch, 2, lanes), F32),
            pltpu.VMEM((n_src, 2, lanes), F32),
            pltpu.VMEM((batch, 2, lanes), F32),
            pltpu.VMEM((HEAD_DIM, lanes), F32),
            pltpu.VMEM((src_rows, lanes), F32),
            pltpu.VMEM((src_rows, lanes), F32),
            pltpu.VMEM((HEAD_DIM, lanes), F32),
            pltpu.VMEM((lanes, HEAD_DIM), F32),
            pltpu.VMEM((batch, srows, HEAD_DIM), BF16),
            pltpu.VMEM((batch * srows, HEAD_DIM), F32),
            pltpu.VMEM((all_rows, q_cols), BF16),
            pltpu.VMEM((n_head, part_rows, part_cols), BF16),
            pltpu.VMEM((n_head, part_rows, part_cols), BF16),
            pltpu.VMEM((n_head, part_rows, part_cols), BF16),
            pltpu.VMEM((out_cols // HEAD_DIM * all_rows, HEAD_DIM), F32),
            dma((q_cols // min(512, q_cols) + 2,)),
            dma,
            dma((batch,)),
            dma((batch,)),
            dma((batch,)),
            dma((n_seq,)),
            dma((n_seq,)),
            dma((batch,)),
            dma((batch,)),
            dma((n_seq // 2,)),
            dma((batch,)),
            dma((batch,)),
            dma((n_seq // 2,)),
            dma((batch,)),
            dma((n_seq,)),
            dma((batch,)),
            dma((batch,)),
            dma((n_head,)),
            dma((n_head,)),
            dma((n_head,)),
            dma((n_head,)),
        ],
        compiler_params=pltpu.CompilerParams(
            collective_id=0, has_side_effects=True, vmem_limit_bytes=56 * 1024 * 1024
        ),
        name="verify_round",
    )(
        hidden_states.transpose(1, 0, 2).reshape(verify * batch, width),
        inverse,
        context_lengths,
        keep_blocks,
        w_query,
        w_key,
        w_value,
        w_out,
        key_cache,
        value_cache,
    )
    return target.reshape(verify, batch, out_cols).transpose(1, 0, 2), drafted


def solution(mesh):
    placed = (
        P(None, None, "seq"),
        P("seq", "head"),
        P("seq", "head"),
        P("seq", "head"),
        P("head", "seq"),
        P(None, "seq", "head"),
        P(None, "seq", "head"),
        P(),
        P(None, "seq"),
    )
    return jax.shard_map(
        functools.partial(per_device, mesh.shape["seq"], mesh.shape["head"]),
        mesh=mesh,
        in_specs=placed,
        out_specs=(P(None, None, "seq"), P(None, None, "seq")),
        check_vma=False,
    )
```

```python
import functools
import math

import jax
import jax.numpy as jnp
import numpy as np
from jax import lax
from jax.experimental import pallas as pl
from jax.experimental.pallas import tpu as pltpu
from jax.sharding import PartitionSpec as P

HEAD_DIM = 128
BLOCK = 128
NEG = -1e30
MESH = pl.DeviceIdType.MESH
F32 = jnp.float32
BF16 = jnp.bfloat16


def round_up(value, unit):
    return -(-value // unit) * unit


def kernel(
    dims,
    hid,
    inv,
    ctx,
    keep,
    wq,
    wk,
    wv,
    wo,
    kc,
    vc,
    out_v,
    out_d,
    w_buf,
    wo_buf,
    k_buf,
    v_buf,
    pack,
    send1,
    recv1,
    qkv,
    query_all,
    send3,
    recv3,
    sendml,
    recvml,
    cos_buf,
    sin_buf,
    mscr,
    lscr,
    coefs,
    coef_t,
    att,
    att32,
    x_buf,
    send4,
    recv4,
    fin,
    y32,
    w_sem,
    wo_sem,
    k_sem,
    v_sem,
    s1_sem,
    r1_sem,
    s2_sem,
    r2_sem,
    s3_sem,
    r3_sem,
    sm_sem,
    rm_sem,
    s5_sem,
    r5_sem,
    f5_sem,
    s4_sem,
    r4_sem,
    s6_sem,
    r6_sem,
):
    n_seq, n_head, batch, verify, kv_local, heads, ctx_local, col_parts = dims
    draft = verify - 1
    group = heads // kv_local
    per = n_seq // batch
    slots = heads + 2 * kv_local
    qrows = verify * heads
    grows = verify * group
    srows = 2 * qrows
    q_cols = heads * HEAD_DIM
    kv_cols = kv_local * HEAD_DIM
    me = lax.axis_index("seq")
    hd = lax.axis_index("head")
    my_b = me // per
    scale = HEAD_DIM ** (-0.5) * math.log2(math.e)
    rows1 = send1.shape[1]
    lines = n_seq // 2
    line, side = me // 2, lax.rem(me, 2)
    partner = me + 1 - 2 * side

    def use_order(i):
        if per > 1:
            return lax.rem(my_b + i, batch)
        return 2 * lax.rem(line + i // 2, lines) + lax.rem(side + i, 2)

    def gather_order(i):
        if per > 1:
            return lax.rem(my_b + i, batch)
        return 2 * lax.rem(line + i, lines) + jnp.where(i < lines, side, 1 - side)

    def is_mine(b):
        return lax.rem(b * per, 2) == side

    def is_own(b):
        return b * per == me

    def on_owner(body):
        if per == 1:
            body()
        else:
            pl.when(lax.rem(me, per) == 0)(body)

    barrier = pltpu.get_barrier_semaphore()
    for off in range(1, n_seq):
        pl.semaphore_signal(
            barrier, inc=1, device_id=(lax.rem(me + off, n_seq), hd), device_id_type=MESH
        )
    for off in range(1, n_head):
        pl.semaphore_signal(
            barrier, inc=1, device_id=(me, lax.rem(hd + off, n_head)), device_id_type=MESH
        )

    step = min(512, q_cols)
    pieces = [(wq, c, step, c) for c in range(0, q_cols, step)]
    pieces += [(wk, 0, kv_cols, q_cols), (wv, 0, kv_cols, q_cols + kv_cols)]
    w_copies = []
    for at, (src, c0, width, d0) in enumerate(pieces):
        copy = pltpu.make_async_copy(
            src.at[:, pl.ds(c0, width)], w_buf.at[:, pl.ds(d0, width)], w_sem.at[at]
        )
        copy.start()
        w_copies.append(copy)

    def cache_copies(b):
        return (
            pltpu.make_async_copy(kc.at[b], k_buf.at[b], k_sem.at[b]),
            pltpu.make_async_copy(vc.at[b], v_buf.at[b], v_sem.at[b]),
        )

    def rotation():
        shape = cos_buf.shape
        row = lax.broadcasted_iota(jnp.int32, shape, 0)
        lane = lax.broadcasted_iota(jnp.int32, shape, 1)
        slot = lax.div(row, verify)
        pos = (ctx[my_b] + (row - slot * verify)).astype(F32)
        angle = pos * inv[...]
        turned = slot < heads + kv_local
        sine = jnp.where(turned, jnp.sin(angle), 0.0)
        cos_buf[...] = jnp.where(turned, jnp.cos(angle), 1.0)
        sin_buf[...] = jnp.where(lane < HEAD_DIM // 2, -sine, sine)

    on_owner(rotation)

    pack[...] = jnp.zeros_like(pack)
    coefs[...] = jnp.zeros_like(coefs)
    x_in = hid[...]
    for copy, (src, c0, width, d0) in zip(w_copies, pieces):
        copy.wait()
        piece = jnp.dot(x_in, w_buf[:, d0 : d0 + width], preferred_element_type=F32)
        for s in range(width // HEAD_DIM):
            slot = d0 // HEAD_DIM + s
            for j in range(verify):
                pack[pl.ds(slot * verify + j, batch, stride=rows1), :] = piece[
                    j * batch : (j + 1) * batch, s * HEAD_DIM : (s + 1) * HEAD_DIM
                ]

    @pl.loop(0, batch)
    def _(i):
        for copy in cache_copies(use_order(i)):
            copy.start()

    wo_copy = pltpu.make_async_copy(wo, wo_buf, wo_sem)
    wo_copy.start()

    pl.semaphore_wait(barrier, n_seq - 1 + n_head - 1)

    def copy1(b, src):
        return pltpu.make_async_remote_copy(
            src_ref=send1.at[b],
            dst_ref=recv1.at[src],
            send_sem=s1_sem.at[b],
            recv_sem=r1_sem.at[src],
            device_id=(b * per, hd),
            device_id_type=MESH,
        )

    @pl.loop(0, batch)
    def _(i):
        b = lax.rem(my_b + 1 + i, batch)
        send1[b] = pack[pl.ds(pl.multiple_of(b * rows1, 16), rows1), :].astype(BF16)

        @pl.when(b * per != me)
        def _():
            copy1(b, me).start()

    def copy_gather(buf, send_sem, recv_sem, b, dst):
        return pltpu.make_async_remote_copy(
            src_ref=buf.at[b],
            dst_ref=buf.at[b],
            send_sem=send_sem.at[dst],
            recv_sem=recv_sem.at[b],
            device_id=(dst, hd),
            device_id_type=MESH,
        )

    def owner_rotate():
        def add(off, acc):
            src = lax.rem(me + off, n_seq)
            copy1(my_b, src).wait_recv()
            return acc + recv1[src].astype(F32)

        total = lax.fori_loop(1, n_seq, add, send1[my_b].astype(F32))
        turned = total * cos_buf[...] + pltpu.roll(total, HEAD_DIM // 2, 1) * sin_buf[...]
        qkv[...] = turned.astype(BF16)
        query_all[my_b] = turned[0 : query_all.shape[1]].astype(BF16)

        @pl.loop(1, n_seq)
        def _(off):
            if per > 1:
                dst = lax.rem(me + off, n_seq)
            else:
                dst = 2 * lax.rem(line + n_seq - off // 2, lines) + lax.rem(side + off, 2)
            copy_gather(query_all, s2_sem, r2_sem, my_b, dst).start()

    on_owner(owner_rotate)

    def statistics(peak, total):
        lane = lax.broadcasted_iota(jnp.int32, (srows, HEAD_DIM), 1)
        wide = jnp.where(lane == 0, peak, jnp.where(lane == 1, total, 0.0))
        extra = sendml.shape[2] - srows
        if extra:
            wide = jnp.concatenate([wide, jnp.zeros((extra, HEAD_DIM), F32)], axis=0)
        return wide.T[0:2, :]

    def softmax(scores, mask):
        masked = jnp.where(mask, scores, NEG)
        peak = jnp.maximum(jnp.max(masked, axis=1, keepdims=True), NEG / 8)
        weights = jnp.exp2(masked - peak)
        return peak, jnp.sum(weights, axis=1, keepdims=True), weights

    def copies_up(b, src):
        return [
            pltpu.make_async_remote_copy(
                src_ref=source.at[b],
                dst_ref=target.at[src],
                send_sem=send_sem.at[b],
                recv_sem=recv_sem.at[src],
                device_id=(b * per, hd),
                device_id_type=MESH,
            )
            for source, target, send_sem, recv_sem in (
                (sendml, recvml, sm_sem, rm_sem),
                (send3, recv3, s3_sem, r3_sem),
            )
        ]

    def attend(b):
        query = query_all[b].astype(F32)[0:qrows]
        row = lax.broadcasted_iota(jnp.int32, query.shape, 0)
        spread = jnp.concatenate(
            [
                jnp.where((row >= kv * grows) & (row < (kv + 1) * grows), query, 0.0)
                for kv in range(kv_local)
            ],
            axis=1,
        ).astype(BF16)
        scores = (
            lax.dot_general(
                spread, k_buf[b], (((1,), (1,)), ((), ())), preferred_element_type=F32
            )
            * scale
        )
        lane = lax.broadcasted_iota(jnp.int32, (1, ctx_local), 1)
        live = lane + me * ctx_local < ctx[b]
        flags = jnp.concatenate(
            [
                jnp.full((1, BLOCK), keep[b, blk], jnp.int32)
                for blk in range(ctx_local // BLOCK)
            ],
            axis=1,
        )
        kept = live & (flags > 0)
        t_peak, t_total, t_weights = softmax(scores, live)
        d_peak, d_total, d_weights = softmax(scores, kept)
        weights = jnp.concatenate([t_weights, d_weights], axis=0).astype(BF16)
        values = jnp.dot(weights, v_buf[b], preferred_element_type=F32)
        blocks = []
        for half in range(2):
            for kv in range(kv_local):
                r0 = half * qrows + kv * grows
                blocks.append(values[r0 : r0 + grows, kv * HEAD_DIM : (kv + 1) * HEAD_DIM])
        send3[b] = jnp.concatenate(blocks, axis=0).astype(BF16)
        sendml[b] = statistics(
            jnp.concatenate([t_peak, d_peak], axis=0),
            jnp.concatenate([t_total, d_total], axis=0),
        )

    together = 2

    @pl.loop(0, batch // together)
    def _(i):
        several = [use_order(i * together + at) for at in range(together)]
        for b in several:

            @pl.when(jnp.logical_not(is_own(b)))
            def _(b=b):
                copy_gather(query_all, s2_sem, r2_sem, b, me).wait_recv()

            for copy in cache_copies(b):
                copy.wait()
        for b in several:
            attend(b)
        for b in several:

            @pl.when(jnp.logical_not(is_own(b)))
            def _(b=b):
                for copy in copies_up(b, me):
                    copy.start()

    def owner_merge():
        rows_all = qkv[...].astype(F32)
        query = rows_all[0:qrows]
        raw = lax.dot_general(
            query.astype(BF16), qkv[...], (((1,), (1,)), ((), ())), preferred_element_type=F32
        )
        scores = raw * scale
        row = lax.broadcasted_iota(jnp.int32, scores.shape, 0)
        col = lax.broadcasted_iota(jnp.int32, scores.shape, 1) - qrows
        row_head = lax.div(row, verify)
        row_j = row - row_head * verify
        row_kv = lax.div(row_head, group)
        first = row_kv * verify
        mask = (col >= first) & (col <= first + row_j)
        peak, total, weights = softmax(scores, mask)
        weights = weights.astype(BF16)
        vrow = lax.broadcasted_iota(jnp.int32, rows_all.shape, 0) - qrows
        shift = kv_local * verify
        moved = pltpu.roll(rows_all, rows_all.shape[0] - shift, 0)
        moved = jnp.where((vrow >= 0) & (vrow < shift), moved, 0.0).astype(BF16)
        values = jnp.dot(weights, moved, preferred_element_type=F32)
        recv3[n_seq] = jnp.concatenate([values, values], axis=0).astype(BF16)
        recvml[n_seq] = statistics(
            jnp.concatenate([peak, peak], axis=0), jnp.concatenate([total, total], axis=0)
        )
        recv3[me] = send3[my_b]
        recvml[me] = sendml[my_b]

        @pl.loop(1, n_seq)
        def _(off):
            for copy in copies_up(my_b, lax.rem(me + off, n_seq)):
                copy.wait_recv()

        n_src = n_seq + 1
        for s in range(n_src):
            both = recvml[s]
            mscr[s : s + 1, :] = both[0:1]
            lscr[s : s + 1, :] = both[1:2]
        m_all = mscr[0:n_src, :]
        l_all = lscr[0:n_src, :]
        factor = jnp.exp2(m_all - jnp.max(m_all, axis=0, keepdims=True))
        norm = jnp.sum(factor * l_all, axis=0, keepdims=True)
        norm = jnp.where(norm > 0.0, norm, 1.0)
        coefs[0:n_src, :] = factor / norm
        coef_t[...] = coefs[...].T
        acc = jnp.zeros((srows, HEAD_DIM), F32)
        for s in range(n_src):
            acc = acc + coef_t[0:srows, s : s + 1] * recv3[s].astype(F32)
        att[my_b] = acc.astype(BF16)

        copy_gather(att, s5_sem, r5_sem, my_b, partner).start()

        @pl.loop(1, lines)
        def _(off):
            dst = 2 * lax.rem(line + off, lines) + side
            copy_gather(att, s5_sem, r5_sem, my_b, dst).start()

    on_owner(owner_merge)

    def copy_forward(b):
        return pltpu.make_async_remote_copy(
            src_ref=att.at[b],
            dst_ref=att.at[b],
            send_sem=f5_sem.at[b],
            recv_sem=r5_sem.at[b],
            device_id=(partner, hd),
            device_id_type=MESH,
        )

    @pl.loop(0, batch)
    def _(i):
        b = gather_order(i)

        @pl.when(jnp.logical_not(is_own(b)))
        def _():
            copy_forward(b).wait_recv()

        @pl.when(is_mine(b) & jnp.logical_not(is_own(b)))
        def _():
            copy_forward(b).start()

        att32[pl.ds(pl.multiple_of(b * srows, 8), srows), :] = att[b].astype(F32)

    planes = [j for j in range(verify)] + [qrows + j for j in range(draft)]
    for pair in range(x_buf.shape[0] // 16):
        for h in range(heads):
            halves = []
            for at in (2 * pair, 2 * pair + 1):
                if at < len(planes):
                    halves.append(
                        att32[pl.ds(planes[at] + h * verify, batch, stride=srows), :]
                    )
                else:
                    halves.append(jnp.zeros((batch, HEAD_DIM), F32))
            x_buf[16 * pair : 16 * pair + 16, h * HEAD_DIM : (h + 1) * HEAD_DIM] = (
                jnp.concatenate(halves, axis=0).astype(BF16)
            )

    part_rows, part_cols = send4.shape[1:]
    all_rows = x_buf.shape[0]

    def place(at):
        return (at // col_parts) * part_rows, (at % col_parts) * part_cols

    def copy4(at, src):
        return pltpu.make_async_remote_copy(
            src_ref=send4.at[at],
            dst_ref=recv4.at[src],
            send_sem=s4_sem.at[at],
            recv_sem=r4_sem.at[src],
            device_id=(me, at),
            device_id_type=MESH,
        )

    wo_copy.wait()
    for at in range(n_head):
        r0, c0 = place(at)
        send4[at] = jnp.dot(
            x_buf[r0 : r0 + part_rows, :],
            wo_buf[:, c0 : c0 + part_cols],
            preferred_element_type=F32,
        ).astype(BF16)

        @pl.when(hd != at)
        def _():
            copy4(at, hd).start()

    def add_head(off, acc):
        src = lax.rem(hd + off, n_head)
        copy4(hd, src).wait_recv()
        return acc + recv4[src].astype(F32)

    fin[hd] = lax.fori_loop(1, n_head, add_head, send4[hd].astype(F32)).astype(BF16)

    def copy6(at, dst):
        return pltpu.make_async_remote_copy(
            src_ref=fin.at[at],
            dst_ref=fin.at[at],
            send_sem=s6_sem.at[dst],
            recv_sem=r6_sem.at[at],
            device_id=(me, dst),
            device_id_type=MESH,
        )

    @pl.loop(1, n_head)
    def _(off):
        copy6(hd, lax.rem(hd + off, n_head)).start()

    @pl.loop(1, n_head)
    def _(off):
        copy6(lax.rem(hd + off, n_head), hd).wait_recv()

    for at in range(n_head):
        r0, c0 = place(at)
        for c in range(part_cols // HEAD_DIM):
            base = (c0 // HEAD_DIM + c) * all_rows + r0
            y32[base : base + part_rows, :] = fin[
                at, :, c * HEAD_DIM : (c + 1) * HEAD_DIM
            ].astype(F32)
    target_rows = verify * batch
    chunks = range(out_v.shape[1] // HEAD_DIM)
    for c in chunks:
        out_v[:, c * HEAD_DIM : (c + 1) * HEAD_DIM] = y32[
            c * all_rows : c * all_rows + target_rows, :
        ].astype(BF16)
    for b in range(batch):
        out_d[b] = jnp.concatenate(
            [
                y32[pl.ds(c * all_rows + target_rows + b, draft, stride=batch), :]
                for c in chunks
            ],
            axis=1,
        ).astype(BF16)

    @pl.loop(0, batch)
    def _(b):
        @pl.when(b * per != me)
        def _():
            copy1(b, me).wait_send()
            for copy in copies_up(b, me):
                copy.wait_send()

        @pl.when(is_mine(b) & jnp.logical_not(is_own(b)))
        def _():
            copy_forward(b).wait_send()

    def owner_sent():
        @pl.loop(1, n_seq)
        def _(off):
            dst = lax.rem(me + off, n_seq)
            copy_gather(query_all, s2_sem, r2_sem, my_b, dst).wait_send()

            @pl.when((dst == partner) | (lax.rem(dst, 2) == side))
            def _():
                copy_gather(att, s5_sem, r5_sem, my_b, dst).wait_send()

    on_owner(owner_sent)

    @pl.loop(1, n_head)
    def _(off):
        dst = lax.rem(hd + off, n_head)
        copy4(dst, hd).wait_send()
        copy6(hd, dst).wait_send()


def per_device(
    n_seq,
    n_head,
    hidden_states,
    w_query,
    w_key,
    w_value,
    w_out,
    key_cache,
    value_cache,
    context_lengths,
    keep_blocks,
):
    batch, verify, width = hidden_states.shape
    draft = verify - 1
    ctx_local = key_cache.shape[1]
    kv_cols = key_cache.shape[2]
    kv_local = kv_cols // HEAD_DIM
    q_cols = w_query.shape[1]
    heads = q_cols // HEAD_DIM
    out_cols = w_out.shape[1]
    slots = heads + 2 * kv_local
    rows1 = round_up(verify * slots, 16)
    srows = 2 * verify * heads
    lanes = round_up(srows, HEAD_DIM)
    n_rows = batch * (verify + draft)
    col_parts = math.gcd(n_head, out_cols // HEAD_DIM)
    row_parts = n_head // col_parts
    part_rows = round_up(-(-n_rows // row_parts), 16)
    part_cols = out_cols // col_parts
    all_rows = part_rows * row_parts
    n_src = n_seq + 1
    src_rows = round_up(n_src, 8)
    qpad = round_up(verify * heads, 16)
    dims = (n_seq, n_head, batch, verify, kv_local, heads, ctx_local, col_parts)

    inverse = (500000.0 ** (-(np.arange(HEAD_DIM // 2) * 2.0) / HEAD_DIM)).astype(np.float32)
    inverse = jnp.asarray(np.concatenate([inverse, inverse])[None, :])

    vmem = pl.BlockSpec(memory_space=pltpu.VMEM)
    smem = pl.BlockSpec(memory_space=pltpu.SMEM)
    hbm = pl.BlockSpec(memory_space=pl.ANY)
    dma = pltpu.SemaphoreType.DMA
    target, drafted = pl.pallas_call(
        functools.partial(kernel, dims),
        out_shape=(
            pltpu.VMEM((batch * verify, out_cols), BF16),
            pltpu.VMEM((batch, draft, out_cols), BF16),
        ),
        in_specs=[vmem, vmem, smem, smem] + [hbm] * 6,
        out_specs=(vmem, vmem),
        scratch_shapes=[
            pltpu.VMEM((width, q_cols + 2 * kv_cols), BF16),
            pltpu.VMEM(w_out.shape, BF16),
            pltpu.VMEM(key_cache.shape, BF16),
            pltpu.VMEM(value_cache.shape, BF16),
            pltpu.VMEM((batch * rows1, HEAD_DIM), F32),
            pltpu.VMEM((batch, rows1, HEAD_DIM), BF16),
            pltpu.VMEM((n_seq, rows1, HEAD_DIM), BF16),
            pltpu.VMEM((rows1, HEAD_DIM), BF16),
            pltpu.VMEM((batch, qpad, HEAD_DIM), BF16),
            pltpu.VMEM((batch, srows, HEAD_DIM), BF16),
            pltpu.VMEM((n_src, srows, HEAD_DIM), BF16),
            pltpu.VMEM((batch, 2, lanes), F32),
            pltpu.VMEM((n_src, 2, lanes), F32),
            pltpu.VMEM((rows1, HEAD_DIM), F32),
            pltpu.VMEM((rows1, HEAD_DIM), F32),
            pltpu.VMEM((src_rows, lanes), F32),
            pltpu.VMEM((src_rows, lanes), F32),
            pltpu.VMEM((HEAD_DIM, lanes), F32),
            pltpu.VMEM((lanes, HEAD_DIM), F32),
            pltpu.VMEM((batch, srows, HEAD_DIM), BF16),
            pltpu.VMEM((batch * srows, HEAD_DIM), F32),
            pltpu.VMEM((all_rows, q_cols), BF16),
            pltpu.VMEM((n_head, part_rows, part_cols), BF16),
            pltpu.VMEM((n_head, part_rows, part_cols), BF16),
            pltpu.VMEM((n_head, part_rows, part_cols), BF16),
            pltpu.VMEM((out_cols // HEAD_DIM * all_rows, HEAD_DIM), F32),
            dma((q_cols // min(512, q_cols) + 2,)),
            dma,
            dma((batch,)),
            dma((batch,)),
            dma((batch,)),
            dma((n_seq,)),
            dma((n_seq,)),
            dma((batch,)),
            dma((batch,)),
            dma((n_seq,)),
            dma((batch,)),
            dma((n_seq,)),
            dma((n_seq,)),
            dma((batch,)),
            dma((batch,)),
            dma((n_head,)),
            dma((n_head,)),
            dma((n_head,)),
            dma((n_head,)),
        ],
        compiler_params=pltpu.CompilerParams(
            collective_id=0, has_side_effects=True, vmem_limit_bytes=56 * 1024 * 1024
        ),
        name="verify_round",
    )(
        hidden_states.transpose(1, 0, 2).reshape(verify * batch, width),
        inverse,
        context_lengths,
        keep_blocks,
        w_query,
        w_key,
        w_value,
        w_out,
        key_cache,
        value_cache,
    )
    return target.reshape(verify, batch, out_cols).transpose(1, 0, 2), drafted


def solution(mesh):
    placed = (
        P(None, None, "seq"),
        P("seq", "head"),
        P("seq", "head"),
        P("seq", "head"),
        P("head", "seq"),
        P(None, "seq", "head"),
        P(None, "seq", "head"),
        P(),
        P(None, "seq"),
    )
    return jax.shard_map(
        functools.partial(per_device, mesh.shape["seq"], mesh.shape["head"]),
        mesh=mesh,
        in_specs=placed,
        out_specs=(P(None, None, "seq"), P(None, None, "seq")),
        check_vma=False,
    )
```

```python
import functools
import math

import jax
import jax.numpy as jnp
import numpy as np
from jax import lax
from jax.experimental import pallas as pl
from jax.experimental.pallas import tpu as pltpu
from jax.sharding import PartitionSpec as P

HEAD_DIM = 128
BLOCK = 128
NEG = -1e30
MESH = pl.DeviceIdType.MESH
F32 = jnp.float32
BF16 = jnp.bfloat16


def round_up(value, unit):
    return -(-value // unit) * unit


def kernel(
    dims,
    hid_in,
    inv_in,
    ctx_in,
    keep_in,
    wq,
    wk,
    wv,
    wo,
    kc,
    vc,
    out_v,
    out_d,
    hid,
    inv,
    ctx,
    keep,
    small_sem,
    w_buf,
    wo_buf,
    k_buf,
    v_buf,
    pack,
    send1,
    recv1,
    qkv,
    query_all,
    send3,
    recv3,
    sendml,
    recvml,
    cos_buf,
    sin_buf,
    mscr,
    lscr,
    coefs,
    coef_t,
    att,
    spare,
    dense,
    att32,
    x_buf,
    send4,
    recv4,
    fin,
    y32,
    w_sem,
    wo_sem,
    k_sem,
    v_sem,
    s1_sem,
    r1_sem,
    s2_sem,
    r2_sem,
    s3_sem,
    r3_sem,
    sm_sem,
    rm_sem,
    s5_sem,
    r5_sem,
    f5_sem,
    s4_sem,
    r4_sem,
    s6_sem,
    r6_sem,
):
    n_seq, n_head, batch, verify, kv_local, heads, ctx_local, col_parts = dims
    draft = verify - 1
    group = heads // kv_local
    per = n_seq // batch
    slots = heads + 2 * kv_local
    qrows = verify * heads
    grows = verify * group
    srows = 2 * qrows
    q_cols = heads * HEAD_DIM
    kv_cols = kv_local * HEAD_DIM
    me = lax.axis_index("seq")
    hd = lax.axis_index("head")
    my_b = me // per
    scale = HEAD_DIM ** (-0.5) * math.log2(math.e)
    rows1 = send1.shape[1]
    crows = att.shape[1]
    lines = n_seq // 2
    line, side = me // 2, lax.rem(me, 2)
    partner = me + 1 - 2 * side

    def use_order(i):
        if per > 1:
            return lax.rem(my_b + i, batch)
        return 2 * lax.rem(line + i // 2, lines) + lax.rem(side + i, 2)

    def gather_order(i):
        if per > 1:
            return lax.rem(my_b + i, batch)
        return 2 * lax.rem(line + i, lines) + jnp.where(i < lines, side, 1 - side)

    def is_mine(b):
        return lax.rem(b * per, 2) == side

    def is_own(b):
        return b * per == me

    def on_owner(body):
        if per == 1:
            body()
        else:
            pl.when(lax.rem(me, per) == 0)(body)

    barrier = pltpu.get_barrier_semaphore()
    for off in range(1, n_seq):
        pl.semaphore_signal(
            barrier, inc=1, device_id=(lax.rem(me + off, n_seq), hd), device_id_type=MESH
        )
    for off in range(1, n_head):
        pl.semaphore_signal(
            barrier, inc=1, device_id=(me, lax.rem(hd + off, n_head)), device_id_type=MESH
        )

    small = [
        pltpu.make_async_copy(src, dst, small_sem.at[at])
        for at, (src, dst) in enumerate(
            ((ctx_in, ctx), (inv_in, inv), (hid_in, hid), (keep_in, keep))
        )
    ]
    for copy in small:
        copy.start()

    step = min(512, q_cols)
    pieces = [(wq, c, step, c) for c in range(0, q_cols, step)]
    pieces += [(wk, 0, kv_cols, q_cols), (wv, 0, kv_cols, q_cols + kv_cols)]
    w_copies = []
    for at, (src, c0, width, d0) in enumerate(pieces):
        copy = pltpu.make_async_copy(
            src.at[:, pl.ds(c0, width)], w_buf.at[:, pl.ds(d0, width)], w_sem.at[at]
        )
        copy.start()
        w_copies.append(copy)

    def cache_copies(b):
        return (
            pltpu.make_async_copy(kc.at[b], k_buf.at[b], k_sem.at[b]),
            pltpu.make_async_copy(vc.at[b], v_buf.at[b], v_sem.at[b]),
        )

    def rotation():
        shape = (8, HEAD_DIM)
        lane = lax.broadcasted_iota(jnp.int32, shape, 1)
        pos = (ctx[my_b] + lax.broadcasted_iota(jnp.int32, shape, 0)).astype(F32)
        angle = pos * inv[...]
        cosine = jnp.cos(angle)
        sine = jnp.sin(angle)
        sine = jnp.where(lane < HEAD_DIM // 2, -sine, sine)
        cos_buf[...] = jnp.ones_like(cos_buf)
        sin_buf[...] = jnp.zeros_like(sin_buf)
        for slot in range(heads + kv_local):
            r0 = slot * verify
            cos_buf[r0 : r0 + 8, :] = cosine
            sin_buf[r0 : r0 + 8, :] = sine
        r0 = (heads + kv_local) * verify
        cos_buf[r0 : r0 + 8, :] = jnp.ones(shape, F32)
        sin_buf[r0 : r0 + 8, :] = jnp.zeros(shape, F32)

    for copy in small:
        copy.wait()
    on_owner(rotation)

    pack[...] = jnp.zeros_like(pack)
    coefs[...] = jnp.zeros_like(coefs)
    x_in = hid[...]
    def copy1(part, b, src):
        rows = pl.ds(*parts[part])
        return pltpu.make_async_remote_copy(
            src_ref=send1.at[b, rows],
            dst_ref=recv1.at[src, rows],
            send_sem=s1_sem.at[part, b],
            recv_sem=r1_sem.at[part, src],
            device_id=(b * per, hd),
            device_id_type=MESH,
        )

    def send_part(part):
        r0, count = parts[part]

        @pl.loop(0, batch)
        def _(i):
            b = lax.rem(my_b + 1 + i, batch)
            rows = pl.ds(pl.multiple_of(b * rows1 + r0, 16), count)
            send1[b, r0 : r0 + count, :] = pack[rows, :].astype(BF16)

            @pl.when(b * per != me)
            def _():
                copy1(part, b, me).start()

    early = rows1 // 2 // 16 * 16
    parts = ((0, early), (early, rows1 - early))
    sent_early = False
    for at, (copy, (src, c0, width, d0)) in enumerate(zip(w_copies, pieces)):
        copy.wait()
        piece = jnp.dot(x_in, w_buf[:, d0 : d0 + width], preferred_element_type=F32)
        for s in range(width // HEAD_DIM):
            slot = d0 // HEAD_DIM + s
            for j in range(verify):
                pack[pl.ds(slot * verify + j, batch, stride=rows1), :] = piece[
                    j * batch : (j + 1) * batch, s * HEAD_DIM : (s + 1) * HEAD_DIM
                ]
        if not sent_early and (d0 + width) // HEAD_DIM * verify >= early:
            sent_early = True
            pl.semaphore_wait(barrier, n_seq - 1 + n_head - 1)
            send_part(0)
    send_part(1)

    @pl.loop(0, batch)
    def _(i):
        for copy in cache_copies(use_order(i)):
            copy.start()

    wo_copy = pltpu.make_async_copy(wo, wo_buf, wo_sem)
    wo_copy.start()

    def copy_gather(buf, send_sem, recv_sem, b, dst):
        return pltpu.make_async_remote_copy(
            src_ref=buf.at[b],
            dst_ref=buf.at[b],
            send_sem=send_sem.at[dst],
            recv_sem=recv_sem.at[b],
            device_id=(dst, hd),
            device_id_type=MESH,
        )

    def owner_rotate():
        def add(off, acc):
            src = lax.rem(me + off, n_seq)
            for part in range(2):
                copy1(part, my_b, src).wait_recv()
            return acc + recv1[src].astype(F32)

        total = lax.fori_loop(1, n_seq, add, send1[my_b].astype(F32))
        turned = total * cos_buf[...] + pltpu.roll(total, HEAD_DIM // 2, 1) * sin_buf[...]
        qkv[...] = turned.astype(BF16)
        query_all[my_b] = turned[0 : query_all.shape[1]].astype(BF16)

        @pl.loop(1, n_seq)
        def _(off):
            if per > 1:
                dst = lax.rem(me + off, n_seq)
            else:
                dst = 2 * lax.rem(line + n_seq - off // 2, lines) + lax.rem(side + off, 2)
            copy_gather(query_all, s2_sem, r2_sem, my_b, dst).start()

    on_owner(owner_rotate)

    def statistics(peak, total):
        lane = lax.broadcasted_iota(jnp.int32, (srows, HEAD_DIM), 1)
        wide = jnp.where(lane == 0, peak, jnp.where(lane == 1, total, 0.0))
        extra = sendml.shape[2] - srows
        if extra:
            wide = jnp.concatenate([wide, jnp.zeros((extra, HEAD_DIM), F32)], axis=0)
        return wide.T[0:2, :]

    def softmax(scores, mask):
        masked = jnp.where(mask, scores, NEG)
        peak = jnp.maximum(jnp.max(masked, axis=1, keepdims=True), NEG / 8)
        weights = jnp.exp2(masked - peak)
        return peak, jnp.sum(weights, axis=1, keepdims=True), weights

    def copies_up(b, src):
        return [
            pltpu.make_async_remote_copy(
                src_ref=source.at[b],
                dst_ref=target.at[src],
                send_sem=send_sem.at[b],
                recv_sem=recv_sem.at[src],
                device_id=(b * per, hd),
                device_id_type=MESH,
            )
            for source, target, send_sem, recv_sem in (
                (sendml, recvml, sm_sem, rm_sem),
                (send3, recv3, s3_sem, r3_sem),
            )
        ]

    def attend(b):
        query = query_all[b].astype(F32)[0:qrows]
        row = lax.broadcasted_iota(jnp.int32, query.shape, 0)
        spread = jnp.concatenate(
            [
                jnp.where((row >= kv * grows) & (row < (kv + 1) * grows), query, 0.0)
                for kv in range(kv_local)
            ],
            axis=1,
        ).astype(BF16)
        scores = (
            lax.dot_general(
                spread, k_buf[b], (((1,), (1,)), ((), ())), preferred_element_type=F32
            )
            * scale
        )
        lane = lax.broadcasted_iota(jnp.int32, (1, ctx_local), 1)
        live = lane + me * ctx_local < ctx[b]
        flags = jnp.concatenate(
            [
                jnp.full((1, BLOCK), keep[b, blk], jnp.int32)
                for blk in range(ctx_local // BLOCK)
            ],
            axis=1,
        )
        kept = live & (flags > 0)
        t_peak, t_total, t_weights = softmax(scores, live)
        d_peak, d_total, d_weights = softmax(scores, kept)
        weights = jnp.concatenate([t_weights, d_weights], axis=0).astype(BF16)
        values = jnp.dot(weights, v_buf[b], preferred_element_type=F32)
        blocks = []
        for half in range(2):
            for kv in range(kv_local):
                r0 = half * qrows + kv * grows
                blocks.append(values[r0 : r0 + grows, kv * HEAD_DIM : (kv + 1) * HEAD_DIM])
        send3[b] = jnp.concatenate(blocks, axis=0).astype(BF16)
        sendml[b] = statistics(
            jnp.concatenate([t_peak, d_peak], axis=0),
            jnp.concatenate([t_total, d_total], axis=0),
        )

    together = 2

    @pl.loop(0, batch // together)
    def _(i):
        several = [use_order(i * together + at) for at in range(together)]
        for b in several:

            @pl.when(jnp.logical_not(is_own(b)))
            def _(b=b):
                copy_gather(query_all, s2_sem, r2_sem, b, me).wait_recv()

            for copy in cache_copies(b):
                copy.wait()
        for b in several:
            attend(b)
        for b in several:

            @pl.when(jnp.logical_not(is_own(b)))
            def _(b=b):
                for copy in copies_up(b, me):
                    copy.start()

    def owner_merge():
        rows_all = qkv[...].astype(F32)
        query = rows_all[0:qrows]
        raw = lax.dot_general(
            query.astype(BF16), qkv[...], (((1,), (1,)), ((), ())), preferred_element_type=F32
        )
        scores = raw * scale
        row = lax.broadcasted_iota(jnp.int32, scores.shape, 0)
        col = lax.broadcasted_iota(jnp.int32, scores.shape, 1) - qrows
        row_head = lax.div(row, verify)
        row_j = row - row_head * verify
        row_kv = lax.div(row_head, group)
        first = row_kv * verify
        mask = (col >= first) & (col <= first + row_j)
        peak, total, weights = softmax(scores, mask)
        weights = weights.astype(BF16)
        vrow = lax.broadcasted_iota(jnp.int32, rows_all.shape, 0) - qrows
        shift = kv_local * verify
        moved = pltpu.roll(rows_all, rows_all.shape[0] - shift, 0)
        moved = jnp.where((vrow >= 0) & (vrow < shift), moved, 0.0).astype(BF16)
        values = jnp.dot(weights, moved, preferred_element_type=F32)
        recv3[n_seq] = jnp.concatenate([values, values], axis=0).astype(BF16)
        recvml[n_seq] = statistics(
            jnp.concatenate([peak, peak], axis=0), jnp.concatenate([total, total], axis=0)
        )
        recv3[me] = send3[my_b]
        recvml[me] = sendml[my_b]

        @pl.loop(1, n_seq)
        def _(off):
            for copy in copies_up(my_b, lax.rem(me + off, n_seq)):
                copy.wait_recv()

        n_src = n_seq + 1
        for s in range(n_src):
            both = recvml[s]
            mscr[s : s + 1, :] = both[0:1]
            lscr[s : s + 1, :] = both[1:2]
        m_all = mscr[0:n_src, :]
        l_all = lscr[0:n_src, :]
        factor = jnp.exp2(m_all - jnp.max(m_all, axis=0, keepdims=True))
        norm = jnp.sum(factor * l_all, axis=0, keepdims=True)
        norm = jnp.where(norm > 0.0, norm, 1.0)
        coefs[0:n_src, :] = factor / norm
        coef_t[...] = coefs[...].T
        acc = jnp.zeros((srows, HEAD_DIM), F32)
        for s in range(n_src):
            acc = acc + coef_t[0:srows, s : s + 1] * recv3[s].astype(F32)
        spare[0:srows, :] = acc
        spare[srows : srows + 8, :] = jnp.zeros((8, HEAD_DIM), F32)
        dense[...] = jnp.zeros_like(dense)
        dense[0:qrows, :] = acc[0:qrows]
        for h in range(heads):
            r0, r1 = qrows + h * draft, qrows + h * verify
            dense[r0 : r0 + 8, :] = spare[r1 : r1 + 8, :]
        att[my_b] = dense[0:crows, :].astype(BF16)

        copy_gather(att, s5_sem, r5_sem, my_b, partner).start()

        @pl.loop(1, lines)
        def _(off):
            dst = 2 * lax.rem(line + off, lines) + side
            copy_gather(att, s5_sem, r5_sem, my_b, dst).start()

    on_owner(owner_merge)

    def copy_forward(b):
        return pltpu.make_async_remote_copy(
            src_ref=att.at[b],
            dst_ref=att.at[b],
            send_sem=f5_sem.at[b],
            recv_sem=r5_sem.at[b],
            device_id=(partner, hd),
            device_id_type=MESH,
        )

    @pl.loop(0, batch)
    def _(i):
        b = gather_order(i)

        @pl.when(jnp.logical_not(is_own(b)))
        def _():
            copy_forward(b).wait_recv()

        @pl.when(is_mine(b) & jnp.logical_not(is_own(b)))
        def _():
            copy_forward(b).start()

        att32[pl.ds(pl.multiple_of(b * crows, 16), crows), :] = att[b].astype(F32)

    planes = [(j, verify) for j in range(verify)]
    planes += [(qrows + j, draft) for j in range(draft)]
    for pair in range(x_buf.shape[0] // 16):
        for h in range(heads):
            halves = []
            for at in (2 * pair, 2 * pair + 1):
                if at < len(planes):
                    start, jump = planes[at]
                    halves.append(att32[pl.ds(start + h * jump, batch, stride=crows), :])
                else:
                    halves.append(jnp.zeros((batch, HEAD_DIM), F32))
            x_buf[16 * pair : 16 * pair + 16, h * HEAD_DIM : (h + 1) * HEAD_DIM] = (
                jnp.concatenate(halves, axis=0).astype(BF16)
            )

    part_rows, part_cols = send4.shape[1:]
    all_rows = x_buf.shape[0]

    def place(at):
        return (at // col_parts) * part_rows, (at % col_parts) * part_cols

    def copy4(at, src):
        return pltpu.make_async_remote_copy(
            src_ref=send4.at[at],
            dst_ref=recv4.at[src],
            send_sem=s4_sem.at[at],
            recv_sem=r4_sem.at[src],
            device_id=(me, at),
            device_id_type=MESH,
        )

    wo_copy.wait()
    for at in range(n_head):
        r0, c0 = place(at)
        send4[at] = jnp.dot(
            x_buf[r0 : r0 + part_rows, :],
            wo_buf[:, c0 : c0 + part_cols],
            preferred_element_type=F32,
        ).astype(BF16)

        @pl.when(hd != at)
        def _():
            copy4(at, hd).start()

    def add_head(off, acc):
        src = lax.rem(hd + off, n_head)
        copy4(hd, src).wait_recv()
        return acc + recv4[src].astype(F32)

    fin[hd] = lax.fori_loop(1, n_head, add_head, send4[hd].astype(F32)).astype(BF16)

    def copy6(at, dst):
        return pltpu.make_async_remote_copy(
            src_ref=fin.at[at],
            dst_ref=fin.at[at],
            send_sem=s6_sem.at[dst],
            recv_sem=r6_sem.at[at],
            device_id=(me, dst),
            device_id_type=MESH,
        )

    @pl.loop(1, n_head)
    def _(off):
        copy6(hd, lax.rem(hd + off, n_head)).start()

    @pl.loop(1, n_head)
    def _(off):
        copy6(lax.rem(hd + off, n_head), hd).wait_recv()

    for at in range(n_head):
        r0, c0 = place(at)
        for c in range(part_cols // HEAD_DIM):
            base = (c0 // HEAD_DIM + c) * all_rows + r0
            y32[base : base + part_rows, :] = fin[
                at, :, c * HEAD_DIM : (c + 1) * HEAD_DIM
            ].astype(F32)
    target_rows = verify * batch
    chunks = range(out_v.shape[1] // HEAD_DIM)
    for c in chunks:
        out_v[:, c * HEAD_DIM : (c + 1) * HEAD_DIM] = y32[
            c * all_rows : c * all_rows + target_rows, :
        ].astype(BF16)
    for b in range(batch):
        out_d[b] = jnp.concatenate(
            [
                y32[pl.ds(c * all_rows + target_rows + b, draft, stride=batch), :]
                for c in chunks
            ],
            axis=1,
        ).astype(BF16)

    @pl.loop(0, batch)
    def _(b):
        @pl.when(b * per != me)
        def _():
            for part in range(2):
                copy1(part, b, me).wait_send()
            for copy in copies_up(b, me):
                copy.wait_send()

        @pl.when(is_mine(b) & jnp.logical_not(is_own(b)))
        def _():
            copy_forward(b).wait_send()

    def owner_sent():
        @pl.loop(1, n_seq)
        def _(off):
            dst = lax.rem(me + off, n_seq)
            copy_gather(query_all, s2_sem, r2_sem, my_b, dst).wait_send()

            @pl.when((dst == partner) | (lax.rem(dst, 2) == side))
            def _():
                copy_gather(att, s5_sem, r5_sem, my_b, dst).wait_send()

    on_owner(owner_sent)

    @pl.loop(1, n_head)
    def _(off):
        dst = lax.rem(hd + off, n_head)
        copy4(dst, hd).wait_send()
        copy6(hd, dst).wait_send()


def per_device(
    n_seq,
    n_head,
    hidden_states,
    w_query,
    w_key,
    w_value,
    w_out,
    key_cache,
    value_cache,
    context_lengths,
    keep_blocks,
):
    batch, verify, width = hidden_states.shape
    draft = verify - 1
    ctx_local = key_cache.shape[1]
    kv_cols = key_cache.shape[2]
    kv_local = kv_cols // HEAD_DIM
    q_cols = w_query.shape[1]
    heads = q_cols // HEAD_DIM
    out_cols = w_out.shape[1]
    slots = heads + 2 * kv_local
    rows1 = round_up(verify * slots, 16)
    srows = 2 * verify * heads
    crows = round_up((verify + draft) * heads, 16)
    lanes = round_up(srows, HEAD_DIM)
    n_rows = batch * (verify + draft)
    col_parts = math.gcd(n_head, out_cols // HEAD_DIM)
    row_parts = n_head // col_parts
    part_rows = round_up(-(-n_rows // row_parts), 16)
    part_cols = out_cols // col_parts
    all_rows = part_rows * row_parts
    n_src = n_seq + 1
    src_rows = round_up(n_src, 8)
    qpad = round_up(verify * heads, 16)
    dims = (n_seq, n_head, batch, verify, kv_local, heads, ctx_local, col_parts)

    inverse = (500000.0 ** (-(np.arange(HEAD_DIM // 2) * 2.0) / HEAD_DIM)).astype(np.float32)
    inverse = jnp.asarray(np.concatenate([inverse, inverse])[None, :])

    vmem = pl.BlockSpec(memory_space=pltpu.VMEM)
    hbm = pl.BlockSpec(memory_space=pl.ANY)
    dma = pltpu.SemaphoreType.DMA
    target, drafted = pl.pallas_call(
        functools.partial(kernel, dims),
        out_shape=(
            pltpu.VMEM((batch * verify, out_cols), BF16),
            pltpu.VMEM((batch, draft, out_cols), BF16),
        ),
        in_specs=[hbm] * 10,
        out_specs=(vmem, vmem),
        scratch_shapes=[
            pltpu.VMEM((verify * batch, width), BF16),
            pltpu.VMEM(inverse.shape, F32),
            pltpu.SMEM(context_lengths.shape, jnp.int32),
            pltpu.SMEM(keep_blocks.shape, jnp.int32),
            dma((4,)),
            pltpu.VMEM((width, q_cols + 2 * kv_cols), BF16),
            pltpu.VMEM(w_out.shape, BF16),
            pltpu.VMEM(key_cache.shape, BF16),
            pltpu.VMEM(value_cache.shape, BF16),
            pltpu.VMEM((batch * rows1, HEAD_DIM), F32),
            pltpu.VMEM((batch, rows1, HEAD_DIM), BF16),
            pltpu.VMEM((n_seq, rows1, HEAD_DIM), BF16),
            pltpu.VMEM((rows1, HEAD_DIM), BF16),
            pltpu.VMEM((batch, qpad, HEAD_DIM), BF16),
            pltpu.VMEM((batch, srows, HEAD_DIM), BF16),
            pltpu.VMEM((n_src, srows, HEAD_DIM), BF16),
            pltpu.VMEM((batch, 2, lanes), F32),
            pltpu.VMEM((n_src, 2, lanes), F32),
            pltpu.VMEM((rows1, HEAD_DIM), F32),
            pltpu.VMEM((rows1, HEAD_DIM), F32),
            pltpu.VMEM((src_rows, lanes), F32),
            pltpu.VMEM((src_rows, lanes), F32),
            pltpu.VMEM((HEAD_DIM, lanes), F32),
            pltpu.VMEM((lanes, HEAD_DIM), F32),
            pltpu.VMEM((batch, crows, HEAD_DIM), BF16),
            pltpu.VMEM((srows + 8, HEAD_DIM), F32),
            pltpu.VMEM((crows + 8, HEAD_DIM), F32),
            pltpu.VMEM((batch * crows, HEAD_DIM), F32),
            pltpu.VMEM((all_rows, q_cols), BF16),
            pltpu.VMEM((n_head, part_rows, part_cols), BF16),
            pltpu.VMEM((n_head, part_rows, part_cols), BF16),
            pltpu.VMEM((n_head, part_rows, part_cols), BF16),
            pltpu.VMEM((out_cols // HEAD_DIM * all_rows, HEAD_DIM), F32),
            dma((q_cols // min(512, q_cols) + 2,)),
            dma,
            dma((batch,)),
            dma((batch,)),
            dma((2, batch)),
            dma((2, n_seq)),
            dma((n_seq,)),
            dma((batch,)),
            dma((batch,)),
            dma((n_seq,)),
            dma((batch,)),
            dma((n_seq,)),
            dma((n_seq,)),
            dma((batch,)),
            dma((batch,)),
            dma((n_head,)),
            dma((n_head,)),
            dma((n_head,)),
            dma((n_head,)),
        ],
        compiler_params=pltpu.CompilerParams(
            collective_id=0, has_side_effects=True, vmem_limit_bytes=56 * 1024 * 1024
        ),
        name="verify_round",
    )(
        hidden_states.transpose(1, 0, 2).reshape(verify * batch, width),
        inverse,
        context_lengths,
        keep_blocks,
        w_query,
        w_key,
        w_value,
        w_out,
        key_cache,
        value_cache,
    )
    return target.reshape(verify, batch, out_cols).transpose(1, 0, 2), drafted


def solution(mesh):
    placed = (
        P(None, None, "seq"),
        P("seq", "head"),
        P("seq", "head"),
        P("seq", "head"),
        P("head", "seq"),
        P(None, "seq", "head"),
        P(None, "seq", "head"),
        P(),
        P(None, "seq"),
    )
    return jax.shard_map(
        functools.partial(per_device, mesh.shape["seq"], mesh.shape["head"]),
        mesh=mesh,
        in_specs=placed,
        out_specs=(P(None, None, "seq"), P(None, None, "seq")),
        check_vma=False,
    )
```

```python
import functools
import math

import jax
import jax.numpy as jnp
import numpy as np
from jax import lax
from jax.experimental import pallas as pl
from jax.experimental.pallas import tpu as pltpu
from jax.sharding import PartitionSpec as P

HEAD_DIM = 128
BLOCK = 128
NEG = -1e30
MESH = pl.DeviceIdType.MESH
F32 = jnp.float32
BF16 = jnp.bfloat16


def round_up(value, unit):
    return -(-value // unit) * unit


def kernel(
    dims,
    hid_in,
    inv_in,
    ctx_in,
    keep_in,
    wq,
    wk,
    wv,
    wo,
    kc,
    vc,
    out_v,
    out_d,
    hid,
    inv,
    ctx,
    keep,
    small_sem,
    w_buf,
    wo_buf,
    k_buf,
    v_buf,
    pack,
    send1,
    recv1,
    pair1,
    qkv,
    query_all,
    send3,
    recv3,
    sendml,
    recvml,
    cos_buf,
    sin_buf,
    mscr,
    lscr,
    coefs,
    coef_t,
    att,
    spare,
    dense,
    att32,
    x_buf,
    send4,
    recv4,
    fin,
    y32,
    w_sem,
    wo_sem,
    k_sem,
    v_sem,
    s1_sem,
    r1_sem,
    p1_sem,
    s2_sem,
    r2_sem,
    s3_sem,
    r3_sem,
    sm_sem,
    rm_sem,
    s5_sem,
    r5_sem,
    f5_sem,
    s4_sem,
    r4_sem,
    s6_sem,
    r6_sem,
):
    n_seq, n_head, batch, verify, kv_local, heads, ctx_local, col_parts = dims
    draft = verify - 1
    group = heads // kv_local
    per = n_seq // batch
    slots = heads + 2 * kv_local
    qrows = verify * heads
    grows = verify * group
    srows = 2 * qrows
    q_cols = heads * HEAD_DIM
    kv_cols = kv_local * HEAD_DIM
    me = lax.axis_index("seq")
    hd = lax.axis_index("head")
    my_b = me // per
    scale = HEAD_DIM ** (-0.5) * math.log2(math.e)
    rows1 = send1.shape[1]
    crows = att.shape[1]
    lines = n_seq // 2
    line, side = me // 2, lax.rem(me, 2)
    partner = me + 1 - 2 * side

    def use_order(i):
        if per > 1:
            return lax.rem(my_b + i, batch)
        return 2 * lax.rem(line + i // 2, lines) + lax.rem(side + i, 2)

    def gather_order(i):
        if per > 1:
            return lax.rem(my_b + i, batch)
        return 2 * lax.rem(line + i, lines) + jnp.where(i < lines, side, 1 - side)

    def side_loop(mine, body):
        if per > 1:

            @pl.loop(0, batch)
            def _(i):
                b = lax.rem(my_b + i, batch)
                pl.when(is_mine(b) if mine else jnp.logical_not(is_mine(b)))(
                    functools.partial(body, b)
                )
        else:

            @pl.loop(0, lines)
            def _(i):
                body(2 * lax.rem(line + 1 + i, lines) + (side if mine else 1 - side))

    def is_mine(b):
        return lax.rem(b * per, 2) == side

    def is_own(b):
        return b * per == me

    def on_owner(body):
        if per == 1:
            body()
        else:
            pl.when(lax.rem(me, per) == 0)(body)

    barrier = pltpu.get_barrier_semaphore()
    for off in range(1, n_seq):
        pl.semaphore_signal(
            barrier, inc=1, device_id=(lax.rem(me + off, n_seq), hd), device_id_type=MESH
        )
    for off in range(1, n_head):
        pl.semaphore_signal(
            barrier, inc=1, device_id=(me, lax.rem(hd + off, n_head)), device_id_type=MESH
        )

    small = [
        pltpu.make_async_copy(src, dst, small_sem.at[at])
        for at, (src, dst) in enumerate(
            ((ctx_in, ctx), (inv_in, inv), (hid_in, hid), (keep_in, keep))
        )
    ]
    for copy in small:
        copy.start()

    step = min(512, q_cols)
    pieces = [(wq, c, step, c) for c in range(0, q_cols, step)]
    pieces += [(wk, 0, kv_cols, q_cols), (wv, 0, kv_cols, q_cols + kv_cols)]
    w_copies = []
    for at, (src, c0, width, d0) in enumerate(pieces):
        copy = pltpu.make_async_copy(
            src.at[:, pl.ds(c0, width)], w_buf.at[:, pl.ds(d0, width)], w_sem.at[at]
        )
        copy.start()
        w_copies.append(copy)

    def cache_copies(b):
        return (
            pltpu.make_async_copy(kc.at[b], k_buf.at[b], k_sem.at[b]),
            pltpu.make_async_copy(vc.at[b], v_buf.at[b], v_sem.at[b]),
        )

    def rotation():
        shape = (8, HEAD_DIM)
        lane = lax.broadcasted_iota(jnp.int32, shape, 1)
        pos = (ctx[my_b] + lax.broadcasted_iota(jnp.int32, shape, 0)).astype(F32)
        angle = pos * inv[...]
        cosine = jnp.cos(angle)
        sine = jnp.sin(angle)
        sine = jnp.where(lane < HEAD_DIM // 2, -sine, sine)
        cos_buf[...] = jnp.ones_like(cos_buf)
        sin_buf[...] = jnp.zeros_like(sin_buf)
        for slot in range(heads + kv_local):
            r0 = slot * verify
            cos_buf[r0 : r0 + 8, :] = cosine
            sin_buf[r0 : r0 + 8, :] = sine
        r0 = (heads + kv_local) * verify
        cos_buf[r0 : r0 + 8, :] = jnp.ones(shape, F32)
        sin_buf[r0 : r0 + 8, :] = jnp.zeros(shape, F32)

    for copy in small:
        copy.wait()
    on_owner(rotation)

    pack[...] = jnp.zeros_like(pack)
    coefs[...] = jnp.zeros_like(coefs)
    spare[...] = jnp.zeros_like(spare)
    dense[...] = jnp.zeros_like(dense)
    x_in = hid[...]
    def copy_pair(part, b):
        rows = pl.ds(*parts[part])
        return pltpu.make_async_remote_copy(
            src_ref=send1.at[b, rows],
            dst_ref=pair1.at[b, rows],
            send_sem=s1_sem.at[part, b],
            recv_sem=p1_sem.at[part, b],
            device_id=(partner, hd),
            device_id_type=MESH,
        )

    def copy1(b, src_line):
        return pltpu.make_async_remote_copy(
            src_ref=send1.at[b],
            dst_ref=recv1.at[src_line],
            send_sem=s1_sem.at[0, b],
            recv_sem=r1_sem.at[src_line],
            device_id=(b * per, hd),
            device_id_type=MESH,
        )

    def pack_rows(b, r0, count):
        return pack[pl.ds(pl.multiple_of(b * rows1 + r0, 16), count), :]

    def send_part(part):
        r0, count = parts[part]

        def body(b):
            send1[b, r0 : r0 + count, :] = pack_rows(b, r0, count).astype(BF16)
            copy_pair(part, b).start()

        side_loop(False, body)

    def paired_sum(b):
        for part in range(2):
            copy_pair(part, b).wait_recv()
        return pack_rows(b, 0, rows1) + pair1[b].astype(F32)

    def send_line(b):
        @pl.when(jnp.logical_not(is_own(b)))
        def _():
            send1[b] = paired_sum(b).astype(BF16)
            copy1(b, line).start()

    early = rows1 // 2 // 16 * 16
    parts = ((0, early), (early, rows1 - early))
    sent_early = False
    for at, (copy, (src, c0, width, d0)) in enumerate(zip(w_copies, pieces)):
        copy.wait()
        piece = jnp.dot(x_in, w_buf[:, d0 : d0 + width], preferred_element_type=F32)
        for s in range(width // HEAD_DIM):
            slot = d0 // HEAD_DIM + s
            for j in range(verify):
                pack[pl.ds(slot * verify + j, batch, stride=rows1), :] = piece[
                    j * batch : (j + 1) * batch, s * HEAD_DIM : (s + 1) * HEAD_DIM
                ]
        if not sent_early and (d0 + width) // HEAD_DIM * verify >= early:
            sent_early = True
            pl.semaphore_wait(barrier, n_seq - 1 + n_head - 1)
            send_part(0)
    send_part(1)
    side_loop(True, send_line)

    @pl.loop(0, batch)
    def _(i):
        for copy in cache_copies(use_order(i)):
            copy.start()

    wo_copy = pltpu.make_async_copy(wo, wo_buf, wo_sem)
    wo_copy.start()

    def copy_gather(buf, send_sem, recv_sem, b, dst):
        return pltpu.make_async_remote_copy(
            src_ref=buf.at[b],
            dst_ref=buf.at[b],
            send_sem=send_sem.at[dst],
            recv_sem=recv_sem.at[b],
            device_id=(dst, hd),
            device_id_type=MESH,
        )

    def owner_rotate():
        def add(off, acc):
            src = lax.rem(line + off, lines)
            copy1(my_b, src).wait_recv()
            return acc + recv1[src].astype(F32)

        total = lax.fori_loop(1, lines, add, paired_sum(my_b))
        turned = total * cos_buf[...] + pltpu.roll(total, HEAD_DIM // 2, 1) * sin_buf[...]
        qkv[...] = turned.astype(BF16)
        query_all[my_b] = turned[0 : query_all.shape[1]].astype(BF16)

        @pl.loop(1, n_seq)
        def _(off):
            if per > 1:
                dst = lax.rem(me + off, n_seq)
            else:
                dst = 2 * lax.rem(line + n_seq - off // 2, lines) + lax.rem(side + off, 2)
            copy_gather(query_all, s2_sem, r2_sem, my_b, dst).start()

    on_owner(owner_rotate)

    def compact(value, at):
        loose = spare.at[at]
        loose[0:srows, :] = value
        tight = dense.at[at]
        for h in range(heads):
            r0, r1 = qrows + h * draft, qrows + h * verify
            tight[r0 : r0 + 8, :] = loose[r1 : r1 + 8, :]
        return jnp.concatenate([value[0:qrows], tight[qrows:crows, :]], axis=0)

    def statistics(peak, total):
        lane = lax.broadcasted_iota(jnp.int32, (srows, HEAD_DIM), 1)
        wide = jnp.where(lane == 0, peak, jnp.where(lane == 1, total, 0.0))
        extra = sendml.shape[2] - srows
        if extra:
            wide = jnp.concatenate([wide, jnp.zeros((extra, HEAD_DIM), F32)], axis=0)
        return wide.T[0:2, :]

    def softmax(scores, mask):
        masked = jnp.where(mask, scores, NEG)
        peak = jnp.maximum(jnp.max(masked, axis=1, keepdims=True), NEG / 8)
        weights = jnp.exp2(masked - peak)
        return peak, jnp.sum(weights, axis=1, keepdims=True), weights

    def copies_up(b, src):
        return [
            pltpu.make_async_remote_copy(
                src_ref=source.at[b],
                dst_ref=target.at[src],
                send_sem=send_sem.at[b],
                recv_sem=recv_sem.at[src],
                device_id=(b * per, hd),
                device_id_type=MESH,
            )
            for source, target, send_sem, recv_sem in (
                (sendml, recvml, sm_sem, rm_sem),
                (send3, recv3, s3_sem, r3_sem),
            )
        ]

    def attend(b, at):
        query = query_all[b].astype(F32)[0:qrows]
        row = lax.broadcasted_iota(jnp.int32, query.shape, 0)
        spread = jnp.concatenate(
            [
                jnp.where((row >= kv * grows) & (row < (kv + 1) * grows), query, 0.0)
                for kv in range(kv_local)
            ],
            axis=1,
        ).astype(BF16)
        scores = (
            lax.dot_general(
                spread, k_buf[b], (((1,), (1,)), ((), ())), preferred_element_type=F32
            )
            * scale
        )
        lane = lax.broadcasted_iota(jnp.int32, (1, ctx_local), 1)
        live = lane + me * ctx_local < ctx[b]
        flags = jnp.concatenate(
            [
                jnp.full((1, BLOCK), keep[b, blk], jnp.int32)
                for blk in range(ctx_local // BLOCK)
            ],
            axis=1,
        )
        kept = live & (flags > 0)
        t_peak, t_total, t_weights = softmax(scores, live)
        d_peak, d_total, d_weights = softmax(scores, kept)
        weights = jnp.concatenate([t_weights, d_weights], axis=0).astype(BF16)
        values = jnp.dot(weights, v_buf[b], preferred_element_type=F32)
        blocks = []
        for half in range(2):
            for kv in range(kv_local):
                r0 = half * qrows + kv * grows
                blocks.append(values[r0 : r0 + grows, kv * HEAD_DIM : (kv + 1) * HEAD_DIM])
        send3[b] = compact(jnp.concatenate(blocks, axis=0), at).astype(BF16)
        sendml[b] = statistics(
            jnp.concatenate([t_peak, d_peak], axis=0),
            jnp.concatenate([t_total, d_total], axis=0),
        )

    together = 2

    @pl.loop(0, batch // together)
    def _(i):
        several = [use_order(i * together + at) for at in range(together)]
        for b in several:

            @pl.when(jnp.logical_not(is_own(b)))
            def _(b=b):
                copy_gather(query_all, s2_sem, r2_sem, b, me).wait_recv()

            for copy in cache_copies(b):
                copy.wait()
        for at, b in enumerate(several):
            attend(b, at)
        for b in several:

            @pl.when(jnp.logical_not(is_own(b)))
            def _(b=b):
                for copy in copies_up(b, me):
                    copy.start()

    def owner_merge():
        rows_all = qkv[...].astype(F32)
        query = rows_all[0:qrows]
        raw = lax.dot_general(
            query.astype(BF16), qkv[...], (((1,), (1,)), ((), ())), preferred_element_type=F32
        )
        scores = raw * scale
        row = lax.broadcasted_iota(jnp.int32, scores.shape, 0)
        col = lax.broadcasted_iota(jnp.int32, scores.shape, 1) - qrows
        row_head = lax.div(row, verify)
        row_j = row - row_head * verify
        row_kv = lax.div(row_head, group)
        first = row_kv * verify
        mask = (col >= first) & (col <= first + row_j)
        peak, total, weights = softmax(scores, mask)
        weights = weights.astype(BF16)
        vrow = lax.broadcasted_iota(jnp.int32, rows_all.shape, 0) - qrows
        shift = kv_local * verify
        moved = pltpu.roll(rows_all, rows_all.shape[0] - shift, 0)
        moved = jnp.where((vrow >= 0) & (vrow < shift), moved, 0.0).astype(BF16)
        values = jnp.dot(weights, moved, preferred_element_type=F32)
        recv3[n_seq] = compact(jnp.concatenate([values, values], axis=0), 0).astype(BF16)
        recvml[n_seq] = statistics(
            jnp.concatenate([peak, peak], axis=0), jnp.concatenate([total, total], axis=0)
        )
        recv3[me] = send3[my_b]
        recvml[me] = sendml[my_b]

        @pl.loop(1, n_seq)
        def _(off):
            for copy in copies_up(my_b, lax.rem(me + off, n_seq)):
                copy.wait_recv()

        n_src = n_seq + 1
        for s in range(n_src):
            both = recvml[s]
            mscr[s : s + 1, :] = both[0:1]
            lscr[s : s + 1, :] = both[1:2]
        m_all = mscr[0:n_src, :]
        l_all = lscr[0:n_src, :]
        factor = jnp.exp2(m_all - jnp.max(m_all, axis=0, keepdims=True))
        norm = jnp.sum(factor * l_all, axis=0, keepdims=True)
        norm = jnp.where(norm > 0.0, norm, 1.0)
        coefs[0:n_src, :] = factor / norm
        coef_t[0:crows, :] = compact(coefs[...].T[0:srows], 0)
        acc = jnp.zeros((crows, HEAD_DIM), F32)
        for s in range(n_src):
            acc = acc + coef_t[0:crows, s : s + 1] * recv3[s].astype(F32)
        att[my_b] = acc.astype(BF16)
        copy_gather(att, s5_sem, r5_sem, my_b, partner).start()

        @pl.loop(1, lines)
        def _(off):
            dst = 2 * lax.rem(line + off, lines) + side
            copy_gather(att, s5_sem, r5_sem, my_b, dst).start()

    on_owner(owner_merge)

    def copy_forward(b):
        return pltpu.make_async_remote_copy(
            src_ref=att.at[b],
            dst_ref=att.at[b],
            send_sem=f5_sem.at[b],
            recv_sem=r5_sem.at[b],
            device_id=(partner, hd),
            device_id_type=MESH,
        )

    @pl.loop(0, batch)
    def _(i):
        b = gather_order(i)

        @pl.when(jnp.logical_not(is_own(b)))
        def _():
            copy_forward(b).wait_recv()

        @pl.when(is_mine(b) & jnp.logical_not(is_own(b)))
        def _():
            copy_forward(b).start()

        att32[pl.ds(pl.multiple_of(b * crows, 16), crows), :] = att[b].astype(F32)

    planes = [(j, verify) for j in range(verify)]
    planes += [(qrows + j, draft) for j in range(draft)]
    for pair in range(x_buf.shape[0] // 16):
        for h in range(heads):
            halves = []
            for at in (2 * pair, 2 * pair + 1):
                if at < len(planes):
                    start, jump = planes[at]
                    halves.append(att32[pl.ds(start + h * jump, batch, stride=crows), :])
                else:
                    halves.append(jnp.zeros((batch, HEAD_DIM), F32))
            x_buf[16 * pair : 16 * pair + 16, h * HEAD_DIM : (h + 1) * HEAD_DIM] = (
                jnp.concatenate(halves, axis=0).astype(BF16)
            )

    part_rows, part_cols = send4.shape[1:]
    all_rows = x_buf.shape[0]

    def place(at):
        return (at // col_parts) * part_rows, (at % col_parts) * part_cols

    def copy4(at, src):
        return pltpu.make_async_remote_copy(
            src_ref=send4.at[at],
            dst_ref=recv4.at[src],
            send_sem=s4_sem.at[at],
            recv_sem=r4_sem.at[src],
            device_id=(me, at),
            device_id_type=MESH,
        )

    wo_copy.wait()
    for at in range(n_head):
        r0, c0 = place(at)
        send4[at] = jnp.dot(
            x_buf[r0 : r0 + part_rows, :],
            wo_buf[:, c0 : c0 + part_cols],
            preferred_element_type=F32,
        ).astype(BF16)

        @pl.when(hd != at)
        def _():
            copy4(at, hd).start()

    def add_head(off, acc):
        src = lax.rem(hd + off, n_head)
        copy4(hd, src).wait_recv()
        return acc + recv4[src].astype(F32)

    fin[hd] = lax.fori_loop(1, n_head, add_head, send4[hd].astype(F32)).astype(BF16)

    def copy6(at, dst):
        return pltpu.make_async_remote_copy(
            src_ref=fin.at[at],
            dst_ref=fin.at[at],
            send_sem=s6_sem.at[dst],
            recv_sem=r6_sem.at[at],
            device_id=(me, dst),
            device_id_type=MESH,
        )

    @pl.loop(1, n_head)
    def _(off):
        copy6(hd, lax.rem(hd + off, n_head)).start()

    @pl.loop(1, n_head)
    def _(off):
        copy6(lax.rem(hd + off, n_head), hd).wait_recv()

    for at in range(n_head):
        r0, c0 = place(at)
        for c in range(part_cols // HEAD_DIM):
            base = (c0 // HEAD_DIM + c) * all_rows + r0
            y32[base : base + part_rows, :] = fin[
                at, :, c * HEAD_DIM : (c + 1) * HEAD_DIM
            ].astype(F32)
    target_rows = verify * batch
    chunks = range(out_v.shape[1] // HEAD_DIM)
    for c in chunks:
        out_v[:, c * HEAD_DIM : (c + 1) * HEAD_DIM] = y32[
            c * all_rows : c * all_rows + target_rows, :
        ].astype(BF16)
    for b in range(batch):
        out_d[b] = jnp.concatenate(
            [
                y32[pl.ds(c * all_rows + target_rows + b, draft, stride=batch), :]
                for c in chunks
            ],
            axis=1,
        ).astype(BF16)

    def pair_sent(b):
        for part in range(2):
            copy_pair(part, b).wait_send()

    def line_sent(b):
        @pl.when(jnp.logical_not(is_own(b)))
        def _():
            copy1(b, line).wait_send()

    side_loop(False, pair_sent)
    side_loop(True, line_sent)

    @pl.loop(0, batch)
    def _(b):
        @pl.when(b * per != me)
        def _():
            for copy in copies_up(b, me):
                copy.wait_send()

        @pl.when(is_mine(b) & jnp.logical_not(is_own(b)))
        def _():
            copy_forward(b).wait_send()

    def owner_sent():
        @pl.loop(1, n_seq)
        def _(off):
            dst = lax.rem(me + off, n_seq)
            copy_gather(query_all, s2_sem, r2_sem, my_b, dst).wait_send()

            @pl.when((dst == partner) | (lax.rem(dst, 2) == side))
            def _():
                copy_gather(att, s5_sem, r5_sem, my_b, dst).wait_send()

    on_owner(owner_sent)

    @pl.loop(1, n_head)
    def _(off):
        dst = lax.rem(hd + off, n_head)
        copy4(dst, hd).wait_send()
        copy6(hd, dst).wait_send()


def per_device(
    n_seq,
    n_head,
    hidden_states,
    w_query,
    w_key,
    w_value,
    w_out,
    key_cache,
    value_cache,
    context_lengths,
    keep_blocks,
):
    batch, verify, width = hidden_states.shape
    draft = verify - 1
    ctx_local = key_cache.shape[1]
    kv_cols = key_cache.shape[2]
    kv_local = kv_cols // HEAD_DIM
    q_cols = w_query.shape[1]
    heads = q_cols // HEAD_DIM
    out_cols = w_out.shape[1]
    slots = heads + 2 * kv_local
    rows1 = round_up(verify * slots, 16)
    srows = 2 * verify * heads
    crows = round_up((verify + draft) * heads, 16)
    lanes = round_up(srows, HEAD_DIM)
    n_rows = batch * (verify + draft)
    col_parts = math.gcd(n_head, out_cols // HEAD_DIM)
    row_parts = n_head // col_parts
    part_rows = round_up(-(-n_rows // row_parts), 16)
    part_cols = out_cols // col_parts
    all_rows = part_rows * row_parts
    n_src = n_seq + 1
    src_rows = round_up(n_src, 8)
    qpad = round_up(verify * heads, 16)
    dims = (n_seq, n_head, batch, verify, kv_local, heads, ctx_local, col_parts)

    inverse = (500000.0 ** (-(np.arange(HEAD_DIM // 2) * 2.0) / HEAD_DIM)).astype(np.float32)
    inverse = jnp.asarray(np.concatenate([inverse, inverse])[None, :])

    vmem = pl.BlockSpec(memory_space=pltpu.VMEM)
    hbm = pl.BlockSpec(memory_space=pl.ANY)
    dma = pltpu.SemaphoreType.DMA
    target, drafted = pl.pallas_call(
        functools.partial(kernel, dims),
        out_shape=(
            pltpu.VMEM((batch * verify, out_cols), BF16),
            pltpu.VMEM((batch, draft, out_cols), BF16),
        ),
        in_specs=[hbm] * 10,
        out_specs=(vmem, vmem),
        scratch_shapes=[
            pltpu.VMEM((verify * batch, width), BF16),
            pltpu.VMEM(inverse.shape, F32),
            pltpu.SMEM(context_lengths.shape, jnp.int32),
            pltpu.SMEM(keep_blocks.shape, jnp.int32),
            dma((4,)),
            pltpu.VMEM((width, q_cols + 2 * kv_cols), BF16),
            pltpu.VMEM(w_out.shape, BF16),
            pltpu.VMEM(key_cache.shape, BF16),
            pltpu.VMEM(value_cache.shape, BF16),
            pltpu.VMEM((batch * rows1, HEAD_DIM), F32),
            pltpu.VMEM((batch, rows1, HEAD_DIM), BF16),
            pltpu.VMEM((n_seq // 2, rows1, HEAD_DIM), BF16),
            pltpu.VMEM((batch, rows1, HEAD_DIM), BF16),
            pltpu.VMEM((rows1, HEAD_DIM), BF16),
            pltpu.VMEM((batch, qpad, HEAD_DIM), BF16),
            pltpu.VMEM((batch, crows, HEAD_DIM), BF16),
            pltpu.VMEM((n_src, crows, HEAD_DIM), BF16),
            pltpu.VMEM((batch, 2, lanes), F32),
            pltpu.VMEM((n_src, 2, lanes), F32),
            pltpu.VMEM((rows1, HEAD_DIM), F32),
            pltpu.VMEM((rows1, HEAD_DIM), F32),
            pltpu.VMEM((src_rows, lanes), F32),
            pltpu.VMEM((src_rows, lanes), F32),
            pltpu.VMEM((HEAD_DIM, lanes), F32),
            pltpu.VMEM((lanes, HEAD_DIM), F32),
            pltpu.VMEM((batch, crows, HEAD_DIM), BF16),
            pltpu.VMEM((2, srows + 8, HEAD_DIM), F32),
            pltpu.VMEM((2, crows + 8, HEAD_DIM), F32),
            pltpu.VMEM((batch * crows, HEAD_DIM), F32),
            pltpu.VMEM((all_rows, q_cols), BF16),
            pltpu.VMEM((n_head, part_rows, part_cols), BF16),
            pltpu.VMEM((n_head, part_rows, part_cols), BF16),
            pltpu.VMEM((n_head, part_rows, part_cols), BF16),
            pltpu.VMEM((out_cols // HEAD_DIM * all_rows, HEAD_DIM), F32),
            dma((q_cols // min(512, q_cols) + 2,)),
            dma,
            dma((batch,)),
            dma((batch,)),
            dma((2, batch)),
            dma((n_seq // 2,)),
            dma((2, batch)),
            dma((n_seq,)),
            dma((batch,)),
            dma((batch,)),
            dma((n_seq,)),
            dma((batch,)),
            dma((n_seq,)),
            dma((n_seq,)),
            dma((batch,)),
            dma((batch,)),
            dma((n_head,)),
            dma((n_head,)),
            dma((n_head,)),
            dma((n_head,)),
        ],
        compiler_params=pltpu.CompilerParams(
            collective_id=0, has_side_effects=True, vmem_limit_bytes=56 * 1024 * 1024
        ),
        name="verify_round",
    )(
        hidden_states.transpose(1, 0, 2).reshape(verify * batch, width),
        inverse,
        context_lengths,
        keep_blocks,
        w_query,
        w_key,
        w_value,
        w_out,
        key_cache,
        value_cache,
    )
    return target.reshape(verify, batch, out_cols).transpose(1, 0, 2), drafted


def solution(mesh):
    placed = (
        P(None, None, "seq"),
        P("seq", "head"),
        P("seq", "head"),
        P("seq", "head"),
        P("head", "seq"),
        P(None, "seq", "head"),
        P(None, "seq", "head"),
        P(),
        P(None, "seq"),
    )
    return jax.shard_map(
        functools.partial(per_device, mesh.shape["seq"], mesh.shape["head"]),
        mesh=mesh,
        in_specs=placed,
        out_specs=(P(None, None, "seq"), P(None, None, "seq")),
        check_vma=False,
    )
```

```python
import functools
import math

import jax
import jax.numpy as jnp
import numpy as np
from jax import lax
from jax.experimental import pallas as pl
from jax.experimental.pallas import tpu as pltpu
from jax.sharding import PartitionSpec as P

HEAD_DIM = 128
BLOCK = 128
NEG = -1e30
MESH = pl.DeviceIdType.MESH
F32 = jnp.float32
BF16 = jnp.bfloat16


def round_up(value, unit):
    return -(-value // unit) * unit


def kernel(
    dims,
    hid_in,
    inv_in,
    ctx_in,
    keep_in,
    wq,
    wk,
    wv,
    wo,
    kc,
    vc,
    out_v,
    out_d,
    hid,
    inv,
    ctx,
    keep,
    small_sem,
    w_buf,
    wo_buf,
    k_buf,
    v_buf,
    pack,
    send1,
    recv1,
    qkv,
    query_all,
    send3,
    recv3,
    sendml,
    recvml,
    cos_buf,
    sin_buf,
    mscr,
    lscr,
    coefs,
    coef_t,
    att,
    spare,
    dense,
    att32,
    x_buf,
    send4,
    recv4,
    fin,
    y32,
    w_sem,
    wo_sem,
    k_sem,
    v_sem,
    s1_sem,
    r1_sem,
    s2_sem,
    r2_sem,
    s3_sem,
    r3_sem,
    sm_sem,
    rm_sem,
    s5_sem,
    r5_sem,
    s4_sem,
    r4_sem,
    s6_sem,
    r6_sem,
):
    n_seq, n_head, batch, verify, kv_local, heads, ctx_local, col_parts = dims
    draft = verify - 1
    group = heads // kv_local
    per = n_seq // batch
    slots = heads + 2 * kv_local
    qrows = verify * heads
    grows = verify * group
    srows = 2 * qrows
    q_cols = heads * HEAD_DIM
    kv_cols = kv_local * HEAD_DIM
    me = lax.axis_index("seq")
    hd = lax.axis_index("head")
    my_b = me // per
    scale = HEAD_DIM ** (-0.5) * math.log2(math.e)
    rows1 = send1.shape[1]
    crows = att.shape[1]
    lines = n_seq // 2
    line, side = me // 2, lax.rem(me, 2)

    def use_order(i):
        if per > 1:
            return lax.rem(my_b + i, batch)
        return 2 * lax.rem(line + i // 2, lines) + lax.rem(side + i, 2)

    def is_own(b):
        return b * per == me

    def on_owner(body):
        if per == 1:
            body()
        else:
            pl.when(lax.rem(me, per) == 0)(body)

    barrier = pltpu.get_barrier_semaphore()
    for off in range(1, n_seq):
        pl.semaphore_signal(
            barrier, inc=1, device_id=(lax.rem(me + off, n_seq), hd), device_id_type=MESH
        )
    for off in range(1, n_head):
        pl.semaphore_signal(
            barrier, inc=1, device_id=(me, lax.rem(hd + off, n_head)), device_id_type=MESH
        )

    small = [
        pltpu.make_async_copy(src, dst, small_sem.at[at])
        for at, (src, dst) in enumerate(
            ((ctx_in, ctx), (inv_in, inv), (hid_in, hid), (keep_in, keep))
        )
    ]
    for copy in small:
        copy.start()

    step = min(512, q_cols)
    pieces = [(wq, c, step, c) for c in range(0, q_cols, step)]
    pieces += [(wk, 0, kv_cols, q_cols), (wv, 0, kv_cols, q_cols + kv_cols)]
    w_copies = []
    for at, (src, c0, width, d0) in enumerate(pieces):
        copy = pltpu.make_async_copy(
            src.at[:, pl.ds(c0, width)], w_buf.at[:, pl.ds(d0, width)], w_sem.at[at]
        )
        copy.start()
        w_copies.append(copy)

    def cache_copies(b):
        return (
            pltpu.make_async_copy(kc.at[b], k_buf.at[b], k_sem.at[b]),
            pltpu.make_async_copy(vc.at[b], v_buf.at[b], v_sem.at[b]),
        )

    def rotation():
        shape = (8, HEAD_DIM)
        lane = lax.broadcasted_iota(jnp.int32, shape, 1)
        pos = (ctx[my_b] + lax.broadcasted_iota(jnp.int32, shape, 0)).astype(F32)
        angle = pos * inv[...]
        cosine = jnp.cos(angle)
        sine = jnp.sin(angle)
        sine = jnp.where(lane < HEAD_DIM // 2, -sine, sine)
        cos_buf[...] = jnp.ones_like(cos_buf)
        sin_buf[...] = jnp.zeros_like(sin_buf)
        for slot in range(heads + kv_local):
            r0 = slot * verify
            cos_buf[r0 : r0 + 8, :] = cosine
            sin_buf[r0 : r0 + 8, :] = sine
        r0 = (heads + kv_local) * verify
        cos_buf[r0 : r0 + 8, :] = jnp.ones(shape, F32)
        sin_buf[r0 : r0 + 8, :] = jnp.zeros(shape, F32)

    for copy in small:
        copy.wait()
    on_owner(rotation)

    pack[...] = jnp.zeros_like(pack)
    coefs[...] = jnp.zeros_like(coefs)
    spare[...] = jnp.zeros_like(spare)
    dense[...] = jnp.zeros_like(dense)
    x_in = hid[...]
    def copy1(part, b, src):
        rows = pl.ds(*parts[part])
        return pltpu.make_async_remote_copy(
            src_ref=send1.at[b, rows],
            dst_ref=recv1.at[src, rows],
            send_sem=s1_sem.at[part, b],
            recv_sem=r1_sem.at[part, src],
            device_id=(b * per, hd),
            device_id_type=MESH,
        )

    def send_part(part):
        r0, count = parts[part]

        @pl.loop(0, batch)
        def _(i):
            b = lax.rem(my_b + 1 + i, batch)
            rows = pl.ds(pl.multiple_of(b * rows1 + r0, 16), count)
            send1[b, r0 : r0 + count, :] = pack[rows, :].astype(BF16)

            @pl.when(b * per != me)
            def _():
                copy1(part, b, me).start()

    early = rows1 // 2 // 16 * 16
    parts = ((0, early), (early, rows1 - early))
    sent_early = False
    for at, (copy, (src, c0, width, d0)) in enumerate(zip(w_copies, pieces)):
        copy.wait()
        piece = jnp.dot(x_in, w_buf[:, d0 : d0 + width], preferred_element_type=F32)
        for s in range(width // HEAD_DIM):
            slot = d0 // HEAD_DIM + s
            for j in range(verify):
                pack[pl.ds(slot * verify + j, batch, stride=rows1), :] = piece[
                    j * batch : (j + 1) * batch, s * HEAD_DIM : (s + 1) * HEAD_DIM
                ]
        if not sent_early and (d0 + width) // HEAD_DIM * verify >= early:
            sent_early = True
            pl.semaphore_wait(barrier, n_seq - 1 + n_head - 1)
            send_part(0)
    send_part(1)

    @pl.loop(0, batch)
    def _(i):
        for copy in cache_copies(use_order(i)):
            copy.start()

    wo_copy = pltpu.make_async_copy(wo, wo_buf, wo_sem)
    wo_copy.start()

    def copy_gather(buf, send_sem, recv_sem, b, dst):
        return pltpu.make_async_remote_copy(
            src_ref=buf.at[b],
            dst_ref=buf.at[b],
            send_sem=send_sem.at[dst],
            recv_sem=recv_sem.at[b],
            device_id=(dst, hd),
            device_id_type=MESH,
        )

    def owner_rotate():
        def add(off, acc):
            src = lax.rem(me + off, n_seq)
            for part in range(2):
                copy1(part, my_b, src).wait_recv()
            return acc + recv1[src].astype(F32)

        total = lax.fori_loop(1, n_seq, add, send1[my_b].astype(F32))
        turned = total * cos_buf[...] + pltpu.roll(total, HEAD_DIM // 2, 1) * sin_buf[...]
        qkv[...] = turned.astype(BF16)
        query_all[my_b] = turned[0 : query_all.shape[1]].astype(BF16)

        @pl.loop(1, n_seq)
        def _(off):
            if per > 1:
                dst = lax.rem(me + off, n_seq)
            else:
                dst = 2 * lax.rem(line + n_seq - off // 2, lines) + lax.rem(side + off, 2)
            copy_gather(query_all, s2_sem, r2_sem, my_b, dst).start()

    on_owner(owner_rotate)

    def compact(value, at):
        loose = spare.at[at]
        loose[0:srows, :] = value
        tight = dense.at[at]
        for h in range(heads):
            r0, r1 = qrows + h * draft, qrows + h * verify
            tight[r0 : r0 + 8, :] = loose[r1 : r1 + 8, :]
        return jnp.concatenate([value[0:qrows], tight[qrows:crows, :]], axis=0)

    def statistics(peak, total):
        lane = lax.broadcasted_iota(jnp.int32, (srows, HEAD_DIM), 1)
        wide = jnp.where(lane == 0, peak, jnp.where(lane == 1, total, 0.0))
        extra = sendml.shape[2] - srows
        if extra:
            wide = jnp.concatenate([wide, jnp.zeros((extra, HEAD_DIM), F32)], axis=0)
        return wide.T[0:2, :]

    def softmax(scores, mask):
        masked = jnp.where(mask, scores, NEG)
        peak = jnp.maximum(jnp.max(masked, axis=1, keepdims=True), NEG / 8)
        weights = jnp.exp2(masked - peak)
        return peak, jnp.sum(weights, axis=1, keepdims=True), weights

    def copies_up(b, src):
        return [
            pltpu.make_async_remote_copy(
                src_ref=source.at[b],
                dst_ref=target.at[src],
                send_sem=send_sem.at[b],
                recv_sem=recv_sem.at[src],
                device_id=(b * per, hd),
                device_id_type=MESH,
            )
            for source, target, send_sem, recv_sem in (
                (sendml, recvml, sm_sem, rm_sem),
                (send3, recv3, s3_sem, r3_sem),
            )
        ]

    def attend(b, at):
        query = query_all[b].astype(F32)[0:qrows]
        row = lax.broadcasted_iota(jnp.int32, query.shape, 0)
        spread = jnp.concatenate(
            [
                jnp.where((row >= kv * grows) & (row < (kv + 1) * grows), query, 0.0)
                for kv in range(kv_local)
            ],
            axis=1,
        ).astype(BF16)
        scores = (
            lax.dot_general(
                spread, k_buf[b], (((1,), (1,)), ((), ())), preferred_element_type=F32
            )
            * scale
        )
        lane = lax.broadcasted_iota(jnp.int32, (1, ctx_local), 1)
        live = lane + me * ctx_local < ctx[b]
        flags = jnp.concatenate(
            [
                jnp.full((1, BLOCK), keep[b, blk], jnp.int32)
                for blk in range(ctx_local // BLOCK)
            ],
            axis=1,
        )
        kept = live & (flags > 0)
        t_peak, t_total, t_weights = softmax(scores, live)
        d_peak, d_total, d_weights = softmax(scores, kept)
        weights = jnp.concatenate([t_weights, d_weights], axis=0).astype(BF16)
        values = jnp.dot(weights, v_buf[b], preferred_element_type=F32)
        blocks = []
        for half in range(2):
            for kv in range(kv_local):
                r0 = half * qrows + kv * grows
                blocks.append(values[r0 : r0 + grows, kv * HEAD_DIM : (kv + 1) * HEAD_DIM])
        send3[b] = compact(jnp.concatenate(blocks, axis=0), at).astype(BF16)
        sendml[b] = statistics(
            jnp.concatenate([t_peak, d_peak], axis=0),
            jnp.concatenate([t_total, d_total], axis=0),
        )

    together = 2

    @pl.loop(0, batch // together)
    def _(i):
        several = [use_order(i * together + at) for at in range(together)]
        for b in several:

            @pl.when(jnp.logical_not(is_own(b)))
            def _(b=b):
                copy_gather(query_all, s2_sem, r2_sem, b, me).wait_recv()

            for copy in cache_copies(b):
                copy.wait()
        for at, b in enumerate(several):
            attend(b, at)
        for b in several:

            @pl.when(jnp.logical_not(is_own(b)))
            def _(b=b):
                for copy in copies_up(b, me):
                    copy.start()

    def owner_merge():
        rows_all = qkv[...].astype(F32)
        query = rows_all[0:qrows]
        raw = lax.dot_general(
            query.astype(BF16), qkv[...], (((1,), (1,)), ((), ())), preferred_element_type=F32
        )
        scores = raw * scale
        row = lax.broadcasted_iota(jnp.int32, scores.shape, 0)
        col = lax.broadcasted_iota(jnp.int32, scores.shape, 1) - qrows
        row_head = lax.div(row, verify)
        row_j = row - row_head * verify
        row_kv = lax.div(row_head, group)
        first = row_kv * verify
        mask = (col >= first) & (col <= first + row_j)
        peak, total, weights = softmax(scores, mask)
        weights = weights.astype(BF16)
        vrow = lax.broadcasted_iota(jnp.int32, rows_all.shape, 0) - qrows
        shift = kv_local * verify
        moved = pltpu.roll(rows_all, rows_all.shape[0] - shift, 0)
        moved = jnp.where((vrow >= 0) & (vrow < shift), moved, 0.0).astype(BF16)
        values = jnp.dot(weights, moved, preferred_element_type=F32)
        recv3[n_seq] = compact(jnp.concatenate([values, values], axis=0), 0).astype(BF16)
        recvml[n_seq] = statistics(
            jnp.concatenate([peak, peak], axis=0), jnp.concatenate([total, total], axis=0)
        )
        recv3[me] = send3[my_b]
        recvml[me] = sendml[my_b]

        @pl.loop(1, n_seq)
        def _(off):
            for copy in copies_up(my_b, lax.rem(me + off, n_seq)):
                copy.wait_recv()

        n_src = n_seq + 1
        for s in range(n_src):
            both = recvml[s]
            mscr[s : s + 1, :] = both[0:1]
            lscr[s : s + 1, :] = both[1:2]
        m_all = mscr[0:n_src, :]
        l_all = lscr[0:n_src, :]
        factor = jnp.exp2(m_all - jnp.max(m_all, axis=0, keepdims=True))
        norm = jnp.sum(factor * l_all, axis=0, keepdims=True)
        norm = jnp.where(norm > 0.0, norm, 1.0)
        coefs[0:n_src, :] = factor / norm
        coef_t[0:crows, :] = compact(coefs[...].T[0:srows], 0)
        acc = jnp.zeros((crows, HEAD_DIM), F32)
        for s in range(n_src):
            acc = acc + coef_t[0:crows, s : s + 1] * recv3[s].astype(F32)
        att[my_b] = acc.astype(BF16)
        @pl.loop(0, lines)
        def _(t):
            far = jnp.where(2 * line < lines, lines - 1 - t, t)
            for at in range(2):
                dst = 2 * far + at

                @pl.when(dst != me)
                def _(dst=dst):
                    copy_gather(att, s5_sem, r5_sem, my_b, dst).start()

    on_owner(owner_merge)

    @pl.loop(0, batch)
    def _(i):
        b = use_order(i)

        @pl.when(jnp.logical_not(is_own(b)))
        def _():
            copy_gather(att, s5_sem, r5_sem, b, me).wait_recv()

        att32[pl.ds(pl.multiple_of(b * crows, 16), crows), :] = att[b].astype(F32)

    planes = [(j, verify) for j in range(verify)]
    planes += [(qrows + j, draft) for j in range(draft)]
    for pair in range(x_buf.shape[0] // 16):
        for h in range(heads):
            halves = []
            for at in (2 * pair, 2 * pair + 1):
                if at < len(planes):
                    start, jump = planes[at]
                    halves.append(att32[pl.ds(start + h * jump, batch, stride=crows), :])
                else:
                    halves.append(jnp.zeros((batch, HEAD_DIM), F32))
            x_buf[16 * pair : 16 * pair + 16, h * HEAD_DIM : (h + 1) * HEAD_DIM] = (
                jnp.concatenate(halves, axis=0).astype(BF16)
            )

    part_rows, part_cols = send4.shape[1:]
    all_rows = x_buf.shape[0]

    def place(at):
        return (at // col_parts) * part_rows, (at % col_parts) * part_cols

    def copy4(at, src):
        return pltpu.make_async_remote_copy(
            src_ref=send4.at[at],
            dst_ref=recv4.at[src],
            send_sem=s4_sem.at[at],
            recv_sem=r4_sem.at[src],
            device_id=(me, at),
            device_id_type=MESH,
        )

    wo_copy.wait()

    @pl.loop(1, n_head + 1)
    def _(off):
        at = lax.rem(hd + off, n_head)
        r0 = pl.multiple_of((at // col_parts) * part_rows, 16)
        c0 = pl.multiple_of(lax.rem(at, col_parts) * part_cols, HEAD_DIM)
        send4[at] = jnp.dot(
            x_buf[pl.ds(r0, part_rows), :],
            wo_buf[:, pl.ds(c0, part_cols)],
            preferred_element_type=F32,
        ).astype(BF16)

        @pl.when(off < n_head)
        def _():
            copy4(at, hd).start()

    def add_head(off, acc):
        src = lax.rem(hd + off, n_head)
        copy4(hd, src).wait_recv()
        return acc + recv4[src].astype(F32)

    fin[hd] = lax.fori_loop(1, n_head, add_head, send4[hd].astype(F32)).astype(BF16)

    def copy6(at, dst):
        return pltpu.make_async_remote_copy(
            src_ref=fin.at[at],
            dst_ref=fin.at[at],
            send_sem=s6_sem.at[dst],
            recv_sem=r6_sem.at[at],
            device_id=(me, dst),
            device_id_type=MESH,
        )

    @pl.loop(1, n_head)
    def _(off):
        copy6(hd, lax.rem(hd + off, n_head)).start()

    @pl.loop(1, n_head)
    def _(off):
        copy6(lax.rem(hd + off, n_head), hd).wait_recv()

    for at in range(n_head):
        r0, c0 = place(at)
        for c in range(part_cols // HEAD_DIM):
            base = (c0 // HEAD_DIM + c) * all_rows + r0
            y32[base : base + part_rows, :] = fin[
                at, :, c * HEAD_DIM : (c + 1) * HEAD_DIM
            ].astype(F32)
    target_rows = verify * batch
    chunks = range(out_v.shape[1] // HEAD_DIM)
    for c in chunks:
        out_v[:, c * HEAD_DIM : (c + 1) * HEAD_DIM] = y32[
            c * all_rows : c * all_rows + target_rows, :
        ].astype(BF16)
    for b in range(batch):
        out_d[b] = jnp.concatenate(
            [
                y32[pl.ds(c * all_rows + target_rows + b, draft, stride=batch), :]
                for c in chunks
            ],
            axis=1,
        ).astype(BF16)

    @pl.loop(0, batch)
    def _(b):
        @pl.when(b * per != me)
        def _():
            for part in range(2):
                copy1(part, b, me).wait_send()
            for copy in copies_up(b, me):
                copy.wait_send()

    def owner_sent():
        @pl.loop(1, n_seq)
        def _(off):
            dst = lax.rem(me + off, n_seq)
            copy_gather(query_all, s2_sem, r2_sem, my_b, dst).wait_send()
            copy_gather(att, s5_sem, r5_sem, my_b, dst).wait_send()

    on_owner(owner_sent)

    @pl.loop(1, n_head)
    def _(off):
        dst = lax.rem(hd + off, n_head)
        copy4(dst, hd).wait_send()
        copy6(hd, dst).wait_send()


def per_device(
    n_seq,
    n_head,
    hidden_states,
    w_query,
    w_key,
    w_value,
    w_out,
    key_cache,
    value_cache,
    context_lengths,
    keep_blocks,
):
    batch, verify, width = hidden_states.shape
    draft = verify - 1
    ctx_local = key_cache.shape[1]
    kv_cols = key_cache.shape[2]
    kv_local = kv_cols // HEAD_DIM
    q_cols = w_query.shape[1]
    heads = q_cols // HEAD_DIM
    out_cols = w_out.shape[1]
    slots = heads + 2 * kv_local
    rows1 = round_up(verify * slots, 16)
    srows = 2 * verify * heads
    crows = round_up((verify + draft) * heads, 16)
    lanes = round_up(srows, HEAD_DIM)
    n_rows = batch * (verify + draft)
    col_parts = math.gcd(n_head, out_cols // HEAD_DIM)
    row_parts = n_head // col_parts
    part_rows = round_up(-(-n_rows // row_parts), 16)
    part_cols = out_cols // col_parts
    all_rows = part_rows * row_parts
    n_src = n_seq + 1
    src_rows = round_up(n_src, 8)
    qpad = round_up(verify * heads, 16)
    dims = (n_seq, n_head, batch, verify, kv_local, heads, ctx_local, col_parts)

    inverse = (500000.0 ** (-(np.arange(HEAD_DIM // 2) * 2.0) / HEAD_DIM)).astype(np.float32)
    inverse = jnp.asarray(np.concatenate([inverse, inverse])[None, :])

    vmem = pl.BlockSpec(memory_space=pltpu.VMEM)
    hbm = pl.BlockSpec(memory_space=pl.ANY)
    dma = pltpu.SemaphoreType.DMA
    target, drafted = pl.pallas_call(
        functools.partial(kernel, dims),
        out_shape=(
            pltpu.VMEM((batch * verify, out_cols), BF16),
            pltpu.VMEM((batch, draft, out_cols), BF16),
        ),
        in_specs=[hbm] * 10,
        out_specs=(vmem, vmem),
        scratch_shapes=[
            pltpu.VMEM((verify * batch, width), BF16),
            pltpu.VMEM(inverse.shape, F32),
            pltpu.SMEM(context_lengths.shape, jnp.int32),
            pltpu.SMEM(keep_blocks.shape, jnp.int32),
            dma((4,)),
            pltpu.VMEM((width, q_cols + 2 * kv_cols), BF16),
            pltpu.VMEM(w_out.shape, BF16),
            pltpu.VMEM(key_cache.shape, BF16),
            pltpu.VMEM(value_cache.shape, BF16),
            pltpu.VMEM((batch * rows1, HEAD_DIM), F32),
            pltpu.VMEM((batch, rows1, HEAD_DIM), BF16),
            pltpu.VMEM((n_seq, rows1, HEAD_DIM), BF16),
            pltpu.VMEM((rows1, HEAD_DIM), BF16),
            pltpu.VMEM((batch, qpad, HEAD_DIM), BF16),
            pltpu.VMEM((batch, crows, HEAD_DIM), BF16),
            pltpu.VMEM((n_src, crows, HEAD_DIM), BF16),
            pltpu.VMEM((batch, 2, lanes), F32),
            pltpu.VMEM((n_src, 2, lanes), F32),
            pltpu.VMEM((rows1, HEAD_DIM), F32),
            pltpu.VMEM((rows1, HEAD_DIM), F32),
            pltpu.VMEM((src_rows, lanes), F32),
            pltpu.VMEM((src_rows, lanes), F32),
            pltpu.VMEM((HEAD_DIM, lanes), F32),
            pltpu.VMEM((lanes, HEAD_DIM), F32),
            pltpu.VMEM((batch, crows, HEAD_DIM), BF16),
            pltpu.VMEM((2, srows + 8, HEAD_DIM), F32),
            pltpu.VMEM((2, crows + 8, HEAD_DIM), F32),
            pltpu.VMEM((batch * crows, HEAD_DIM), F32),
            pltpu.VMEM((all_rows, q_cols), BF16),
            pltpu.VMEM((n_head, part_rows, part_cols), BF16),
            pltpu.VMEM((n_head, part_rows, part_cols), BF16),
            pltpu.VMEM((n_head, part_rows, part_cols), BF16),
            pltpu.VMEM((out_cols // HEAD_DIM * all_rows, HEAD_DIM), F32),
            dma((q_cols // min(512, q_cols) + 2,)),
            dma,
            dma((batch,)),
            dma((batch,)),
            dma((2, batch)),
            dma((2, n_seq)),
            dma((n_seq,)),
            dma((batch,)),
            dma((batch,)),
            dma((n_seq,)),
            dma((batch,)),
            dma((n_seq,)),
            dma((n_seq,)),
            dma((batch,)),
            dma((n_head,)),
            dma((n_head,)),
            dma((n_head,)),
            dma((n_head,)),
        ],
        compiler_params=pltpu.CompilerParams(
            collective_id=0, has_side_effects=True, vmem_limit_bytes=56 * 1024 * 1024
        ),
        name="verify_round",
    )(
        hidden_states.transpose(1, 0, 2).reshape(verify * batch, width),
        inverse,
        context_lengths,
        keep_blocks,
        w_query,
        w_key,
        w_value,
        w_out,
        key_cache,
        value_cache,
    )
    return target.reshape(verify, batch, out_cols).transpose(1, 0, 2), drafted


def solution(mesh):
    placed = (
        P(None, None, "seq"),
        P("seq", "head"),
        P("seq", "head"),
        P("seq", "head"),
        P("head", "seq"),
        P(None, "seq", "head"),
        P(None, "seq", "head"),
        P(),
        P(None, "seq"),
    )
    return jax.shard_map(
        functools.partial(per_device, mesh.shape["seq"], mesh.shape["head"]),
        mesh=mesh,
        in_specs=placed,
        out_specs=(P(None, None, "seq"), P(None, None, "seq")),
        check_vma=False,
    )
```

```python
import functools
import math

import jax
import jax.numpy as jnp
import numpy as np
from jax import lax
from jax.experimental import pallas as pl
from jax.experimental.pallas import tpu as pltpu
from jax.sharding import PartitionSpec as P

HEAD_DIM = 128
BLOCK = 128
NEG = -1e30
MESH = pl.DeviceIdType.MESH
F32 = jnp.float32
BF16 = jnp.bfloat16


def round_up(value, unit):
    return -(-value // unit) * unit


def kernel(
    dims,
    hid_in,
    inv_in,
    ctx_in,
    keep_in,
    wq,
    wk,
    wv,
    wo,
    kc,
    vc,
    out_v,
    out_d,
    hid,
    inv,
    ctx,
    keep,
    small_sem,
    w_buf,
    wo_buf,
    k_buf,
    v_buf,
    pack,
    send1,
    recv1,
    qkv,
    query_all,
    send3,
    recv3,
    sendml,
    recvml,
    cos_buf,
    sin_buf,
    mscr,
    lscr,
    coefs,
    coef_t,
    att,
    spare,
    dense,
    att32,
    x_buf,
    send4,
    recv4,
    fin,
    y32,
    w_sem,
    wo_sem,
    k_sem,
    v_sem,
    s1_sem,
    r1_sem,
    s2_sem,
    r2_sem,
    s3_sem,
    r3_sem,
    sm_sem,
    rm_sem,
    s5_sem,
    r5_sem,
    s4_sem,
    r4_sem,
    s6_sem,
    r6_sem,
):
    n_seq, n_head, batch, verify, kv_local, heads, ctx_local, col_parts = dims
    draft = verify - 1
    group = heads // kv_local
    per = n_seq // batch
    slots = heads + 2 * kv_local
    qrows = verify * heads
    grows = verify * group
    srows = 2 * qrows
    q_cols = heads * HEAD_DIM
    kv_cols = kv_local * HEAD_DIM
    me = lax.axis_index("seq")
    hd = lax.axis_index("head")
    my_b = me // per
    scale = HEAD_DIM ** (-0.5) * math.log2(math.e)
    rows1 = send1.shape[1]
    crows = att.shape[1]
    lines = n_seq // 2
    line, side = me // 2, lax.rem(me, 2)

    def use_order(i):
        if per > 1:
            return lax.rem(my_b + i, batch)
        return 2 * lax.rem(line + i // 2, lines) + lax.rem(side + i, 2)

    def far_order(i):
        t = i // 2
        return 2 * jnp.where(2 * line < lines, lines - 1 - t, t) + lax.rem(i, 2)

    def is_own(b):
        return b * per == me

    def on_owner(body):
        if per == 1:
            body()
        else:
            pl.when(lax.rem(me, per) == 0)(body)

    barrier = pltpu.get_barrier_semaphore()
    for off in range(1, n_seq):
        pl.semaphore_signal(
            barrier, inc=1, device_id=(lax.rem(me + off, n_seq), hd), device_id_type=MESH
        )
    for off in range(1, n_head):
        pl.semaphore_signal(
            barrier, inc=1, device_id=(me, lax.rem(hd + off, n_head)), device_id_type=MESH
        )

    small = [
        pltpu.make_async_copy(src, dst, small_sem.at[at])
        for at, (src, dst) in enumerate(
            ((ctx_in, ctx), (inv_in, inv), (hid_in, hid), (keep_in, keep))
        )
    ]
    for copy in small:
        copy.start()

    step = min(512, q_cols)
    pieces = [(wq, c, step, c) for c in range(0, q_cols, step)]
    pieces += [(wk, 0, kv_cols, q_cols), (wv, 0, kv_cols, q_cols + kv_cols)]
    w_copies = []
    for at, (src, c0, width, d0) in enumerate(pieces):
        copy = pltpu.make_async_copy(
            src.at[:, pl.ds(c0, width)], w_buf.at[:, pl.ds(d0, width)], w_sem.at[at]
        )
        copy.start()
        w_copies.append(copy)

    def cache_copies(b):
        return (
            pltpu.make_async_copy(kc.at[b], k_buf.at[b], k_sem.at[b]),
            pltpu.make_async_copy(vc.at[b], v_buf.at[b], v_sem.at[b]),
        )

    def rotation():
        shape = (8, HEAD_DIM)
        lane = lax.broadcasted_iota(jnp.int32, shape, 1)
        pos = (ctx[my_b] + lax.broadcasted_iota(jnp.int32, shape, 0)).astype(F32)
        angle = pos * inv[...]
        cosine = jnp.cos(angle)
        sine = jnp.sin(angle)
        sine = jnp.where(lane < HEAD_DIM // 2, -sine, sine)
        cos_buf[...] = jnp.ones_like(cos_buf)
        sin_buf[...] = jnp.zeros_like(sin_buf)
        for slot in range(heads + kv_local):
            r0 = slot * verify
            cos_buf[r0 : r0 + 8, :] = cosine
            sin_buf[r0 : r0 + 8, :] = sine
        r0 = (heads + kv_local) * verify
        cos_buf[r0 : r0 + 8, :] = jnp.ones(shape, F32)
        sin_buf[r0 : r0 + 8, :] = jnp.zeros(shape, F32)

    for copy in small:
        copy.wait()
    on_owner(rotation)

    pack[...] = jnp.zeros_like(pack)
    coefs[...] = jnp.zeros_like(coefs)
    spare[...] = jnp.zeros_like(spare)
    dense[...] = jnp.zeros_like(dense)
    x_in = hid[...]
    def copy1(part, b, src):
        rows = pl.ds(*parts[part])
        return pltpu.make_async_remote_copy(
            src_ref=send1.at[b, rows],
            dst_ref=recv1.at[src, rows],
            send_sem=s1_sem.at[part, b],
            recv_sem=r1_sem.at[part, src],
            device_id=(b * per, hd),
            device_id_type=MESH,
        )

    def send_part(part):
        r0, count = parts[part]

        @pl.loop(0, batch)
        def _(i):
            b = far_order(i) if per == 1 else lax.rem(my_b + 1 + i, batch)
            rows = pl.ds(pl.multiple_of(b * rows1 + r0, 16), count)
            send1[b, r0 : r0 + count, :] = pack[rows, :].astype(BF16)

            @pl.when(b * per != me)
            def _():
                copy1(part, b, me).start()

    early = rows1 // 2 // 16 * 16
    parts = ((0, early), (early, rows1 - early))
    sent_early = False
    for at, (copy, (src, c0, width, d0)) in enumerate(zip(w_copies, pieces)):
        copy.wait()
        piece = jnp.dot(x_in, w_buf[:, d0 : d0 + width], preferred_element_type=F32)
        for s in range(width // HEAD_DIM):
            slot = d0 // HEAD_DIM + s
            for j in range(verify):
                pack[pl.ds(slot * verify + j, batch, stride=rows1), :] = piece[
                    j * batch : (j + 1) * batch, s * HEAD_DIM : (s + 1) * HEAD_DIM
                ]
        if not sent_early and (d0 + width) // HEAD_DIM * verify >= early:
            sent_early = True
            pl.semaphore_wait(barrier, n_seq - 1 + n_head - 1)
            send_part(0)
    send_part(1)

    @pl.loop(0, batch)
    def _(i):
        for copy in cache_copies(use_order(i)):
            copy.start()

    wo_copy = pltpu.make_async_copy(wo, wo_buf, wo_sem)
    wo_copy.start()

    def copy_gather(buf, send_sem, recv_sem, b, dst):
        return pltpu.make_async_remote_copy(
            src_ref=buf.at[b],
            dst_ref=buf.at[b],
            send_sem=send_sem.at[dst],
            recv_sem=recv_sem.at[b],
            device_id=(dst, hd),
            device_id_type=MESH,
        )

    def owner_rotate():
        def add(off, acc):
            src = lax.rem(me + off, n_seq)
            for part in range(2):
                copy1(part, my_b, src).wait_recv()
            return acc + recv1[src].astype(F32)

        total = lax.fori_loop(1, n_seq, add, send1[my_b].astype(F32))
        turned = total * cos_buf[...] + pltpu.roll(total, HEAD_DIM // 2, 1) * sin_buf[...]
        qkv[...] = turned.astype(BF16)
        query_all[my_b] = turned[0 : query_all.shape[1]].astype(BF16)

        @pl.loop(0, n_seq)
        def _(i):
            dst = far_order(i)

            @pl.when(dst != me)
            def _():
                copy_gather(query_all, s2_sem, r2_sem, my_b, dst).start()

    on_owner(owner_rotate)

    def compact(value, at):
        loose = spare.at[at]
        loose[0:srows, :] = value
        tight = dense.at[at]
        for h in range(heads):
            r0, r1 = qrows + h * draft, qrows + h * verify
            tight[r0 : r0 + 8, :] = loose[r1 : r1 + 8, :]
        return jnp.concatenate([value[0:qrows], tight[qrows:crows, :]], axis=0)

    def statistics(peak, total):
        lane = lax.broadcasted_iota(jnp.int32, (srows, HEAD_DIM), 1)
        wide = jnp.where(lane == 0, peak, jnp.where(lane == 1, total, 0.0))
        extra = sendml.shape[2] - srows
        if extra:
            wide = jnp.concatenate([wide, jnp.zeros((extra, HEAD_DIM), F32)], axis=0)
        return wide.T[0:2, :]

    def softmax(scores, mask):
        masked = jnp.where(mask, scores, NEG)
        peak = jnp.maximum(jnp.max(masked, axis=1, keepdims=True), NEG / 8)
        weights = jnp.exp2(masked - peak)
        return peak, jnp.sum(weights, axis=1, keepdims=True), weights

    def copies_up(b, src):
        return [
            pltpu.make_async_remote_copy(
                src_ref=source.at[b],
                dst_ref=target.at[src],
                send_sem=send_sem.at[b],
                recv_sem=recv_sem.at[src],
                device_id=(b * per, hd),
                device_id_type=MESH,
            )
            for source, target, send_sem, recv_sem in (
                (sendml, recvml, sm_sem, rm_sem),
                (send3, recv3, s3_sem, r3_sem),
            )
        ]

    def attend(b, at):
        query = query_all[b].astype(F32)[0:qrows]
        row = lax.broadcasted_iota(jnp.int32, query.shape, 0)
        spread = jnp.concatenate(
            [
                jnp.where((row >= kv * grows) & (row < (kv + 1) * grows), query, 0.0)
                for kv in range(kv_local)
            ],
            axis=1,
        ).astype(BF16)
        scores = (
            lax.dot_general(
                spread, k_buf[b], (((1,), (1,)), ((), ())), preferred_element_type=F32
            )
            * scale
        )
        lane = lax.broadcasted_iota(jnp.int32, (1, ctx_local), 1)
        live = lane + me * ctx_local < ctx[b]
        flags = jnp.concatenate(
            [
                jnp.full((1, BLOCK), keep[b, blk], jnp.int32)
                for blk in range(ctx_local // BLOCK)
            ],
            axis=1,
        )
        kept = live & (flags > 0)
        t_peak, t_total, t_weights = softmax(scores, live)
        d_peak, d_total, d_weights = softmax(scores, kept)
        weights = jnp.concatenate([t_weights, d_weights], axis=0).astype(BF16)
        values = jnp.dot(weights, v_buf[b], preferred_element_type=F32)
        blocks = []
        for half in range(2):
            for kv in range(kv_local):
                r0 = half * qrows + kv * grows
                blocks.append(values[r0 : r0 + grows, kv * HEAD_DIM : (kv + 1) * HEAD_DIM])
        send3[b] = compact(jnp.concatenate(blocks, axis=0), at).astype(BF16)
        sendml[b] = statistics(
            jnp.concatenate([t_peak, d_peak], axis=0),
            jnp.concatenate([t_total, d_total], axis=0),
        )

    together = 2

    @pl.loop(0, batch // together)
    def _(i):
        several = [use_order(i * together + at) for at in range(together)]
        for b in several:

            @pl.when(jnp.logical_not(is_own(b)))
            def _(b=b):
                copy_gather(query_all, s2_sem, r2_sem, b, me).wait_recv()

            for copy in cache_copies(b):
                copy.wait()
        for at, b in enumerate(several):
            attend(b, at)
        for b in several:

            @pl.when(jnp.logical_not(is_own(b)))
            def _(b=b):
                for copy in copies_up(b, me):
                    copy.start()

    def owner_merge():
        rows_all = qkv[...].astype(F32)
        query = rows_all[0:qrows]
        raw = lax.dot_general(
            query.astype(BF16), qkv[...], (((1,), (1,)), ((), ())), preferred_element_type=F32
        )
        scores = raw * scale
        row = lax.broadcasted_iota(jnp.int32, scores.shape, 0)
        col = lax.broadcasted_iota(jnp.int32, scores.shape, 1) - qrows
        row_head = lax.div(row, verify)
        row_j = row - row_head * verify
        row_kv = lax.div(row_head, group)
        first = row_kv * verify
        mask = (col >= first) & (col <= first + row_j)
        peak, total, weights = softmax(scores, mask)
        weights = weights.astype(BF16)
        vrow = lax.broadcasted_iota(jnp.int32, rows_all.shape, 0) - qrows
        shift = kv_local * verify
        moved = pltpu.roll(rows_all, rows_all.shape[0] - shift, 0)
        moved = jnp.where((vrow >= 0) & (vrow < shift), moved, 0.0).astype(BF16)
        values = jnp.dot(weights, moved, preferred_element_type=F32)
        recv3[n_seq] = compact(jnp.concatenate([values, values], axis=0), 0).astype(BF16)
        recvml[n_seq] = statistics(
            jnp.concatenate([peak, peak], axis=0), jnp.concatenate([total, total], axis=0)
        )
        recv3[me] = send3[my_b]
        recvml[me] = sendml[my_b]

        @pl.loop(1, n_seq)
        def _(off):
            for copy in copies_up(my_b, lax.rem(me + off, n_seq)):
                copy.wait_recv()

        n_src = n_seq + 1
        for s in range(n_src):
            both = recvml[s]
            mscr[s : s + 1, :] = both[0:1]
            lscr[s : s + 1, :] = both[1:2]
        m_all = mscr[0:n_src, :]
        l_all = lscr[0:n_src, :]
        factor = jnp.exp2(m_all - jnp.max(m_all, axis=0, keepdims=True))
        norm = jnp.sum(factor * l_all, axis=0, keepdims=True)
        norm = jnp.where(norm > 0.0, norm, 1.0)
        coefs[0:n_src, :] = factor / norm
        coef_t[0:crows, :] = compact(coefs[...].T[0:srows], 0)
        acc = jnp.zeros((crows, HEAD_DIM), F32)
        for s in range(n_src):
            acc = acc + coef_t[0:crows, s : s + 1] * recv3[s].astype(F32)
        att[my_b] = acc.astype(BF16)
        @pl.loop(0, n_seq)
        def _(i):
            dst = far_order(i)

            @pl.when(dst != me)
            def _():
                copy_gather(att, s5_sem, r5_sem, my_b, dst).start()

    on_owner(owner_merge)

    @pl.loop(0, batch)
    def _(i):
        b = use_order(i)

        @pl.when(jnp.logical_not(is_own(b)))
        def _():
            copy_gather(att, s5_sem, r5_sem, b, me).wait_recv()

        att32[pl.ds(pl.multiple_of(b * crows, 16), crows), :] = att[b].astype(F32)

    planes = [(j, verify) for j in range(verify)]
    planes += [(qrows + j, draft) for j in range(draft)]
    for pair in range(x_buf.shape[0] // 16):
        for h in range(heads):
            halves = []
            for at in (2 * pair, 2 * pair + 1):
                if at < len(planes):
                    start, jump = planes[at]
                    halves.append(att32[pl.ds(start + h * jump, batch, stride=crows), :])
                else:
                    halves.append(jnp.zeros((batch, HEAD_DIM), F32))
            x_buf[16 * pair : 16 * pair + 16, h * HEAD_DIM : (h + 1) * HEAD_DIM] = (
                jnp.concatenate(halves, axis=0).astype(BF16)
            )

    part_rows, part_cols = send4.shape[1:]
    all_rows = x_buf.shape[0]

    def place(at):
        return (at // col_parts) * part_rows, (at % col_parts) * part_cols

    def copy4(at, src):
        return pltpu.make_async_remote_copy(
            src_ref=send4.at[at],
            dst_ref=recv4.at[src],
            send_sem=s4_sem.at[at],
            recv_sem=r4_sem.at[src],
            device_id=(me, at),
            device_id_type=MESH,
        )

    wo_copy.wait()

    @pl.loop(1, n_head + 1)
    def _(off):
        at = lax.rem(hd + off, n_head)
        r0 = pl.multiple_of((at // col_parts) * part_rows, 16)
        c0 = pl.multiple_of(lax.rem(at, col_parts) * part_cols, HEAD_DIM)
        send4[at] = jnp.dot(
            x_buf[pl.ds(r0, part_rows), :],
            wo_buf[:, pl.ds(c0, part_cols)],
            preferred_element_type=F32,
        ).astype(BF16)

        @pl.when(off < n_head)
        def _():
            copy4(at, hd).start()

    def add_head(off, acc):
        src = lax.rem(hd + off, n_head)
        copy4(hd, src).wait_recv()
        return acc + recv4[src].astype(F32)

    fin[hd] = lax.fori_loop(1, n_head, add_head, send4[hd].astype(F32)).astype(BF16)

    def copy6(at, dst):
        return pltpu.make_async_remote_copy(
            src_ref=fin.at[at],
            dst_ref=fin.at[at],
            send_sem=s6_sem.at[dst],
            recv_sem=r6_sem.at[at],
            device_id=(me, dst),
            device_id_type=MESH,
        )

    @pl.loop(1, n_head)
    def _(off):
        copy6(hd, lax.rem(hd + off, n_head)).start()

    @pl.loop(1, n_head)
    def _(off):
        copy6(lax.rem(hd + off, n_head), hd).wait_recv()

    for at in range(n_head):
        r0, c0 = place(at)
        for c in range(part_cols // HEAD_DIM):
            base = (c0 // HEAD_DIM + c) * all_rows + r0
            y32[base : base + part_rows, :] = fin[
                at, :, c * HEAD_DIM : (c + 1) * HEAD_DIM
            ].astype(F32)
    target_rows = verify * batch
    chunks = range(out_v.shape[1] // HEAD_DIM)
    for c in chunks:
        out_v[:, c * HEAD_DIM : (c + 1) * HEAD_DIM] = y32[
            c * all_rows : c * all_rows + target_rows, :
        ].astype(BF16)
    for b in range(batch):
        out_d[b] = jnp.concatenate(
            [
                y32[pl.ds(c * all_rows + target_rows + b, draft, stride=batch), :]
                for c in chunks
            ],
            axis=1,
        ).astype(BF16)

    @pl.loop(0, batch)
    def _(b):
        @pl.when(b * per != me)
        def _():
            for part in range(2):
                copy1(part, b, me).wait_send()
            for copy in copies_up(b, me):
                copy.wait_send()

    def owner_sent():
        @pl.loop(1, n_seq)
        def _(off):
            dst = lax.rem(me + off, n_seq)
            copy_gather(query_all, s2_sem, r2_sem, my_b, dst).wait_send()
            copy_gather(att, s5_sem, r5_sem, my_b, dst).wait_send()

    on_owner(owner_sent)

    @pl.loop(1, n_head)
    def _(off):
        dst = lax.rem(hd + off, n_head)
        copy4(dst, hd).wait_send()
        copy6(hd, dst).wait_send()


def per_device(
    n_seq,
    n_head,
    hidden_states,
    w_query,
    w_key,
    w_value,
    w_out,
    key_cache,
    value_cache,
    context_lengths,
    keep_blocks,
):
    batch, verify, width = hidden_states.shape
    draft = verify - 1
    ctx_local = key_cache.shape[1]
    kv_cols = key_cache.shape[2]
    kv_local = kv_cols // HEAD_DIM
    q_cols = w_query.shape[1]
    heads = q_cols // HEAD_DIM
    out_cols = w_out.shape[1]
    slots = heads + 2 * kv_local
    rows1 = round_up(verify * slots, 16)
    srows = 2 * verify * heads
    crows = round_up((verify + draft) * heads, 16)
    lanes = round_up(srows, HEAD_DIM)
    n_rows = batch * (verify + draft)
    col_parts = math.gcd(n_head, out_cols // HEAD_DIM)
    row_parts = n_head // col_parts
    part_rows = round_up(-(-n_rows // row_parts), 16)
    part_cols = out_cols // col_parts
    all_rows = part_rows * row_parts
    n_src = n_seq + 1
    src_rows = round_up(n_src, 8)
    qpad = round_up(verify * heads, 16)
    dims = (n_seq, n_head, batch, verify, kv_local, heads, ctx_local, col_parts)

    inverse = (500000.0 ** (-(np.arange(HEAD_DIM // 2) * 2.0) / HEAD_DIM)).astype(np.float32)
    inverse = jnp.asarray(np.concatenate([inverse, inverse])[None, :])

    vmem = pl.BlockSpec(memory_space=pltpu.VMEM)
    hbm = pl.BlockSpec(memory_space=pl.ANY)
    dma = pltpu.SemaphoreType.DMA
    target, drafted = pl.pallas_call(
        functools.partial(kernel, dims),
        out_shape=(
            pltpu.VMEM((batch * verify, out_cols), BF16),
            pltpu.VMEM((batch, draft, out_cols), BF16),
        ),
        in_specs=[hbm] * 10,
        out_specs=(vmem, vmem),
        scratch_shapes=[
            pltpu.VMEM((verify * batch, width), BF16),
            pltpu.VMEM(inverse.shape, F32),
            pltpu.SMEM(context_lengths.shape, jnp.int32),
            pltpu.SMEM(keep_blocks.shape, jnp.int32),
            dma((4,)),
            pltpu.VMEM((width, q_cols + 2 * kv_cols), BF16),
            pltpu.VMEM(w_out.shape, BF16),
            pltpu.VMEM(key_cache.shape, BF16),
            pltpu.VMEM(value_cache.shape, BF16),
            pltpu.VMEM((batch * rows1, HEAD_DIM), F32),
            pltpu.VMEM((batch, rows1, HEAD_DIM), BF16),
            pltpu.VMEM((n_seq, rows1, HEAD_DIM), BF16),
            pltpu.VMEM((rows1, HEAD_DIM), BF16),
            pltpu.VMEM((batch, qpad, HEAD_DIM), BF16),
            pltpu.VMEM((batch, crows, HEAD_DIM), BF16),
            pltpu.VMEM((n_src, crows, HEAD_DIM), BF16),
            pltpu.VMEM((batch, 2, lanes), F32),
            pltpu.VMEM((n_src, 2, lanes), F32),
            pltpu.VMEM((rows1, HEAD_DIM), F32),
            pltpu.VMEM((rows1, HEAD_DIM), F32),
            pltpu.VMEM((src_rows, lanes), F32),
            pltpu.VMEM((src_rows, lanes), F32),
            pltpu.VMEM((HEAD_DIM, lanes), F32),
            pltpu.VMEM((lanes, HEAD_DIM), F32),
            pltpu.VMEM((batch, crows, HEAD_DIM), BF16),
            pltpu.VMEM((2, srows + 8, HEAD_DIM), F32),
            pltpu.VMEM((2, crows + 8, HEAD_DIM), F32),
            pltpu.VMEM((batch * crows, HEAD_DIM), F32),
            pltpu.VMEM((all_rows, q_cols), BF16),
            pltpu.VMEM((n_head, part_rows, part_cols), BF16),
            pltpu.VMEM((n_head, part_rows, part_cols), BF16),
            pltpu.VMEM((n_head, part_rows, part_cols), BF16),
            pltpu.VMEM((out_cols // HEAD_DIM * all_rows, HEAD_DIM), F32),
            dma((q_cols // min(512, q_cols) + 2,)),
            dma,
            dma((batch,)),
            dma((batch,)),
            dma((2, batch)),
            dma((2, n_seq)),
            dma((n_seq,)),
            dma((batch,)),
            dma((batch,)),
            dma((n_seq,)),
            dma((batch,)),
            dma((n_seq,)),
            dma((n_seq,)),
            dma((batch,)),
            dma((n_head,)),
            dma((n_head,)),
            dma((n_head,)),
            dma((n_head,)),
        ],
        compiler_params=pltpu.CompilerParams(
            collective_id=0, has_side_effects=True, vmem_limit_bytes=56 * 1024 * 1024
        ),
        name="verify_round",
    )(
        hidden_states.transpose(1, 0, 2).reshape(verify * batch, width),
        inverse,
        context_lengths,
        keep_blocks,
        w_query,
        w_key,
        w_value,
        w_out,
        key_cache,
        value_cache,
    )
    return target.reshape(verify, batch, out_cols).transpose(1, 0, 2), drafted


def solution(mesh):
    placed = (
        P(None, None, "seq"),
        P("seq", "head"),
        P("seq", "head"),
        P("seq", "head"),
        P("head", "seq"),
        P(None, "seq", "head"),
        P(None, "seq", "head"),
        P(),
        P(None, "seq"),
    )
    return jax.shard_map(
        functools.partial(per_device, mesh.shape["seq"], mesh.shape["head"]),
        mesh=mesh,
        in_specs=placed,
        out_specs=(P(None, None, "seq"), P(None, None, "seq")),
        check_vma=False,
    )
```

```python
import functools
import math

import jax
import jax.numpy as jnp
import numpy as np
from jax import lax
from jax.experimental import pallas as pl
from jax.experimental.pallas import tpu as pltpu
from jax.sharding import PartitionSpec as P

HEAD_DIM = 128
BLOCK = 128
NEG = -1e30
MESH = pl.DeviceIdType.MESH
F32 = jnp.float32
BF16 = jnp.bfloat16


def round_up(value, unit):
    return -(-value // unit) * unit


def kernel(
    dims,
    hid_in,
    inv_in,
    ctx_in,
    keep_in,
    wq,
    wk,
    wv,
    wo,
    kc,
    vc,
    out_v,
    out_d,
    hid,
    inv,
    ctx,
    keep,
    small_sem,
    w_buf,
    wo_buf,
    k_buf,
    v_buf,
    pack,
    send1,
    recv1,
    qkv,
    query_all,
    send3,
    recv3,
    sendml,
    recvml,
    cos_buf,
    sin_buf,
    mscr,
    lscr,
    coefs,
    coef_t,
    att,
    spare,
    dense,
    att32,
    x_buf,
    send4,
    recv4,
    fin,
    y32,
    w_sem,
    wo_sem,
    k_sem,
    v_sem,
    s1_sem,
    r1_sem,
    s2_sem,
    r2_sem,
    s3_sem,
    r3_sem,
    sm_sem,
    rm_sem,
    s5_sem,
    r5_sem,
    s4_sem,
    r4_sem,
    s6_sem,
    r6_sem,
):
    n_seq, n_head, batch, verify, kv_local, heads, ctx_local, col_parts = dims
    draft = verify - 1
    group = heads // kv_local
    per = n_seq // batch
    slots = heads + 2 * kv_local
    qrows = verify * heads
    grows = verify * group
    srows = 2 * qrows
    q_cols = heads * HEAD_DIM
    kv_cols = kv_local * HEAD_DIM
    me = lax.axis_index("seq")
    hd = lax.axis_index("head")
    my_b = me // per
    scale = HEAD_DIM ** (-0.5) * math.log2(math.e)
    rows1 = send1.shape[1]
    crows = att.shape[1]
    lines = n_seq // 2
    line, side = me // 2, lax.rem(me, 2)

    def use_order(i):
        if per > 1:
            return lax.rem(my_b + i, batch)
        return 2 * lax.rem(line + i // 2, lines) + lax.rem(side + i, 2)

    def is_own(b):
        return b * per == me

    def on_owner(body):
        if per == 1:
            body()
        else:
            pl.when(lax.rem(me, per) == 0)(body)

    barrier = pltpu.get_barrier_semaphore()
    for off in range(1, n_seq):
        pl.semaphore_signal(
            barrier, inc=1, device_id=(lax.rem(me + off, n_seq), hd), device_id_type=MESH
        )
    for off in range(1, n_head):
        pl.semaphore_signal(
            barrier, inc=1, device_id=(me, lax.rem(hd + off, n_head)), device_id_type=MESH
        )

    small = [
        pltpu.make_async_copy(src, dst, small_sem.at[at])
        for at, (src, dst) in enumerate(
            ((ctx_in, ctx), (inv_in, inv), (hid_in, hid), (keep_in, keep))
        )
    ]
    for copy in small:
        copy.start()

    step = min(512, q_cols)
    pieces = [(wq, c, step, c) for c in range(0, q_cols, step)]
    pieces += [(wk, 0, kv_cols, q_cols), (wv, 0, kv_cols, q_cols + kv_cols)]
    w_copies = []
    for at, (src, c0, width, d0) in enumerate(pieces):
        copy = pltpu.make_async_copy(
            src.at[:, pl.ds(c0, width)], w_buf.at[:, pl.ds(d0, width)], w_sem.at[at]
        )
        copy.start()
        w_copies.append(copy)

    def cache_copies(b):
        return (
            pltpu.make_async_copy(kc.at[b], k_buf.at[b], k_sem.at[b]),
            pltpu.make_async_copy(vc.at[b], v_buf.at[b], v_sem.at[b]),
        )

    def rotation():
        shape = (8, HEAD_DIM)
        lane = lax.broadcasted_iota(jnp.int32, shape, 1)
        pos = (ctx[my_b] + lax.broadcasted_iota(jnp.int32, shape, 0)).astype(F32)
        angle = pos * inv[...]
        cosine = jnp.cos(angle)
        sine = jnp.sin(angle)
        sine = jnp.where(lane < HEAD_DIM // 2, -sine, sine)
        cos_buf[...] = jnp.ones_like(cos_buf)
        sin_buf[...] = jnp.zeros_like(sin_buf)
        for slot in range(heads + kv_local):
            r0 = slot * verify
            cos_buf[r0 : r0 + 8, :] = cosine
            sin_buf[r0 : r0 + 8, :] = sine
        r0 = (heads + kv_local) * verify
        cos_buf[r0 : r0 + 8, :] = jnp.ones(shape, F32)
        sin_buf[r0 : r0 + 8, :] = jnp.zeros(shape, F32)

    for copy in small:
        copy.wait()
    on_owner(rotation)

    pack[...] = jnp.zeros_like(pack)
    coefs[...] = jnp.zeros_like(coefs)
    spare[...] = jnp.zeros_like(spare)
    dense[...] = jnp.zeros_like(dense)
    x_in = hid[...]
    def copy1(part, b, src):
        rows = pl.ds(*parts[part])
        return pltpu.make_async_remote_copy(
            src_ref=send1.at[b, rows],
            dst_ref=recv1.at[src, rows],
            send_sem=s1_sem.at[part, b],
            recv_sem=r1_sem.at[part, src],
            device_id=(b * per, hd),
            device_id_type=MESH,
        )

    def send_part(part):
        r0, count = parts[part]

        @pl.loop(0, batch)
        def _(i):
            b = lax.rem(my_b + 1 + i, batch)
            rows = pl.ds(pl.multiple_of(b * rows1 + r0, 16), count)
            send1[b, r0 : r0 + count, :] = pack[rows, :].astype(BF16)

            @pl.when(b * per != me)
            def _():
                copy1(part, b, me).start()

    parts = ((0, rows1),)
    for copy, (src, c0, width, d0) in zip(w_copies, pieces):
        copy.wait()
        piece = jnp.dot(x_in, w_buf[:, d0 : d0 + width], preferred_element_type=F32)
        for s in range(width // HEAD_DIM):
            slot = d0 // HEAD_DIM + s
            for j in range(verify):
                pack[pl.ds(slot * verify + j, batch, stride=rows1), :] = piece[
                    j * batch : (j + 1) * batch, s * HEAD_DIM : (s + 1) * HEAD_DIM
                ]
    pl.semaphore_wait(barrier, n_seq - 1 + n_head - 1)
    send_part(0)

    @pl.loop(0, batch)
    def _(i):
        for copy in cache_copies(use_order(i)):
            copy.start()

    wo_copy = pltpu.make_async_copy(wo, wo_buf, wo_sem)
    wo_copy.start()

    def copy_gather(buf, send_sem, recv_sem, b, dst):
        return pltpu.make_async_remote_copy(
            src_ref=buf.at[b],
            dst_ref=buf.at[b],
            send_sem=send_sem.at[dst],
            recv_sem=recv_sem.at[b],
            device_id=(dst, hd),
            device_id_type=MESH,
        )

    def owner_rotate():
        def add(off, acc):
            src = lax.rem(me + off, n_seq)
            for part in range(len(parts)):
                copy1(part, my_b, src).wait_recv()
            return acc + recv1[src].astype(F32)

        total = lax.fori_loop(1, n_seq, add, send1[my_b].astype(F32))
        turned = total * cos_buf[...] + pltpu.roll(total, HEAD_DIM // 2, 1) * sin_buf[...]
        qkv[...] = turned.astype(BF16)
        query_all[my_b] = turned[0 : query_all.shape[1]].astype(BF16)

        @pl.loop(1, n_seq)
        def _(off):
            if per > 1:
                dst = lax.rem(me + off, n_seq)
            else:
                dst = 2 * lax.rem(line + n_seq - off // 2, lines) + lax.rem(side + off, 2)
            copy_gather(query_all, s2_sem, r2_sem, my_b, dst).start()

    on_owner(owner_rotate)

    def compact(value, at):
        loose = spare.at[at]
        loose[0:srows, :] = value
        tight = dense.at[at]
        for h in range(heads):
            r0, r1 = qrows + h * draft, qrows + h * verify
            tight[r0 : r0 + 8, :] = loose[r1 : r1 + 8, :]
        return jnp.concatenate([value[0:qrows], tight[qrows:crows, :]], axis=0)

    def statistics(peak, total):
        lane = lax.broadcasted_iota(jnp.int32, (srows, HEAD_DIM), 1)
        wide = jnp.where(lane == 0, peak, jnp.where(lane == 1, total, 0.0))
        extra = sendml.shape[2] - srows
        if extra:
            wide = jnp.concatenate([wide, jnp.zeros((extra, HEAD_DIM), F32)], axis=0)
        return wide.T[0:2, :]

    def softmax(scores, mask):
        masked = jnp.where(mask, scores, NEG)
        peak = jnp.maximum(jnp.max(masked, axis=1, keepdims=True), NEG / 8)
        weights = jnp.exp2(masked - peak)
        return peak, jnp.sum(weights, axis=1, keepdims=True), weights

    def copies_up(b, src):
        return [
            pltpu.make_async_remote_copy(
                src_ref=source.at[b],
                dst_ref=target.at[src],
                send_sem=send_sem.at[b],
                recv_sem=recv_sem.at[src],
                device_id=(b * per, hd),
                device_id_type=MESH,
            )
            for source, target, send_sem, recv_sem in (
                (sendml, recvml, sm_sem, rm_sem),
                (send3, recv3, s3_sem, r3_sem),
            )
        ]

    def attend(b, at):
        query = query_all[b].astype(F32)[0:qrows]
        row = lax.broadcasted_iota(jnp.int32, query.shape, 0)
        spread = jnp.concatenate(
            [
                jnp.where((row >= kv * grows) & (row < (kv + 1) * grows), query, 0.0)
                for kv in range(kv_local)
            ],
            axis=1,
        ).astype(BF16)
        scores = (
            lax.dot_general(
                spread, k_buf[b], (((1,), (1,)), ((), ())), preferred_element_type=F32
            )
            * scale
        )
        lane = lax.broadcasted_iota(jnp.int32, (1, ctx_local), 1)
        live = lane + me * ctx_local < ctx[b]
        flags = jnp.concatenate(
            [
                jnp.full((1, BLOCK), keep[b, blk], jnp.int32)
                for blk in range(ctx_local // BLOCK)
            ],
            axis=1,
        )
        kept = live & (flags > 0)
        t_peak, t_total, t_weights = softmax(scores, live)
        d_peak, d_total, d_weights = softmax(scores, kept)
        weights = jnp.concatenate([t_weights, d_weights], axis=0).astype(BF16)
        values = jnp.dot(weights, v_buf[b], preferred_element_type=F32)
        blocks = []
        for half in range(2):
            for kv in range(kv_local):
                r0 = half * qrows + kv * grows
                blocks.append(values[r0 : r0 + grows, kv * HEAD_DIM : (kv + 1) * HEAD_DIM])
        send3[b] = compact(jnp.concatenate(blocks, axis=0), at).astype(BF16)
        sendml[b] = statistics(
            jnp.concatenate([t_peak, d_peak], axis=0),
            jnp.concatenate([t_total, d_total], axis=0),
        )

    together = 2

    @pl.loop(0, batch // together)
    def _(i):
        several = [use_order(i * together + at) for at in range(together)]
        for b in several:

            @pl.when(jnp.logical_not(is_own(b)))
            def _(b=b):
                copy_gather(query_all, s2_sem, r2_sem, b, me).wait_recv()

            for copy in cache_copies(b):
                copy.wait()
        for at, b in enumerate(several):
            attend(b, at)
        for b in several:

            @pl.when(jnp.logical_not(is_own(b)))
            def _(b=b):
                for copy in copies_up(b, me):
                    copy.start()

    def owner_merge():
        rows_all = qkv[...].astype(F32)
        query = rows_all[0:qrows]
        raw = lax.dot_general(
            query.astype(BF16), qkv[...], (((1,), (1,)), ((), ())), preferred_element_type=F32
        )
        scores = raw * scale
        row = lax.broadcasted_iota(jnp.int32, scores.shape, 0)
        col = lax.broadcasted_iota(jnp.int32, scores.shape, 1) - qrows
        row_head = lax.div(row, verify)
        row_j = row - row_head * verify
        row_kv = lax.div(row_head, group)
        first = row_kv * verify
        mask = (col >= first) & (col <= first + row_j)
        peak, total, weights = softmax(scores, mask)
        weights = weights.astype(BF16)
        vrow = lax.broadcasted_iota(jnp.int32, rows_all.shape, 0) - qrows
        shift = kv_local * verify
        moved = pltpu.roll(rows_all, rows_all.shape[0] - shift, 0)
        moved = jnp.where((vrow >= 0) & (vrow < shift), moved, 0.0).astype(BF16)
        values = jnp.dot(weights, moved, preferred_element_type=F32)
        recv3[n_seq] = compact(jnp.concatenate([values, values], axis=0), 0).astype(BF16)
        recvml[n_seq] = statistics(
            jnp.concatenate([peak, peak], axis=0), jnp.concatenate([total, total], axis=0)
        )
        recv3[me] = send3[my_b]
        recvml[me] = sendml[my_b]

        @pl.loop(1, n_seq)
        def _(off):
            for copy in copies_up(my_b, lax.rem(me + off, n_seq)):
                copy.wait_recv()

        n_src = n_seq + 1
        for s in range(n_src):
            both = recvml[s]
            mscr[s : s + 1, :] = both[0:1]
            lscr[s : s + 1, :] = both[1:2]
        m_all = mscr[0:n_src, :]
        l_all = lscr[0:n_src, :]
        factor = jnp.exp2(m_all - jnp.max(m_all, axis=0, keepdims=True))
        norm = jnp.sum(factor * l_all, axis=0, keepdims=True)
        norm = jnp.where(norm > 0.0, norm, 1.0)
        coefs[0:n_src, :] = factor / norm
        coef_t[0:crows, :] = compact(coefs[...].T[0:srows], 0)
        acc = jnp.zeros((crows, HEAD_DIM), F32)
        for s in range(n_src):
            acc = acc + coef_t[0:crows, s : s + 1] * recv3[s].astype(F32)
        att[my_b] = acc.astype(BF16)
        @pl.loop(0, lines)
        def _(t):
            far = jnp.where(2 * line < lines, lines - 1 - t, t)
            for at in range(2):
                dst = 2 * far + at

                @pl.when(dst != me)
                def _(dst=dst):
                    copy_gather(att, s5_sem, r5_sem, my_b, dst).start()

    on_owner(owner_merge)

    @pl.loop(0, batch)
    def _(i):
        b = use_order(i)

        @pl.when(jnp.logical_not(is_own(b)))
        def _():
            copy_gather(att, s5_sem, r5_sem, b, me).wait_recv()

        att32[pl.ds(pl.multiple_of(b * crows, 16), crows), :] = att[b].astype(F32)

    planes = [(j, verify) for j in range(verify)]
    planes += [(qrows + j, draft) for j in range(draft)]
    for pair in range(x_buf.shape[0] // 16):
        for h in range(heads):
            halves = []
            for at in (2 * pair, 2 * pair + 1):
                if at < len(planes):
                    start, jump = planes[at]
                    halves.append(att32[pl.ds(start + h * jump, batch, stride=crows), :])
                else:
                    halves.append(jnp.zeros((batch, HEAD_DIM), F32))
            x_buf[16 * pair : 16 * pair + 16, h * HEAD_DIM : (h + 1) * HEAD_DIM] = (
                jnp.concatenate(halves, axis=0).astype(BF16)
            )

    part_rows, part_cols = send4.shape[1:]
    all_rows = x_buf.shape[0]

    def place(at):
        return (at // col_parts) * part_rows, (at % col_parts) * part_cols

    def copy4(at, src):
        return pltpu.make_async_remote_copy(
            src_ref=send4.at[at],
            dst_ref=recv4.at[src],
            send_sem=s4_sem.at[at],
            recv_sem=r4_sem.at[src],
            device_id=(me, at),
            device_id_type=MESH,
        )

    wo_copy.wait()

    @pl.loop(1, n_head + 1)
    def _(off):
        at = lax.rem(hd + off, n_head)
        r0 = pl.multiple_of((at // col_parts) * part_rows, 16)
        c0 = pl.multiple_of(lax.rem(at, col_parts) * part_cols, HEAD_DIM)
        send4[at] = jnp.dot(
            x_buf[pl.ds(r0, part_rows), :],
            wo_buf[:, pl.ds(c0, part_cols)],
            preferred_element_type=F32,
        ).astype(BF16)

        @pl.when(off < n_head)
        def _():
            copy4(at, hd).start()

    def add_head(off, acc):
        src = lax.rem(hd + off, n_head)
        copy4(hd, src).wait_recv()
        return acc + recv4[src].astype(F32)

    fin[hd] = lax.fori_loop(1, n_head, add_head, send4[hd].astype(F32)).astype(BF16)

    def copy6(at, dst):
        return pltpu.make_async_remote_copy(
            src_ref=fin.at[at],
            dst_ref=fin.at[at],
            send_sem=s6_sem.at[dst],
            recv_sem=r6_sem.at[at],
            device_id=(me, dst),
            device_id_type=MESH,
        )

    @pl.loop(1, n_head)
    def _(off):
        copy6(hd, lax.rem(hd + off, n_head)).start()

    @pl.loop(1, n_head)
    def _(off):
        copy6(lax.rem(hd + off, n_head), hd).wait_recv()

    for at in range(n_head):
        r0, c0 = place(at)
        for c in range(part_cols // HEAD_DIM):
            base = (c0 // HEAD_DIM + c) * all_rows + r0
            y32[base : base + part_rows, :] = fin[
                at, :, c * HEAD_DIM : (c + 1) * HEAD_DIM
            ].astype(F32)
    target_rows = verify * batch
    chunks = range(out_v.shape[1] // HEAD_DIM)
    for c in chunks:
        out_v[:, c * HEAD_DIM : (c + 1) * HEAD_DIM] = y32[
            c * all_rows : c * all_rows + target_rows, :
        ].astype(BF16)
    for b in range(batch):
        out_d[b] = jnp.concatenate(
            [
                y32[pl.ds(c * all_rows + target_rows + b, draft, stride=batch), :]
                for c in chunks
            ],
            axis=1,
        ).astype(BF16)

    @pl.loop(0, batch)
    def _(b):
        @pl.when(b * per != me)
        def _():
            for part in range(len(parts)):
                copy1(part, b, me).wait_send()
            for copy in copies_up(b, me):
                copy.wait_send()

    def owner_sent():
        @pl.loop(1, n_seq)
        def _(off):
            dst = lax.rem(me + off, n_seq)
            copy_gather(query_all, s2_sem, r2_sem, my_b, dst).wait_send()
            copy_gather(att, s5_sem, r5_sem, my_b, dst).wait_send()

    on_owner(owner_sent)

    @pl.loop(1, n_head)
    def _(off):
        dst = lax.rem(hd + off, n_head)
        copy4(dst, hd).wait_send()
        copy6(hd, dst).wait_send()


def per_device(
    n_seq,
    n_head,
    hidden_states,
    w_query,
    w_key,
    w_value,
    w_out,
    key_cache,
    value_cache,
    context_lengths,
    keep_blocks,
):
    batch, verify, width = hidden_states.shape
    draft = verify - 1
    ctx_local = key_cache.shape[1]
    kv_cols = key_cache.shape[2]
    kv_local = kv_cols // HEAD_DIM
    q_cols = w_query.shape[1]
    heads = q_cols // HEAD_DIM
    out_cols = w_out.shape[1]
    slots = heads + 2 * kv_local
    rows1 = round_up(verify * slots, 16)
    srows = 2 * verify * heads
    crows = round_up((verify + draft) * heads, 16)
    lanes = round_up(srows, HEAD_DIM)
    n_rows = batch * (verify + draft)
    col_parts = math.gcd(n_head, out_cols // HEAD_DIM)
    row_parts = n_head // col_parts
    part_rows = round_up(-(-n_rows // row_parts), 16)
    part_cols = out_cols // col_parts
    all_rows = part_rows * row_parts
    n_src = n_seq + 1
    src_rows = round_up(n_src, 8)
    qpad = round_up(verify * heads, 16)
    dims = (n_seq, n_head, batch, verify, kv_local, heads, ctx_local, col_parts)

    inverse = (500000.0 ** (-(np.arange(HEAD_DIM // 2) * 2.0) / HEAD_DIM)).astype(np.float32)
    inverse = jnp.asarray(np.concatenate([inverse, inverse])[None, :])

    vmem = pl.BlockSpec(memory_space=pltpu.VMEM)
    hbm = pl.BlockSpec(memory_space=pl.ANY)
    dma = pltpu.SemaphoreType.DMA
    target, drafted = pl.pallas_call(
        functools.partial(kernel, dims),
        out_shape=(
            pltpu.VMEM((batch * verify, out_cols), BF16),
            pltpu.VMEM((batch, draft, out_cols), BF16),
        ),
        in_specs=[hbm] * 10,
        out_specs=(vmem, vmem),
        scratch_shapes=[
            pltpu.VMEM((verify * batch, width), BF16),
            pltpu.VMEM(inverse.shape, F32),
            pltpu.SMEM(context_lengths.shape, jnp.int32),
            pltpu.SMEM(keep_blocks.shape, jnp.int32),
            dma((4,)),
            pltpu.VMEM((width, q_cols + 2 * kv_cols), BF16),
            pltpu.VMEM(w_out.shape, BF16),
            pltpu.VMEM(key_cache.shape, BF16),
            pltpu.VMEM(value_cache.shape, BF16),
            pltpu.VMEM((batch * rows1, HEAD_DIM), F32),
            pltpu.VMEM((batch, rows1, HEAD_DIM), BF16),
            pltpu.VMEM((n_seq, rows1, HEAD_DIM), BF16),
            pltpu.VMEM((rows1, HEAD_DIM), BF16),
            pltpu.VMEM((batch, qpad, HEAD_DIM), BF16),
            pltpu.VMEM((batch, crows, HEAD_DIM), BF16),
            pltpu.VMEM((n_src, crows, HEAD_DIM), BF16),
            pltpu.VMEM((batch, 2, lanes), F32),
            pltpu.VMEM((n_src, 2, lanes), F32),
            pltpu.VMEM((rows1, HEAD_DIM), F32),
            pltpu.VMEM((rows1, HEAD_DIM), F32),
            pltpu.VMEM((src_rows, lanes), F32),
            pltpu.VMEM((src_rows, lanes), F32),
            pltpu.VMEM((HEAD_DIM, lanes), F32),
            pltpu.VMEM((lanes, HEAD_DIM), F32),
            pltpu.VMEM((batch, crows, HEAD_DIM), BF16),
            pltpu.VMEM((2, srows + 8, HEAD_DIM), F32),
            pltpu.VMEM((2, crows + 8, HEAD_DIM), F32),
            pltpu.VMEM((batch * crows, HEAD_DIM), F32),
            pltpu.VMEM((all_rows, q_cols), BF16),
            pltpu.VMEM((n_head, part_rows, part_cols), BF16),
            pltpu.VMEM((n_head, part_rows, part_cols), BF16),
            pltpu.VMEM((n_head, part_rows, part_cols), BF16),
            pltpu.VMEM((out_cols // HEAD_DIM * all_rows, HEAD_DIM), F32),
            dma((q_cols // min(512, q_cols) + 2,)),
            dma,
            dma((batch,)),
            dma((batch,)),
            dma((1, batch)),
            dma((1, n_seq)),
            dma((n_seq,)),
            dma((batch,)),
            dma((batch,)),
            dma((n_seq,)),
            dma((batch,)),
            dma((n_seq,)),
            dma((n_seq,)),
            dma((batch,)),
            dma((n_head,)),
            dma((n_head,)),
            dma((n_head,)),
            dma((n_head,)),
        ],
        compiler_params=pltpu.CompilerParams(
            collective_id=0, has_side_effects=True, vmem_limit_bytes=56 * 1024 * 1024
        ),
        name="verify_round",
    )(
        hidden_states.transpose(1, 0, 2).reshape(verify * batch, width),
        inverse,
        context_lengths,
        keep_blocks,
        w_query,
        w_key,
        w_value,
        w_out,
        key_cache,
        value_cache,
    )
    return target.reshape(verify, batch, out_cols).transpose(1, 0, 2), drafted


def solution(mesh):
    placed = (
        P(None, None, "seq"),
        P("seq", "head"),
        P("seq", "head"),
        P("seq", "head"),
        P("head", "seq"),
        P(None, "seq", "head"),
        P(None, "seq", "head"),
        P(),
        P(None, "seq"),
    )
    return jax.shard_map(
        functools.partial(per_device, mesh.shape["seq"], mesh.shape["head"]),
        mesh=mesh,
        in_specs=placed,
        out_specs=(P(None, None, "seq"), P(None, None, "seq")),
        check_vma=False,
    )
```
